128 devices in a mesh: dp: 32 (over x, y, core), chan: 4 (over z).
Axes of the slice: x: 4, y: 4, z: 4, core: 2. Of those that a mesh axis runs over, the one named last changes fastest.
Arguments:
- features: float32 [294912, 112], P(('dp', 'chan')), may hold values from -32 to 32
- seg_units: int32 [128, 3], P('dp'), may hold values from 1 to 3, 6 in all within a row
- w_expand: float32 [112, 672], P(None, 'chan'), may hold values from -0.5 to 0.5
- gain_one: float32 [672], P('chan'), may hold values from 0.5 to 1.5
- bias_one: float32 [672], P('chan'), may hold values from -0.5 to 0.5
- w_depth: float32 [5, 5, 672], P(None, None, 'chan'), may hold values from -1.25 to 1.25
- gain_two: float32 [672], P('chan'), may hold values from 0.5 to 1.5
- bias_two: float32 [672], P('chan'), may hold values from -0.5 to 0.5
- w_reduce: float32 [672, 28], P('chan'), may hold values from -0.25 to 0.25
- b_reduce: float32 [28], replicated, may hold values from -4 to 4
- w_excite: float32 [28, 672], P(None, 'chan'), may hold values from -1 to 1
- b_excite: float32 [672], P('chan'), may hold values from -4 to 4
- w_project: float32 [672, 112], P('chan'), may hold values from -0.25 to 0.25
- gain_three: float32 [112], replicated, may hold values from 0.5 to 1.5
- bias_three: float32 [112], replicated, may hold values from -0.5 to 0.5
- cotangent: float32 [294912, 112], P(('dp', 'chan')), may hold values from -6 to 6
Outputs:
- output: float32 [294912, 112], P(('dp', 'chan'))
- input_grad: float32 [294912, 112], P(('dp', 'chan'))
- grad_expand: float32 [112, 672], P(None, 'chan')
- grad_gain_one: float32 [672], P('chan')
- grad_bias_one: float32 [672], P('chan')
- grad_depth: float32 [5, 5, 672], P(None, None, 'chan')
- grad_gain_two: float32 [672], P('chan')
- grad_bias_two: float32 [672], P('chan')
- grad_reduce: float32 [672, 28], P('chan')
- grad_reduce_bias: float32 [28], replicated
- grad_excite: float32 [28, 672], P(None, 'chan')
- grad_excite_bias: float32 [672], P('chan')
- grad_project: float32 [672, 112], P('chan')
- grad_gain_three: float32 [112], replicated
- grad_bias_three: float32 [112], replicated
The draws below stay inside these ranges and needn't reach their ends.
Inputs may be any that keep to these rules, and one draw needn't show every extreme that they name: `seg_units`: in each slot the 3 lengths sum to 6 and the largest is exactly 3.
All inputs are finite; a program needn't handle non-finite values.
Results may differ from the reference program's by a relative error of at most 0.0003.
Values sent between devices are 32-bit elements; how exact they have to be, the bound alone decides.
A program may use at most 576 MiB of HBM per device.

```python
import math
import jax
import jax.numpy as jnp
import numpy as np
from jax import lax

D = 112
EXP = 672
SQZ = 28
KS = 5
H = 6
W = 4
FRAMES = 96
BLOCK = 16
NSEG = 3
MOST = 3
SLOTS = 128
ROWS = 294912


def draw_features(key, part):
    key = jax.random.fold_in(key, 7)
    keys = jax.random.split(key, 2)
    blocks = FRAMES // BLOCK
    draw_shape = (SLOTS, blocks, BLOCK * H * W, D)
    rough_part = jnp.clip(jax.random.normal(keys[0], draw_shape, jnp.float32), -4.0, 4.0)
    offsets = 0.7 * jnp.clip(jax.random.normal(keys[1], (SLOTS, blocks, 1, D), jnp.float32), -3.0, 3.0)
    slot_rise = jnp.exp(math.log(3.0) * jnp.arange(SLOTS, dtype=jnp.float32) / max(SLOTS - 1, 1)).reshape(SLOTS, 1, 1, 1)
    return ((rough_part + offsets) * slot_rise).reshape(SLOTS * FRAMES * H * W, D)


def steps_of(own_key, shape, shards, least, high):
    def one(dim, parts):
        heights = jax.random.uniform(jax.random.fold_in(jax.random.fold_in(own_key, 6), dim), (parts,), jnp.float32, least / len(shards), high / len(shards))
        return jnp.repeat(jnp.exp(heights), shape[dim] // parts).reshape((-1,) + (1,) * (len(shape) - dim - 1))

    loudness = one(*shards[0])
    for cut in shards[1:]:
        loudness = loudness * one(*cut)
    return loudness


def profile(count, total, bound, lean):
    portions = [(1 << 20) // math.isqrt(grade ** lean) + 1 for grade in range(2, count + 1)]
    surplus, given = total - bound - (count - 1), [1] * (count - 1)
    while surplus > 0:
        candidates = [i for i in range(count - 1) if given[i] < bound]
        mass, remaining = sum([portions[i] for i in candidates]), surplus
        for i in candidates:
            addition = min(bound - given[i], max(1, remaining * portions[i] // mass), surplus)
            given[i] = given[i] + addition
            surplus = surplus - addition
    return np.array([bound] + given)


def uneven(key, amount, total, reach, slope):
    if amount == 2:
        one = jax.random.randint(key, (), max(1, total - reach), min(reach, total - 1) + 1)
        return jnp.stack([one, total - one])
    lengths = jnp.asarray(profile(amount, total, reach, slope), jnp.int32)
    pairs = (amount - 1) // 2
    donor, receiver = lengths[1:1 + 2 * pairs:2], lengths[2:2 + 2 * pairs:2]
    room = jnp.minimum(donor - 1, reach - receiver)
    shifted = jax.random.randint(jax.random.fold_in(key, 1), (pairs,), 0, 1 << 20) % (room + 1)
    lengths = lengths.at[1:1 + 2 * pairs:2].set(donor - shifted).at[2:2 + 2 * pairs:2].set(receiver + shifted)
    return lengths[jax.random.permutation(jax.random.fold_in(key, 2), amount)]


def normal_values(stream_key, dims, deviation, reach, cuts=(), kind=jnp.bfloat16):
    drawn = jax.random.normal(stream_key, dims, jnp.float32) * deviation
    if len(cuts) > 0:
        drawn = steps_of(stream_key, dims, cuts, -0.22, 0.18) * drawn
    return jnp.clip(drawn, min=-reach, max=reach).astype(kind)


def setup_inputs(seed: int = 0) -> dict:
    arg_keys = jax.random.split(jax.random.key(seed), 17)
    return {
        "features": draw_features(jax.random.fold_in(arg_keys[16], 71), 0),
        "seg_units": jax.vmap(lambda own: uneven(own, NSEG, FRAMES // BLOCK, MOST, 0))(jax.random.split(arg_keys[1], SLOTS)).reshape((SLOTS, NSEG)).astype(jnp.int32),
        "w_expand": normal_values(arg_keys[2], (D, EXP), D ** -0.5, 0.5, ((1, 4),), jnp.float32),
        "gain_one": jnp.clip(0.5 + 1.0 * jax.random.uniform(arg_keys[3], (EXP,), jnp.float32) ** steps_of(arg_keys[3], (EXP,), ((0, 4),), -0.2, 0.2), 0.5, 1.5),
        "bias_one": jnp.clip(jax.random.uniform(arg_keys[4], (EXP,), jnp.float32, -0.5, 0.5) * steps_of(arg_keys[4], (EXP,), ((0, 4),), -0.4, 0.0), -0.5, 0.5),
        "w_depth": normal_values(arg_keys[5], (KS, KS, EXP), (KS * KS) ** -0.5, 1.25, ((2, 4),), jnp.float32),
        "gain_two": jnp.clip(0.5 + 1.0 * jax.random.uniform(arg_keys[6], (EXP,), jnp.float32) ** steps_of(arg_keys[6], (EXP,), ((0, 4),), -0.2, 0.2), 0.5, 1.5),
        "bias_two": jnp.clip(jax.random.uniform(arg_keys[7], (EXP,), jnp.float32, -0.5, 0.5) * steps_of(arg_keys[7], (EXP,), ((0, 4),), -0.4, 0.0), -0.5, 0.5),
        "w_reduce": normal_values(arg_keys[8], (EXP, SQZ), EXP ** -0.5, 0.25, ((0, 4),), jnp.float32),
        "b_reduce": normal_values(arg_keys[9], (SQZ,), 1.0, 4.0, (), jnp.float32),
        "w_excite": normal_values(arg_keys[10], (SQZ, EXP), SQZ ** -0.5, 1.0, ((1, 4),), jnp.float32),
        "b_excite": normal_values(arg_keys[11], (EXP,), 1.0, 4.0, ((0, 4),), jnp.float32),
        "w_project": normal_values(arg_keys[12], (EXP, D), EXP ** -0.5, 0.25, ((0, 4),), jnp.float32),
        "gain_three": jnp.clip(jax.random.uniform(arg_keys[13], (D,), jnp.float32, 0.5, 1.5), 0.5, 1.5),
        "bias_three": jnp.clip(jax.random.uniform(arg_keys[14], (D,), jnp.float32, -0.5, 0.5), -0.5, 0.5),
        "cotangent": normal_values(arg_keys[15], (ROWS, D), 1.0, 6.0, ((0, 128),), jnp.float32),
    }


EPSILON = 0.001
PRECISE = lax.Precision.HIGHEST

@jax.custom_vjp
def low(v):
    return lax.optimization_barrier(v.astype(jnp.bfloat16)).astype(jnp.float32)

@jax.custom_vjp
def low_back(v):
    return v

def low_keep(v):
    return (low(v), None)

def low_pass(kept, grad):
    return (grad,)

def back_keep(v):
    return (v, None)

def back_low(kept, grad):
    return (low(grad),)
low.defvjp(low_keep, low_pass)
low_back.defvjp(back_keep, back_low)

def segment_table(seg_units, frames, first):
    slot_count = seg_units.shape[0]
    widths = (seg_units * BLOCK).astype(jnp.int32)
    upper_end = jnp.cumsum(widths, axis=1) + (jnp.arange(slot_count, dtype=jnp.int32) * FRAMES)[:, None]
    upper_end = upper_end.reshape(-1).astype(jnp.int32)
    lower_end = upper_end - widths.reshape(-1)
    frame_index = (first + jnp.arange(frames, dtype=jnp.int32)).astype(jnp.int32)
    inside = (frame_index[:, None] >= lower_end[None, :]) & (frame_index[:, None] < upper_end[None, :])
    counts = (widths * (H * W)).reshape(-1).astype(jnp.float32)
    return (inside.astype(jnp.float32), counts)

def depthwise(frames_in, kernel):
    radius_cells = kernel.shape[0] // 2
    padded = jnp.pad(frames_in, ((0, 0), (radius_cells, radius_cells), (radius_cells, radius_cells), (0, 0)))
    tall_cells = frames_in.shape[1]
    wide_cells = frames_in.shape[2]
    result = jnp.zeros(frames_in.shape, jnp.float32)
    for shift_down in range(kernel.shape[0]):
        for shift_right in range(kernel.shape[1]):
            window = padded[:, shift_down:shift_down + tall_cells, shift_right:shift_right + wide_cells, :]
            result = result + window * kernel[shift_down, shift_right]
    return result

def batch_norm(values, gain, bias):
    mean_value = lax.optimization_barrier(jnp.mean(values, axis=0))
    centred = values - mean_value
    spread = lax.optimization_barrier(jnp.mean(centred * centred, axis=0))
    return centred * lax.rsqrt(spread + EPSILON) * gain + bias

def reference(features, seg_units, w_expand, gain_one, bias_one, w_depth, gain_two, bias_two, w_reduce, b_reduce, w_excite, b_excite, w_project, gain_three, bias_three, cotangent):
    frames = SLOTS * FRAMES
    seg_table, counts = segment_table(seg_units, frames, 0)

    def forward(features, w_expand, gain_one, bias_one, w_depth, gain_two, bias_two, w_reduce, b_reduce, w_excite, b_excite, w_project, gain_three, bias_three):
        expanded = jnp.dot(features, w_expand, precision=PRECISE)
        active_one = jax.nn.silu(batch_norm(expanded, gain_one, bias_one))
        depth_out = depthwise(active_one.reshape(frames, H, W, EXP), w_depth).reshape(expanded.shape)
        active_two = jax.nn.silu(batch_norm(depth_out, gain_two, bias_two))
        framed = active_two.reshape(frames, H * W, EXP)
        pooled = jnp.einsum('fs,fe->se', seg_table, lax.optimization_barrier(jnp.sum(framed, axis=1)), precision=PRECISE) / counts[:, None]
        squeezed = jax.nn.silu(jnp.dot(pooled, w_reduce, precision=PRECISE) + b_reduce)
        gate_values = jax.nn.sigmoid(jnp.dot(squeezed, w_excite, precision=PRECISE) + b_excite)
        row_gate = jnp.dot(seg_table, gate_values, precision=PRECISE)
        scaled = (framed * row_gate[:, None, :]).reshape(expanded.shape)
        projected = jnp.dot(scaled, w_project, precision=PRECISE)
        return features + batch_norm(projected, gain_three, bias_three)
    output, pullback = jax.vjp(forward, features, w_expand, gain_one, bias_one, w_depth, gain_two, bias_two, w_reduce, b_reduce, w_excite, b_excite, w_project, gain_three, bias_three)
    grads = pullback(cotangent)
    return (output, grads[0], grads[1], grads[2], grads[3], grads[4], grads[5], grads[6], grads[7], grads[8], grads[9], grads[10], grads[11], grads[12], grads[13])
```

```python
import jax
import jax.numpy as jnp
from jax import lax
from jax.experimental import pallas as pl
from jax.experimental.pallas import tpu as pltpu
from jax.sharding import PartitionSpec as P

MESH = pl.DeviceIdType.MESH
F32 = jnp.float32
BF16 = jnp.bfloat16
EPSILON = 0.001
PRECISE = lax.Precision.HIGHEST
D = 112
SQZ = 28
EXP = 672
H, W, CELLS = 6, 4, 24
TAPS = 25
BLOCK, BLOCKS = 16, 6
ROWS = 2304
CHUNK = BLOCK * CELLS
LANE = 128
WIDE = 768
GROUPS = WIDE // LANE
TOTAL = 294912.0
OWN = 168
REST = OWN - LANE

AT_EXPAND, AT_DEPTH, AT_VECS, AT_PROJECT, AT_REDUCE, AT_EXCITE, PANEL = 0, 112, 137, 144, 256, 288, 320
AT_R, AT_X, AT_B = 32, 64, 96


def split(values):
    high = values.astype(BF16)
    return high, (values - high.astype(F32)).astype(BF16)


def mm(a, b):
    return lax.dot_general(a, b, (((1,), (0,)), ((), ())), preferred_element_type=F32)


def mm_nt(a, b):
    return lax.dot_general(a, b, (((1,), (1,)), ((), ())), preferred_element_type=F32)


def exact(a, b, dims):
    return lax.dot_general(a, b, ((dims[:1], dims[1:]), ((), ())), precision=PRECISE, preferred_element_type=F32)


def place():
    dp = lax.axis_index("dp")
    z = lax.axis_index("chan")
    return dp // 8, lax.rem(dp // 2, 4), lax.rem(dp, 2), z


def column_peers():
    x, y, c, z = place()
    mine = z * 2 + c
    peers = []
    for k in range(1, 8):
        r = lax.rem(mine + k, 8)
        peers.append((r, (x * 8 + y * 2 + lax.rem(r, 2), r // 2)))
    return mine, peers


def plane_peers():
    x, y, c, z = place()
    mine = x * 4 + y
    peers = []
    for k in range(1, 16):
        r = lax.rem(mine + k, 16)
        peers.append((r, ((r // 4) * 8 + lax.rem(r, 4) * 2 + c, z)))
    return mine, peers


def push(sources, slots, mine, peers, send, recv):
    for rank, device in peers:
        pltpu.make_async_remote_copy(
            src_ref=sources(rank),
            dst_ref=slots.at[mine],
            send_sem=send,
            recv_sem=recv,
            device_id=device,
            device_id_type=MESH,
        ).start()


def drain(view, sem):
    pltpu.make_async_copy(view, view, sem).wait()


def add_slots(slots, count):
    total = slots[0]
    for k in range(1, count):
        total = total + slots[k]
    return total


class Vector:
    def __init__(self, near, far, sems):
        self.near, self.far, self.sems = near, far, sems

    def start(self, value):
        self.mine, peers = column_peers()
        self.near[self.mine] = value
        push(lambda rank: self.near.at[self.mine], self.near, self.mine, peers, self.sems.at[0], self.sems.at[1])

    def middle(self):
        drain(self.near.at[pl.ds(0, 7)], self.sems.at[1])
        mine, peers = plane_peers()
        self.far[mine] = add_slots(self.near, 8)
        push(lambda rank: self.far.at[mine], self.far, mine, peers, self.sems.at[2], self.sems.at[3])

    def finish(self):
        drain(self.far.at[pl.ds(0, 15)], self.sems.at[3])
        return add_slots(self.far, 16)

    def close(self):
        drain(self.near.at[pl.ds(0, 7)], self.sems.at[0])
        drain(self.far.at[pl.ds(0, 15)], self.sems.at[2])


class Panel:
    def __init__(self, source, first, parts, second, third, sems, cut):
        self.source, self.first, self.parts, self.second, self.third = source, first, parts, second, third
        self.sems, self.cut = sems, cut

    def start(self):
        mine, peers = plane_peers()
        self.first[mine] = self.source[mine]
        push(lambda rank: self.source.at[rank], self.first, mine, peers, self.sems.at[0], self.sems.at[1])

    def middle(self):
        drain(self.first.at[pl.ds(0, 15)], self.sems.at[1])
        total = add_slots(self.first, 16)
        mine, peers = column_peers()
        if self.cut:
            for z in range(4):
                self.parts[z, :, 0:LANE] = total[:, z * LANE : (z + 1) * LANE]
                rest = 4 + z // 2
                self.parts[z, :, LANE : 2 * LANE] = total[:, rest * LANE : (rest + 1) * LANE]
            self.second[mine] = self.parts[mine // 2]
            push(lambda rank: self.parts.at[rank // 2], self.second, mine, peers, self.sems.at[2], self.sems.at[3])
        else:
            self.second[mine] = total
            push(lambda rank: self.second.at[mine], self.second, mine, peers, self.sems.at[2], self.sems.at[3])

    def last(self):
        drain(self.second.at[pl.ds(0, 7)], self.sems.at[3])
        mine, peers = plane_peers()
        self.third[mine] = add_slots(self.second, 8)
        push(lambda rank: self.third.at[mine], self.third, mine, peers, self.sems.at[4], self.sems.at[5])

    def finish(self):
        drain(self.third.at[pl.ds(0, 15)], self.sems.at[5])
        return self.third[...].reshape(128, self.third.shape[-1])

    def close(self):
        drain(self.first.at[pl.ds(0, 15)], self.sems.at[0])
        drain(self.second.at[pl.ds(0, 7)], self.sems.at[2])
        drain(self.third.at[pl.ds(0, 15)], self.sems.at[4])


def half_gate(values, scale, shift):
    h = values * scale + shift
    return h, jnp.tanh(h)


def slope_of(h, th):
    return (0.5 + 0.5 * th) * (1.0 + (h - h * th))


def sigmoid(v):
    return 1.0 / (1.0 + jnp.exp(-v))


def kernel(
    f_in, q_in, panel_in, vecs, units,
    out, igrad, o_expand, o_project, o_depth, o_reduce, o_excite, o_vecs, o_small,
    f_rows, q_rows, p_rows, f3, ft, pg3, pgt,
    e_ref, a1, dv, q2, act_hi, act_lo,
    gathered, we, wp, wr, wx, we_b, wp_b, wd, par, gw, cov_we,
    pool, gates, spread, gg, sums, vec, gp_panel, misc, ge_panel, g_panel,
    near1, far1, near2, far2, near3, far3,
    g_first, g_second, g_third,
    p_first, p_parts, p_second, p_third,
    m_first, m_parts, m_second, m_third,
    e_first, e_parts, e_second, e_third,
    w_sems, v_sems, s_sems,
):
    x, y, c, z = place()
    barrier = pltpu.get_barrier_semaphore()
    col_mine, col_peers = column_peers()
    plane_mine, pl_peers = plane_peers()
    for _, device in col_peers + pl_peers:
        pl.semaphore_signal(barrier, inc=1, device_id=device, device_id_type=MESH)
    pl.semaphore_wait(barrier, 22)

    gathered[z] = panel_in[...]
    sections = ((0, AT_DEPTH), (AT_DEPTH, AT_PROJECT), (AT_PROJECT, PANEL))
    for s, (lo, hi) in enumerate(sections):
        for k in range(1, 4):
            pltpu.make_async_remote_copy(
                src_ref=gathered.at[z, pl.ds(lo, hi - lo)],
                dst_ref=gathered.at[z, pl.ds(lo, hi - lo)],
                send_sem=w_sems.at[0, s],
                recv_sem=w_sems.at[1, s],
                device_id={"chan": lax.rem(z + k, 4)},
                device_id_type=MESH,
            ).start()

    def section(s, way):
        lo, hi = sections[s]
        drain(gathered.at[pl.ds(0, 3), pl.ds(lo, hi - lo)], w_sems.at[way, s])

    def assembled(lo, rows):
        parts = [gathered[k, lo : lo + rows, 0:LANE] for k in range(4)]
        for k in (0, 2):
            parts.append(gathered[k, lo : lo + rows, LANE : 2 * LANE] + gathered[k + 1, lo : lo + rows, LANE : 2 * LANE])
        return jnp.concatenate(parts, axis=1)

    lane = lax.broadcasted_iota(jnp.int32, (2, 8, LANE), 2)
    f_rows[...] = jnp.where(lax.broadcasted_iota(jnp.int32, (288, 8, LANE), 2) == D, 1.0, 0.0)
    q_rows[...] = jnp.zeros_like(q_rows)

    @pl.loop(0, BLOCKS)
    def _(b):
        for cell in range(CELLS):
            t = (b * CELLS + cell) * 2
            rows = pl.ds(b * CHUNK + cell, BLOCK, stride=CELLS)
            f_rows[pl.ds(t, 2), :, 0:D] = f_in[rows, :].reshape(2, 8, D)
            q_rows[pl.ds(t, 2), :, 0:D] = q_in[rows, :].reshape(2, 8, D)

    @pl.loop(0, 18)
    def _(i):
        v = f_rows[pl.ds(i * 16, 16)].reshape(128, LANE)
        rows = pl.ds(i * 128, 128)
        hi, lo = split(v)
        f3[rows, 0:128] = hi
        f3[rows, 128:256] = hi
        f3[rows, 256:384] = lo
        hi, lo = split(v.T)
        ft[0:128, rows] = hi
        ft[128:256, rows] = lo

    gram = mm(ft[...], f3[:, 128:384])
    gram = gram[0:128, 0:128] + (gram[0:128, 128:256] + gram[128:256, 0:128]) + gram[128:256, 128:256]
    g_panel[...] = gram.reshape(16, 8, LANE)
    reduce_g = Panel(g_panel, g_first, None, g_second, g_third, s_sems.at[0], False)
    reduce_g.start()

    section(0, 1)
    we[0:D, :] = assembled(0, D)
    we[D:128, :] = jnp.zeros((128 - D, WIDE), F32)
    hi, lo = split(we[...])
    we_b[0:128, :] = hi
    we_b[128:256, :] = lo

    @pl.loop(0, BLOCKS)
    def _(b):
        rows = pl.ds(b * CHUNK, CHUNK)
        for n in range(3):
            cols = slice(n * 256, (n + 1) * 256)
            r = mm(f3[rows, 0:256], we_b[:, cols]) + mm(f3[rows, 256:384], we_b[0:128, cols])
            e_ref[pl.ds(b * 48, 48), :, cols] = r.reshape(48, 8, 256)

    reduce_g.middle()
    section(1, 1)
    taps = assembled(AT_DEPTH, 32)
    for t in range(TAPS):
        wd[t] = jnp.broadcast_to(taps[t : t + 1], (8, WIDE))
    gain1, bias1, gain2, bias2, bx = [taps[TAPS + i : TAPS + i + 1] for i in range(5)]
    section(2, 1)
    wp[0:D, :] = assembled(AT_PROJECT, D)
    wp[D:128, :] = jnp.zeros((128 - D, WIDE), F32)
    wr[...] = assembled(AT_REDUCE, 32)
    wx[...] = assembled(AT_EXCITE, 32)
    reduce_g.last()
    gram = reduce_g.finish() * (1.0 / TOTAL)
    f_mean_row = gram[D : D + 1, :]
    f_mean = gram[:, D : D + 1]
    cov = gram - f_mean * f_mean_row
    cov_we[...] = exact(cov, we[...], (1, 0))
    mean1 = jnp.sum(we[...] * f_mean, axis=0, keepdims=True)
    inv1 = lax.rsqrt(jnp.sum(we[...] * cov_we[...], axis=0, keepdims=True) + EPSILON)
    s1 = gain1 * inv1
    t1 = bias1 - mean1 * s1

    def put(i, row):
        par[i] = jnp.broadcast_to(row, (8, WIDE))

    put(0, 0.5 * s1)
    put(1, 0.5 * t1)

    @pl.loop(0, GROUPS)
    def _(g):
        cols = pl.ds(pl.multiple_of(g * LANE, LANE), LANE)

        def block(b, carry):
            total, square = carry
            base = b * 48
            scale, shift = par[0, :, cols], par[1, :, cols]
            for cell in range(CELLS):
                at = pl.ds(base + 2 * cell, 2)
                h, th = half_gate(e_ref[at, :, cols], scale, shift)
                a1[at, :, cols] = h + h * th
            for i in range(H):
                acc = [None] * W
                for a in range(5):
                    ii = i + a - 2
                    if not 0 <= ii < H:
                        continue
                    w = [wd[a * 5 + k, :, cols] for k in range(5)]
                    for jj in range(W):
                        v = a1[pl.ds(base + 2 * (ii * W + jj), 2), :, cols]
                        for j in range(W):
                            k = jj - j + 2
                            if 0 <= k < 5:
                                term = v * w[k]
                                acc[j] = term if acc[j] is None else acc[j] + term
                for j in range(W):
                    dv[pl.ds(base + 2 * (i * W + j), 2), :, cols] = acc[j]
                    total = total + (acc[j][0] + acc[j][1])
                    sq = acc[j] * acc[j]
                    square = square + (sq[0] + sq[1])
            return total, square

        zero = jnp.zeros((8, LANE), F32)
        total, square = lax.fori_loop(0, BLOCKS, block, (zero, zero))
        sums[pl.ds(g, 1), :] = jnp.sum(total, axis=0, keepdims=True)
        sums[pl.ds(g + 8, 1), :] = jnp.sum(square, axis=0, keepdims=True)

    def wide(rows, first):
        return jnp.concatenate([rows[first + g : first + g + 1, :] for g in range(GROUPS)], axis=1)

    def reduce_vector(near, far, index, value):
        v = Vector(near, far, v_sems.at[index])
        v.start(value)
        v.middle()
        return v, v.finish()

    sum2, got = reduce_vector(near1, far1, 0, sums[...])
    mean2 = wide(got, 0) * (1.0 / TOTAL)
    inv2 = lax.rsqrt(wide(got, 8) * (1.0 / TOTAL) - mean2 * mean2 + EPSILON)
    s2 = gain2 * inv2
    t2 = bias2 - mean2 * s2
    put(2, 0.5 * s2)
    put(3, 0.5 * t2)

    @pl.loop(0, GROUPS)
    def _(g):
        cols = pl.ds(pl.multiple_of(g * LANE, LANE), LANE)

        @pl.loop(0, BLOCKS)
        def _(b):
            scale, shift = par[2, :, cols], par[3, :, cols]
            pooled = jnp.zeros((8, LANE), F32)
            for cell in range(CELLS):
                at = pl.ds(b * 48 + 2 * cell, 2)
                h, th = half_gate(dv[at, :, cols], scale, shift)
                act = h + h * th
                q2[at, :, cols] = slope_of(h, th)
                pooled = pooled + (act[0] + act[1])
                hi, lo = split(act.reshape(16, LANE))
                rows = pl.ds(b * CHUNK + 16 * cell, 16)
                act_hi[rows, cols] = hi
                act_lo[rows, cols] = lo
            pool[b, :, cols] = pooled

    seg = lax.broadcasted_iota(jnp.int32, (8, LANE), 0)
    blk = lax.broadcasted_iota(jnp.int32, (8, LANE), 1)
    u0, u1, u2 = units[z, 0], units[z, 1], units[z, 2]
    lower = jnp.where(seg == 0, 0, jnp.where(seg == 1, u0, u0 + u1))
    length = jnp.where(seg == 0, u0, jnp.where(seg == 1, u1, u2))
    member = jnp.where((seg < 3) & (blk >= lower) & (blk < lower + length), 1.0, 0.0)
    per_count = jnp.where(seg < 3, 1.0 / (length * (BLOCK * CELLS)).astype(F32), 0.0)[:, 0:1]
    live = jnp.where(seg < 3, 1.0, 0.0)[:, 0:1]

    pooled = jnp.zeros((8, WIDE), F32)
    for b in range(BLOCKS):
        pooled = pooled + member[:, b : b + 1] * jnp.sum(pool[b], axis=0, keepdims=True)
    pooled = pooled * per_count
    reduced = exact(pooled, wr[...], (1, 1)) + vecs[0:1, 0:32]
    sig_r = sigmoid(reduced)
    squeezed = reduced * sig_r * live
    gate = sigmoid(exact(squeezed, wx[...], (1, 0)) + bx)

    def of_blocks(rows, b):
        return jnp.sum(member[:, b : b + 1] * rows, axis=0, keepdims=True)

    for b in range(BLOCKS):
        gates[b : b + 1, :] = of_blocks(gate, b)

    def project(b, carry):
        rows = pl.ds(b * CHUNK, CHUNK)
        hi, lo = split(wp[...] * gates[pl.ds(b, 1), :])
        wp_b[b, 0:128, :] = hi
        wp_b[b, 128:256, :] = lo
        r = mm_nt(act_hi[rows, :], wp_b[b])
        r = r[:, 0:128] + r[:, 128:256] + mm_nt(act_lo[rows, :], wp_b[b, 0:128, :])
        r = r.reshape(48, 8, LANE)
        q = q_rows[pl.ds(b * 48, 48)]
        p_rows[pl.ds(b * 48, 48)] = r
        return tuple(old + jnp.sum(new, axis=0) for old, new in zip(carry, (r, r * r, q, q * r)))

    zero = jnp.zeros((8, LANE), F32)
    four = lax.fori_loop(0, BLOCKS, project, (zero,) * 4)
    for i in range(4):
        vec[i : i + 1, :] = jnp.sum(four[i], axis=0, keepdims=True)
    sum3, got = reduce_vector(near2, far2, 1, vec[...])
    got = got * (1.0 / TOTAL)
    gain3, bias3 = vecs[1:2, :], vecs[2:3, :]
    mean3 = got[0:1]
    inv3 = lax.rsqrt(got[1:2] - mean3 * mean3 + EPSILON)
    b3 = got[2:3]
    g3 = (got[3:4] - mean3 * got[2:3]) * inv3
    o_small[0:1, :] = g3[:, 0:D] * TOTAL
    o_small[1:2, :] = b3[:, 0:D] * TOTAL
    s3 = gain3 * inv3
    t3 = bias3 - mean3 * s3
    pg_p = -s3 * inv3 * g3
    pg_0 = -s3 * b3 - pg_p * mean3

    @pl.loop(0, BLOCKS)
    def _(b):
        for cell in range(CELLS):
            at = pl.ds(b * 48 + 2 * cell, 2)
            r = f_rows[at] + (p_rows[at] * s3 + t3)
            out[pl.ds(b * CHUNK + cell, BLOCK, stride=CELLS), :] = r.reshape(16, LANE)[:, 0:D]

    @pl.loop(0, 18)
    def _(i):
        at = pl.ds(i * 16, 16)
        v = (q_rows[at] * s3 + (p_rows[at] * pg_p + pg_0)).reshape(128, LANE)
        rows = pl.ds(i * 128, 128)
        hi, lo = split(v)
        pg3[rows, 0:128] = hi
        pg3[rows, 128:256] = hi
        pg3[rows, 256:384] = lo
        hi, lo = split(v.T)
        pgt[0:128, rows] = hi
        pgt[128:256, rows] = lo

    gp_panel[...] = jnp.zeros_like(gp_panel)
    for b in range(BLOCKS):
        rows = slice(b * CHUNK, (b + 1) * CHUNK)
        for n in range(3):
            cols = slice(n * 256, (n + 1) * 256)
            m = mm(pgt[:, rows], act_hi[rows, cols])
            m = m[0:128] + m[128:256] + mm(pgt[0:128, rows], act_lo[rows, cols])
            gg[b : b + 1, cols] = jnp.sum(m * wp[:, cols], axis=0, keepdims=True)
            gp_panel[:, :, cols] += (m * gates[b : b + 1, cols]).reshape(16, 8, 256)
    reduce_p = Panel(gp_panel, p_first, p_parts, p_second, p_third, s_sems.at[1], True)
    reduce_p.start()

    gate_grad = jnp.zeros((8, WIDE), F32)
    for b in range(BLOCKS):
        gate_grad = gate_grad + member[:, b : b + 1] * gg[b : b + 1, :]
    excite_in = gate_grad * gate * (1.0 - gate)
    misc[...] = jnp.zeros_like(misc)
    misc[AT_X // 8 : AT_X // 8 + 4] = exact(squeezed, excite_in, (0, 0)).reshape(4, 8, WIDE)
    reduced_grad = exact(excite_in, wx[...], (1, 1)) * (sig_r * (1.0 + reduced * (1.0 - sig_r))) * live
    misc[AT_R // 8 : AT_R // 8 + 4] = exact(reduced_grad, pooled, (0, 0)).reshape(4, 8, WIDE)
    misc[AT_B // 8, 0:1, :] = jnp.sum(excite_in, axis=0, keepdims=True)
    for k in range(4):
        misc[AT_B // 8, 1:2, k * LANE : k * LANE + 32] = jnp.sum(reduced_grad, axis=0, keepdims=True)
    pooled_grad = exact(reduced_grad, wr[...], (1, 0)) * per_count
    for b in range(BLOCKS):
        spread[b : b + 1, :] = of_blocks(pooled_grad, b)

    par[8] = jnp.zeros((8, WIDE), F32)
    par[9] = jnp.zeros((8, WIDE), F32)

    @pl.loop(0, BLOCKS)
    def _(b):
        rows = pl.ds(b * CHUNK, CHUNK)
        at = pl.ds(b * 48, 48)
        for n in range(3):
            cols = slice(n * 256, (n + 1) * 256)
            r = mm(pg3[rows, 0:256], wp_b[b, :, cols]) + mm(pg3[rows, 256:384], wp_b[b, 0:128, cols])
            r = (r.reshape(48, 8, 256) + spread[pl.ds(b, 1), cols]) * q2[at, :, cols]
            q2[at, :, cols] = r
            par[8, :, cols] += jnp.sum(r, axis=0)
            par[9, :, cols] += jnp.sum(r * dv[at, :, cols], axis=0)

    for g in range(GROUPS):
        cols = slice(g * LANE, (g + 1) * LANE)
        sums[g : g + 1, :] = jnp.sum(par[8, :, cols], axis=0, keepdims=True)
        sums[g + 8 : g + 9, :] = jnp.sum(par[9, :, cols], axis=0, keepdims=True)
    sum4, got = reduce_vector(near3.at[0], far3.at[0], 2, sums[...])
    b2 = wide(got, 0)
    g2 = (wide(got, 8) - mean2 * b2) * inv2
    c1 = s2
    c3 = -s2 * inv2 * g2 * (1.0 / TOTAL)
    c2 = -s2 * b2 * (1.0 / TOTAL) - c3 * mean2
    put(4, c1)
    put(5, c2)
    put(6, c3)

    def own_lanes(rows):
        first = rows[:, 0:LANE]
        rest = rows[:, LANE : 2 * LANE]
        rest = jnp.where(lax.rem(z, 2) == 1, pltpu.roll(rest, 64, 1), rest)
        return first, rest

    def own_vector(row):
        first = jnp.zeros((1, LANE), F32)
        rest = jnp.zeros((1, LANE), F32)
        for k in range(4):
            first = jnp.where(z == k, row[:, k * LANE : (k + 1) * LANE], first)
        for k in range(2):
            rest = jnp.where(z // 2 == k, row[:, (4 + k) * LANE : (5 + k) * LANE], rest)
        rest = jnp.where(lax.rem(z, 2) == 1, pltpu.roll(rest, 64, 1), rest)
        return first, rest

    def emit_vector(i, row):
        first, rest = own_vector(row)
        o_vecs[i : i + 1, 0:LANE] = first
        o_vecs[i : i + 1, LANE:OWN] = rest[:, 0:REST]

    emit_vector(2, g2)
    emit_vector(3, b2)

    gw[...] = jnp.zeros_like(gw)

    @pl.loop(0, GROUPS)
    def _(g):
        cols = pl.ds(pl.multiple_of(g * LANE, LANE), LANE)

        def block(b, carry):
            total, product = carry
            base = b * 48
            k1, k2, k3 = par[4, :, cols], par[5, :, cols], par[6, :, cols]
            for cell in range(CELLS):
                at = pl.ds(base + 2 * cell, 2)
                q2[at, :, cols] = q2[at, :, cols] * k1 + (dv[at, :, cols] * k3 + k2)
            scale, shift = par[0, :, cols], par[1, :, cols]
            for ip in range(H):
                act = [a1[pl.ds(base + 2 * (ip * W + jp), 2), :, cols] for jp in range(W)]
                acc = [None] * W
                for a in range(5):
                    i = ip - a + 2
                    if not 0 <= i < H:
                        continue
                    w = [wd[a * 5 + k, :, cols] for k in range(5)]
                    part = [None] * 5
                    for j in range(W):
                        v = q2[pl.ds(base + 2 * (i * W + j), 2), :, cols]
                        for jp in range(W):
                            k = jp - j + 2
                            if 0 <= k < 5:
                                term = v * w[k]
                                acc[jp] = term if acc[jp] is None else acc[jp] + term
                                prod = v * act[jp]
                                part[k] = prod if part[k] is None else part[k] + prod
                    for k in range(5):
                        gw[a * 5 + k, :, cols] += part[k][0] + part[k][1]
                for jp in range(W):
                    at = pl.ds(base + 2 * (ip * W + jp), 2)
                    e = e_ref[at, :, cols]
                    h, th = half_gate(e, scale, shift)
                    q = acc[jp] * slope_of(h, th)
                    hi, lo = split(q.reshape(16, LANE))
                    rows = pl.ds(b * CHUNK + 16 * (ip * W + jp), 16)
                    act_hi[rows, cols] = hi
                    act_lo[rows, cols] = lo
                    total = total + (q[0] + q[1])
                    qe = q * e
                    product = product + (qe[0] + qe[1])
            return total, product

        zero = jnp.zeros((8, LANE), F32)
        total, product = lax.fori_loop(0, BLOCKS, block, (zero, zero))
        sums[pl.ds(g, 1), :] = jnp.sum(total, axis=0, keepdims=True)
        sums[pl.ds(g + 8, 1), :] = jnp.sum(product, axis=0, keepdims=True)

    sum5 = Vector(near3.at[1], far3.at[1], v_sems.at[3])
    sum5.start(sums[...])
    for t in range(TAPS):
        misc[t // 8, t % 8 : t % 8 + 1, :] = jnp.sum(gw[t], axis=0, keepdims=True)
    reduce_m = Panel(misc, m_first, m_parts, m_second, m_third, s_sems.at[2], True)
    reduce_m.start()
    for n in range(3):
        cols = slice(n * 256, (n + 1) * 256)
        m = mm(ft[...], act_hi[:, cols])
        m = m[0:128] + m[128:256] + mm(ft[0:128, :], act_lo[:, cols])
        ge_panel[:, :, cols] = m.reshape(16, 8, 256)
    reduce_e = Panel(ge_panel, e_first, e_parts, e_second, e_third, s_sems.at[3], True)
    reduce_e.start()
    sum5.middle()
    reduce_p.middle()
    reduce_m.middle()
    reduce_e.middle()
    reduce_p.last()
    got = sum5.finish()
    reduce_m.last()
    reduce_e.last()
    b1 = wide(got, 0)
    g1 = (wide(got, 8) - mean1 * b1) * inv1
    emit_vector(0, g1)
    emit_vector(1, b1)
    k3 = -s1 * inv1 * g1 * (1.0 / TOTAL)
    k2 = -s1 * b1 * (1.0 / TOTAL) - k3 * mean1
    hi, lo = split(we[...] * s1)
    we_b[0:128, :] = hi
    we_b[128:256, :] = lo
    mix = exact(we[...] * k3, we[...], (1, 1))
    const = exact(jnp.broadcast_to(k2, (8, WIDE)), we[...], (1, 1))[0:1, :]
    mix = jnp.where(lax.broadcasted_iota(jnp.int32, (128, LANE), 0) == D, const, mix)
    mix_hi, mix_lo = split(mix)
    mix_all = jnp.concatenate([mix_hi, mix_lo], axis=0)

    @pl.loop(0, BLOCKS)
    def _(b):
        rows = pl.ds(b * CHUNK, CHUNK)
        r = mm_nt(act_hi[rows, :], we_b[...])
        r = r[:, 0:128] + r[:, 128:256] + mm_nt(act_lo[rows, :], we_b[0:128, :])
        r = r + mm(f3[rows, 0:256], mix_all) + mm(f3[rows, 256:384], mix_hi)
        r = q_rows[pl.ds(b * 48, 48)] + r.reshape(48, 8, LANE)
        p_rows[pl.ds(b * 48, 48)] = r
        for cell in range(CELLS):
            at = pl.ds(b * 48 + 2 * cell, 2)
            igrad[pl.ds(b * CHUNK + cell, BLOCK, stride=CELLS), :] = p_rows[at].reshape(16, LANE)[:, 0:D]

    def own_wide(rows):
        first = jnp.zeros((rows.shape[0], LANE), F32)
        rest = jnp.zeros((rows.shape[0], LANE), F32)
        for k in range(4):
            first = jnp.where(z == k, rows[:, k * LANE : (k + 1) * LANE], first)
        for k in range(2):
            rest = jnp.where(z // 2 == k, rows[:, (4 + k) * LANE : (5 + k) * LANE], rest)
        return jnp.concatenate([first, rest], axis=1)

    total_p = reduce_p.finish()
    first, rest = own_lanes(total_p)
    o_project[0:LANE, :] = first.T[:, 0:D]
    o_project[LANE:OWN, :] = rest.T[0:REST, 0:D]
    total_m = reduce_m.finish()
    first, rest = own_lanes(total_m)
    o_depth[:, 0:LANE] = first[0:TAPS]
    o_depth[:, LANE:OWN] = rest[0:TAPS, 0:REST]
    o_excite[:, 0:LANE] = first[AT_X : AT_X + SQZ]
    o_excite[:, LANE:OWN] = rest[AT_X : AT_X + SQZ, 0:REST]
    o_reduce[0:LANE, :] = first.T[:, AT_R : AT_R + SQZ]
    o_reduce[LANE:OWN, :] = rest.T[0:REST, AT_R : AT_R + SQZ]
    o_vecs[4:5, 0:LANE] = first[AT_B : AT_B + 1]
    o_vecs[4:5, LANE:OWN] = rest[AT_B : AT_B + 1, 0:REST]
    o_small[2:3, :] = first[AT_B + 1 : AT_B + 2, 0:D]
    total_e = reduce_e.finish()
    fix = own_wide(s1) * (total_e - f_mean * own_wide(b1) - own_wide(cov_we[...]) * own_wide(inv1 * g1))
    first, rest = own_lanes(fix)
    o_expand[:, 0:LANE] = first[0:D]
    o_expand[:, LANE:OWN] = rest[0:D, 0:REST]

    for s in range(3):
        section(s, 0)
    for item in (reduce_g, sum2, sum3, sum4, sum5, reduce_p, reduce_m, reduce_e):
        item.close()


def body(
    features, seg_units, w_expand, gain_one, bias_one, w_depth, gain_two, bias_two,
    w_reduce, b_reduce, w_excite, b_excite, w_project, gain_three, bias_three, cotangent,
):
    z = lax.axis_index("chan")
    rows = jnp.concatenate(
        [
            w_expand,
            w_depth.reshape(TAPS, OWN),
            jnp.stack([gain_one, bias_one, gain_two, bias_two, b_excite]),
            jnp.zeros((2, OWN), F32),
            w_project.T,
            w_reduce.T,
            jnp.zeros((4, OWN), F32),
            w_excite,
            jnp.zeros((4, OWN), F32),
        ],
        axis=0,
    )
    rest = jnp.pad(rows[:, LANE:], ((0, 0), (0, 64 - REST)))
    blank = jnp.zeros_like(rest)
    odd = lax.rem(z, 2) == 1
    panel = jnp.concatenate([rows[:, :LANE], jnp.where(odd, blank, rest), jnp.where(odd, rest, blank)], axis=1)
    small = jnp.stack(
        [
            jnp.pad(b_reduce, (0, LANE - SQZ)),
            jnp.pad(gain_three, (0, LANE - D)),
            jnp.pad(bias_three, (0, LANE - D)),
        ]
    )
    small = jnp.pad(small, ((0, 5), (0, 0)))
    vm = pl.BlockSpec(memory_space=pltpu.VMEM)
    big = pltpu.VMEM((288, 8, WIDE), F32)
    rows128 = pltpu.VMEM((288, 8, LANE), F32)
    half = pltpu.VMEM((ROWS, WIDE), BF16)

    def f32(*shape):
        return pltpu.VMEM(shape, F32)

    def b16(*shape):
        return pltpu.VMEM(shape, BF16)

    panel_scratch = [f32(16, 8, WIDE), f32(4, 8, 256), f32(8, 8, 256), f32(16, 8, 256)]
    result = pl.pallas_call(
        kernel,
        out_shape=(
            jax.ShapeDtypeStruct((ROWS, D), F32),
            jax.ShapeDtypeStruct((ROWS, D), F32),
            jax.ShapeDtypeStruct((D, OWN), F32),
            jax.ShapeDtypeStruct((OWN, D), F32),
            jax.ShapeDtypeStruct((TAPS, OWN), F32),
            jax.ShapeDtypeStruct((OWN, SQZ), F32),
            jax.ShapeDtypeStruct((SQZ, OWN), F32),
            jax.ShapeDtypeStruct((8, OWN), F32),
            jax.ShapeDtypeStruct((8, D), F32),
        ),
        in_specs=[vm, vm, vm, vm, pl.BlockSpec(memory_space=pltpu.SMEM)],
        out_specs=(vm,) * 9,
        scratch_shapes=[
            rows128, rows128, rows128, b16(ROWS, 384), b16(256, ROWS), b16(ROWS, 384), b16(256, ROWS),
            big, big, big, big, half, half,
            f32(4, PANEL, 256), f32(128, WIDE), f32(128, WIDE), f32(32, WIDE), f32(32, WIDE),
            b16(256, WIDE), b16(BLOCKS, 256, WIDE), f32(TAPS, 8, WIDE), f32(10, 8, WIDE), f32(TAPS, 8, WIDE), f32(128, WIDE),
            f32(8, 8, WIDE), f32(8, WIDE), f32(8, WIDE), f32(8, WIDE), f32(16, LANE), f32(8, LANE),
            f32(16, 8, WIDE), f32(16, 8, WIDE), f32(16, 8, WIDE), f32(16, 8, LANE),
            f32(8, 16, LANE), f32(16, 16, LANE), f32(8, 8, LANE), f32(16, 8, LANE), f32(2, 8, 16, LANE), f32(2, 16, 16, LANE),
            f32(16, 8, LANE), f32(8, 8, LANE), f32(16, 8, LANE),
        ]
        + panel_scratch * 3
        + [
            pltpu.SemaphoreType.DMA((2, 3)),
            pltpu.SemaphoreType.DMA((4, 4)),
            pltpu.SemaphoreType.DMA((4, 6)),
        ],
        compiler_params=pltpu.CompilerParams(
            collective_id=0, has_side_effects=True, vmem_limit_bytes=64 * 1024 * 1024 - 65536
        ),
    )(features, cotangent, panel, small, seg_units)
    out, igrad, expand, project, depth, reduce, excite, vecs, little = result
    return (
        out,
        igrad,
        expand,
        vecs[0],
        vecs[1],
        depth.reshape(5, 5, OWN),
        vecs[2],
        vecs[3],
        reduce,
        little[2, :SQZ],
        excite,
        vecs[4],
        project,
        little[0],
        little[1],
    )


def solution(mesh):
    placed = (
        P(("dp", "chan"), None),
        P("dp", None),
        P(None, "chan"),
        P("chan"),
        P("chan"),
        P(None, None, "chan"),
        P("chan"),
        P("chan"),
        P("chan", None),
        P(),
        P(None, "chan"),
        P("chan"),
        P("chan", None),
        P(),
        P(),
        P(("dp", "chan"), None),
    )
    return jax.shard_map(
        body,
        mesh=mesh,
        in_specs=placed,
        out_specs=(
            P(("dp", "chan"), None),
            P(("dp", "chan"), None),
            P(None, "chan"),
            P("chan"),
            P("chan"),
            P(None, None, "chan"),
            P("chan"),
            P("chan"),
            P("chan", None),
            P(),
            P(None, "chan"),
            P("chan"),
            P("chan", None),
            P(),
            P(),
        ),
        check_vma=False,
    )
```

```python
import jax
import jax.numpy as jnp
from jax import lax
from jax.experimental import pallas as pl
from jax.experimental.pallas import tpu as pltpu
from jax.sharding import PartitionSpec as P

MESH = pl.DeviceIdType.MESH
F32 = jnp.float32
BF16 = jnp.bfloat16
EPSILON = 0.001
PRECISE = lax.Precision.HIGHEST
D = 112
SQZ = 28
EXP = 672
H, W, CELLS = 6, 4, 24
TAPS = 25
BLOCK, BLOCKS = 16, 6
ROWS = 2304
CHUNK = BLOCK * CELLS
LANE = 128
WIDE = 768
GROUPS = WIDE // LANE
TOTAL = 294912.0
OWN = 168
REST = OWN - LANE

AT_EXPAND, AT_DEPTH, AT_VECS, AT_PROJECT, AT_REDUCE, AT_EXCITE, PANEL = 0, 112, 137, 144, 256, 288, 320
AT_R, AT_X, AT_B = 32, 64, 96
OUT_PROJECT, OUT_MISC, OUT_VECS, OUT_SMALL, RESULTS = 128, 256, 384, 392, 400
GROUP = 2 * LANE


REPS = {}


def rep(name):
    count = REPS.get(name, 1)

    def run(fn):
        if count == 1:
            fn()
        else:
            lax.fori_loop(0, count, lambda i, carry: (fn(), carry)[1], 0)

    return run


def rloop(name, size):
    count = REPS.get(name, 1)

    def run(fn):
        if count == 1:
            pl.loop(0, size)(fn)
        else:
            pl.loop(0, size * count)(lambda i: fn(lax.rem(i, size)))

    return run


def split(values):
    high = values.astype(BF16)
    return high, (values - high.astype(F32)).astype(BF16)


def mm(a, b):
    return lax.dot_general(a, b, (((1,), (0,)), ((), ())), preferred_element_type=F32)


def mm_nt(a, b):
    return lax.dot_general(a, b, (((1,), (1,)), ((), ())), preferred_element_type=F32)


def exact(a, b, dims):
    return lax.dot_general(a, b, ((dims[:1], dims[1:]), ((), ())), precision=PRECISE, preferred_element_type=F32)


def place():
    dp = lax.axis_index("dp")
    z = lax.axis_index("chan")
    return dp // 8, lax.rem(dp // 2, 4), lax.rem(dp, 2), z


def ring(step):
    return min(step, 4 - step)


def column_peers():
    x, y, c, z = place()
    moves = [(dz, dc) for dz in range(4) for dc in range(2) if dz or dc]
    moves.sort(key=lambda m: -10 * ring(m[0]) - m[1])
    peers = []
    for dz, dc in moves:
        pz, pc = lax.rem(z + dz, 4), lax.rem(c + dc, 2)
        peers.append((pz * 2 + pc, (x * 8 + y * 2 + pc, pz)))
    return z * 2 + c, peers


def plane_peers():
    x, y, c, z = place()
    moves = [(dx, dy) for dx in range(4) for dy in range(4) if dx or dy]
    moves.sort(key=lambda m: -ring(m[0]) - ring(m[1]))
    peers = []
    for dx, dy in moves:
        px, py = lax.rem(x + dx, 4), lax.rem(y + dy, 4)
        peers.append((px * 4 + py, (px * 8 + py * 2 + c, z)))
    return x * 4 + y, peers


def push(sources, slots, mine, peers, send, recv):
    for rank, device in peers:
        pltpu.make_async_remote_copy(
            src_ref=sources(rank),
            dst_ref=slots.at[mine],
            send_sem=send,
            recv_sem=recv,
            device_id=device,
            device_id_type=MESH,
        ).start()


def drain(view, sem):
    pltpu.make_async_copy(view, view, sem).wait()


def add_slots(slots, count):
    total = slots[0]
    for k in range(1, count):
        total = total + slots[k]
    return total


class Vector:
    def __init__(self, near, far, sems):
        self.near, self.far, self.sems = near, far, sems

    def start(self, value):
        mine, peers = column_peers()
        self.near[mine] = value
        push(lambda rank: self.near.at[mine], self.near, mine, peers, self.sems.at[0], self.sems.at[1])

    def middle(self):
        drain(self.near.at[pl.ds(0, 7)], self.sems.at[1])
        mine, peers = plane_peers()
        self.far[mine] = add_slots(self.near, 8)
        push(lambda rank: self.far.at[mine], self.far, mine, peers, self.sems.at[2], self.sems.at[3])

    def finish(self):
        drain(self.far.at[pl.ds(0, 15)], self.sems.at[3])
        return add_slots(self.far, 16)

    def close(self):
        drain(self.near.at[pl.ds(0, 7)], self.sems.at[0])
        drain(self.far.at[pl.ds(0, 15)], self.sems.at[2])


class Square:
    def __init__(self, source, first, second, third, sems):
        self.source, self.first, self.second, self.third, self.sems = source, first, second, third, sems

    def start(self):
        mine, peers = column_peers()
        self.first[mine] = self.source[mine]
        push(lambda rank: self.source.at[rank], self.first, mine, peers, self.sems.at[0], self.sems.at[1])

    def middle(self):
        drain(self.first.at[pl.ds(0, 7)], self.sems.at[1])
        mine, peers = plane_peers()
        self.second[mine] = add_slots(self.first, 8)
        push(lambda rank: self.second.at[mine], self.second, mine, peers, self.sems.at[2], self.sems.at[3])

    def last(self):
        drain(self.second.at[pl.ds(0, 15)], self.sems.at[3])
        mine, peers = column_peers()
        self.third[mine] = add_slots(self.second, 16)
        push(lambda rank: self.third.at[mine], self.third, mine, peers, self.sems.at[4], self.sems.at[5])

    def finish(self):
        drain(self.third.at[pl.ds(0, 7)], self.sems.at[5])
        return self.third[...].reshape(128, LANE)

    def close(self):
        drain(self.first.at[pl.ds(0, 7)], self.sems.at[0])
        drain(self.second.at[pl.ds(0, 15)], self.sems.at[2])
        drain(self.third.at[pl.ds(0, 7)], self.sems.at[4])


class Panel:
    def __init__(self, source, first, parts, second, third, sems):
        self.source, self.first, self.parts, self.second, self.third, self.sems = source, first, parts, second, third, sems

    def start(self, group):
        mine, peers = plane_peers()
        self.first[group, mine] = self.source[group, mine]
        push(
            lambda rank: self.source.at[group, rank], self.first.at[group], mine, peers,
            self.sems.at[0], self.sems.at[1 + group],
        )

    def middle(self):
        totals = []
        for group in range(3):
            drain(self.first.at[group, pl.ds(0, 15)], self.sems.at[1 + group])
            totals.append(add_slots(self.first.at[group], 16))
        mine, peers = column_peers()
        for z in range(4):
            half = (z % 2) * LANE
            self.parts[z, :, 0:LANE] = totals[z // 2][:, half : half + LANE]
            half = (z // 2) * LANE
            self.parts[z, :, LANE:GROUP] = totals[2][:, half : half + LANE]
        self.second[mine] = self.parts[mine // 2]
        push(lambda rank: self.parts.at[rank // 2], self.second, mine, peers, self.sems.at[4], self.sems.at[5])

    def last(self):
        drain(self.second.at[pl.ds(0, 7)], self.sems.at[5])
        mine, peers = plane_peers()
        self.third[mine] = add_slots(self.second, 8)
        push(lambda rank: self.third.at[mine], self.third, mine, peers, self.sems.at[6], self.sems.at[7])

    def finish(self):
        drain(self.third.at[pl.ds(0, 15)], self.sems.at[7])
        return self.third[...].reshape(128, GROUP)

    def close(self):
        for group in range(3):
            drain(self.first.at[group, pl.ds(0, 15)], self.sems.at[0])
        drain(self.second.at[pl.ds(0, 7)], self.sems.at[4])
        drain(self.third.at[pl.ds(0, 15)], self.sems.at[6])


def half_gate(values, scale, shift):
    h = values * scale + shift
    return h, jnp.tanh(h)


def slope_of(h, th):
    return (0.5 + 0.5 * th) * (1.0 + (h - h * th))


def sigmoid(v):
    return 1.0 / (1.0 + jnp.exp(-v))


def lanes_of(g):
    return pl.ds(pl.multiple_of(g * LANE, LANE), LANE)


def fold(v):
    return v[0] + v[1]


def row_sum(v):
    return jnp.sum(v, axis=0, keepdims=True)


def products(target, left, right, base, cols):
    for a in range(5):
        acc = [None] * 5
        for i in range(H):
            ii = i + a - 2
            if not 0 <= ii < H:
                continue
            other = [right[pl.ds(base + 2 * (ii * W + jj), 2), :, cols] for jj in range(W)]
            for j in range(W):
                v = left[pl.ds(base + 2 * (i * W + j), 2), :, cols]
                for jj in range(W):
                    k = jj - j + 2
                    if 0 <= k < 5:
                        term = v * other[jj]
                        acc[k] = term if acc[k] is None else acc[k] + term
        for k in range(5):
            target[a * 5 + k, :, cols] += fold(acc[k])


def kernel(
    f_in, q_in, we_in, wp_in, wr_in, wx_in, wd_in, ga1_in, bi1_in, ga2_in, bi2_in, bx_in, br_in, ga3_in, bi3_in, units,
    out, igrad, o_panel,
    stage, wide_stage,
    f_rows, q_rows, p_rows, f3, ft, pg3, pgt,
    e_ref, a1, dv, q2, act_hi, act_lo,
    gathered, we, wp, wr, wx, we_b, wp_b, wd, par, tq, td, cells, cov_we,
    pool, gates, spread, gg, vec, sums, gp_panel, misc, ge_panel, g_panel,
    near, far,
    g_first, g_second, g_third,
    p_first, p_parts, p_second, p_third,
    m_first, m_parts, m_second, m_third,
    e_first, e_parts, e_second, e_third,
    w_sems, v_sems, g_sems, s_sems,
):
    x, y, c, z = place()
    barrier = pltpu.get_barrier_semaphore()
    for _, device in column_peers()[1] + plane_peers()[1]:
        pl.semaphore_signal(barrier, inc=1, device_id=device, device_id_type=MESH)

    vectors = [Vector(near.at[i], far.at[i], v_sems.at[i]) for i in range(7)]
    sum2a, sum2b, sum3, sum4a, sum4b, sum5a, sum5b = vectors
    reduce_g = Square(g_panel, g_first, g_second, g_third, g_sems)
    reduce_p = Panel(gp_panel, p_first, p_parts, p_second, p_third, s_sems.at[0])
    reduce_m = Panel(misc, m_first, m_parts, m_second, m_third, s_sems.at[1])
    reduce_e = Panel(ge_panel, e_first, e_parts, e_second, e_third, s_sems.at[2])

    ones = jnp.where(lax.broadcasted_iota(jnp.int32, (16, ROWS), 0) == 0, 1.0, 0.0)
    hi, lo = split(jnp.concatenate([f_in[...], ones], axis=0))
    ft[0:128, :] = hi
    ft[128:256, :] = lo
    gram = mm_nt(ft[...], ft[...])
    gram = gram[0:128, 0:128] + (gram[0:128, 128:256] + gram[128:256, 0:128]) + gram[128:256, 128:256]
    g_panel[...] = gram.reshape(8, 16, LANE)
    pl.semaphore_wait(barrier, 22)
    reduce_g.start()

    sections = ((0, AT_DEPTH), (AT_DEPTH, AT_PROJECT), (AT_PROJECT, PANEL))
    odd = lax.rem(z, 2) == 1

    def send_section(s):
        lo, hi = sections[s]
        rest = gathered[z, lo:hi, LANE:GROUP]
        gathered[z, lo:hi, LANE:GROUP] = jnp.where(odd, pltpu.roll(rest, 64, 1), rest)
        for k in (2, 1, 3):
            pltpu.make_async_remote_copy(
                src_ref=gathered.at[z, pl.ds(lo, hi - lo)],
                dst_ref=gathered.at[z, pl.ds(lo, hi - lo)],
                send_sem=w_sems.at[0, s],
                recv_sem=w_sems.at[1, s],
                device_id={"chan": lax.rem(z + k, 4)},
                device_id_type=MESH,
            ).start()

    def section(s, way):
        lo, hi = sections[s]
        drain(gathered.at[pl.ds(0, 3), pl.ds(lo, hi - lo)], w_sems.at[way, s])

    def assembled(lo, rows):
        parts = [gathered[k, lo : lo + rows, 0:LANE] for k in range(4)]
        for k in (0, 2):
            parts.append(gathered[k, lo : lo + rows, LANE:GROUP] + gathered[k + 1, lo : lo + rows, LANE:GROUP])
        return jnp.concatenate(parts, axis=1)

    gathered[z] = jnp.zeros((PANEL, GROUP), F32)
    wide_stage[...] = jnp.zeros_like(wide_stage)
    wide_stage[0:OWN, 0:D] = we_in[...]
    gathered[z, 0:D, :] = wide_stage[...].T[0:D]
    send_section(0)
    for a in range(5):
        gathered[z, AT_DEPTH + 5 * a : AT_DEPTH + 5 * a + 5, 0:OWN] = wd_in[a]
    for i, row in enumerate((ga1_in, bi1_in, ga2_in, bi2_in, bx_in)):
        gathered[z, AT_VECS + i : AT_VECS + i + 1, 0:OWN] = row[...]
    send_section(1)

    tail = jnp.where(lax.broadcasted_iota(jnp.int32, (16, LANE), 0) == 0, 1.0, 0.0)

    def rows_of(source, tail, target):
        @pl.loop(0, BLOCKS)
        def _(b):
            for i in range(3):
                v = source[:, pl.ds(pl.multiple_of(b * CHUNK + i * LANE, LANE), LANE)]
                stage[i * LANE : (i + 1) * LANE, :] = jnp.concatenate([v, tail], axis=0).T
            for cell in range(CELLS):
                v = stage[pl.ds(cell, BLOCK, stride=CELLS), :]
                target[pl.ds((b * CELLS + cell) * 2, 2)] = v.reshape(2, 8, LANE)

    rows_of(f_in, tail, f_rows)

    @rloop("ft", 18)
    def _(i):
        v = f_rows[pl.ds(i * 16, 16)].reshape(128, LANE)
        rows = pl.ds(pl.multiple_of(i * 128, 128), 128)
        hi, lo = split(v)
        f3[rows, 0:128] = hi
        f3[rows, 128:256] = hi
        f3[rows, 256:384] = lo
        hi, lo = split(v.T)
        ft[0:128, rows] = hi
        ft[128:256, rows] = lo

    reduce_g.middle()

    section(0, 1)
    we[0:D, :] = assembled(0, D)
    we[D:128, :] = jnp.zeros((128 - D, WIDE), F32)
    hi, lo = split(we[...])
    we_b[0:128, :] = hi
    we_b[128:256, :] = lo

    @rloop("E", BLOCKS)
    def _(b):
        rows = pl.ds(pl.multiple_of(b * CHUNK, CHUNK), CHUNK)
        for n in range(3):
            cols = slice(n * GROUP, (n + 1) * GROUP)
            r = mm(f3[rows, 0:256], we_b[:, cols]) + mm(f3[rows, 256:384], we_b[0:128, cols])
            e_ref[pl.ds(b * 48, 48), :, cols] = r.reshape(48, 8, GROUP)

    reduce_g.last()
    section(1, 1)
    taps = assembled(AT_DEPTH, 32)
    for t in range(TAPS):
        wd[t] = jnp.broadcast_to(taps[t : t + 1], (8, WIDE))
    gain1, bias1, gain2, bias2, bx = [taps[TAPS + i : TAPS + i + 1] for i in range(5)]
    rows_of(q_in, jnp.zeros((16, LANE), F32), q_rows)
    sums[...] = jnp.zeros_like(sums)
    tq[...] = jnp.zeros_like(tq)
    td[...] = jnp.zeros_like(td)
    cells[...] = jnp.zeros_like(cells)

    gram = reduce_g.finish() * (1.0 / TOTAL)
    wide_stage[0:OWN, 0:D] = wp_in[...]
    gathered[z, AT_PROJECT : AT_PROJECT + D, :] = wide_stage[...].T[0:D]
    gathered[z, AT_REDUCE : AT_REDUCE + SQZ, 0:OWN] = wr_in[...]
    gathered[z, AT_EXCITE : AT_EXCITE + SQZ, 0:OWN] = wx_in[...]
    send_section(2)
    f_mean_row = gram[D : D + 1, :]
    f_mean = gram[:, D : D + 1]
    cov = gram - f_mean * f_mean_row
    cov_we[...] = exact(cov, we[...], (1, 0))
    mean1 = row_sum(we[...] * f_mean)
    inv1 = lax.rsqrt(row_sum(we[...] * cov_we[...]) + EPSILON)
    s1 = gain1 * inv1
    t1 = bias1 - mean1 * s1

    def put(i, row, lo=0, hi=WIDE):
        par[i, :, lo:hi] = jnp.broadcast_to(row, (8, hi - lo))

    put(0, 0.5 * s1)
    put(1, 0.5 * t1)

    def put_sums(first, second, g, low, size):
        sums[pl.ds(g - low, 1), :] = row_sum(first)
        sums[pl.ds(g - low + size, 1), :] = row_sum(second)

    @rloop("conv1", GROUPS)
    def _(g):
        cols = lanes_of(g)

        def block(b, carry):
            total, square = carry
            base = b * 48
            scale, shift = par[0, :, cols], par[1, :, cols]
            for cell in range(CELLS):
                at = pl.ds(base + 2 * cell, 2)
                h, th = half_gate(e_ref[at, :, cols], scale, shift)
                a1[at, :, cols] = h + h * th
            for i in range(H):
                acc = [None] * W
                for a in range(5):
                    ii = i + a - 2
                    if not 0 <= ii < H:
                        continue
                    w = [wd[a * 5 + k, :, cols] for k in range(5)]
                    for jj in range(W):
                        v = a1[pl.ds(base + 2 * (ii * W + jj), 2), :, cols]
                        for j in range(W):
                            k = jj - j + 2
                            if 0 <= k < 5:
                                term = v * w[k]
                                acc[j] = term if acc[j] is None else acc[j] + term
                for j in range(W):
                    dv[pl.ds(base + 2 * (i * W + j), 2), :, cols] = acc[j]
                    total = total + fold(acc[j])
                    square = square + fold(acc[j] * acc[j])
            return total, square

        zero = jnp.zeros((8, LANE), F32)
        total, square = lax.fori_loop(0, BLOCKS, block, (zero, zero))
        put_sums(total, square, g, jnp.where(g < 3, 0, 3), 3)

        @pl.when(g == 2)
        def _():
            sum2a.start(sums[...])

        @pl.when(g == 5)
        def _():
            sum2a.middle()
            sum2b.start(sums[...])

    def wide(rows, first, count):
        return jnp.concatenate([rows[first + g : first + g + 1, :] for g in range(count)], axis=1)

    mean2, inv2 = [None] * 2, [None] * 2

    def second_norm(got, lo, hi):
        count = (hi - lo) // LANE
        mean = wide(got, 0, count) * (1.0 / TOTAL)
        inv = lax.rsqrt(wide(got, count, count) * (1.0 / TOTAL) - mean * mean + EPSILON)
        scale = par[7, 0:1, lo:hi] * inv
        put(2, 0.5 * scale, lo, hi)
        put(3, 0.5 * (par[8, 0:1, lo:hi] - mean * scale), lo, hi)
        put(9, mean, lo, hi)
        put(10, inv, lo, hi)
        put(11, scale, lo, hi)

    put(7, gain2)
    put(8, bias2)

    def one_products(g):
        cols = lanes_of(g)

        @pl.loop(0, BLOCKS)
        def _(b):
            products(td, dv, a1, b * 48, cols)
            for cell in range(CELLS):
                cells[cell, :, cols] += fold(a1[pl.ds(b * 48 + 2 * cell, 2), :, cols])

    def one_activation(g):
        cols = lanes_of(g)

        @pl.loop(0, BLOCKS)
        def _(b):
            scale, shift = par[2, :, cols], par[3, :, cols]
            pooled = jnp.zeros((8, LANE), F32)
            for cell in range(CELLS):
                at = pl.ds(b * 48 + 2 * cell, 2)
                h, th = half_gate(dv[at, :, cols], scale, shift)
                q2[at, :, cols] = th
                act = h + h * th
                pooled = pooled + fold(act)
                hi, lo = split(act.reshape(16, LANE))
                rows = pl.ds(b * CHUNK + 16 * cell, 16)
                act_hi[rows, cols] = hi
                act_lo[rows, cols] = lo
            pool[b, :, cols] = pooled

    @pl.loop(0, 12)
    def _(step):
        @pl.when(step == 3)
        def _():
            sum2b.middle()

        @pl.when(step == 5)
        def _():
            second_norm(sum2a.finish(), 0, 3 * LANE)

        @pl.when(step == 9)
        def _():
            second_norm(sum2b.finish(), 3 * LANE, WIDE)

        early = (step < 5) | (step == 8)

        @pl.when(early)
        def _():
            one_products(jnp.where(step == 8, 5, step))

        @pl.when(jnp.logical_not(early))
        def _():
            one_activation(jnp.where(step < 8, step - 5, step - 6))

    section(2, 1)
    wp[0:D, :] = assembled(AT_PROJECT, D)
    wp[D:128, :] = jnp.zeros((128 - D, WIDE), F32)
    wr[...] = assembled(AT_REDUCE, 32)
    wx[...] = assembled(AT_EXCITE, 32)
    seg = lax.broadcasted_iota(jnp.int32, (8, LANE), 0)
    blk = lax.broadcasted_iota(jnp.int32, (8, LANE), 1)
    u0, u1, u2 = units[z, 0], units[z, 1], units[z, 2]
    lower = jnp.where(seg == 0, 0, jnp.where(seg == 1, u0, u0 + u1))
    length = jnp.where(seg == 0, u0, jnp.where(seg == 1, u1, u2))
    member = jnp.where((seg < 3) & (blk >= lower) & (blk < lower + length), 1.0, 0.0)
    per_count = jnp.where(seg < 3, 1.0 / (length * (BLOCK * CELLS)).astype(F32), 0.0)[:, 0:1]
    live = jnp.where(seg < 3, 1.0, 0.0)[:, 0:1]

    vec[...] = jnp.zeros((8, LANE), F32)
    vec[0:1, 0:SQZ] = br_in[...]
    pooled = jnp.zeros((8, WIDE), F32)
    for b in range(BLOCKS):
        pooled = pooled + member[:, b : b + 1] * row_sum(pool[b])
    pooled = pooled * per_count
    reduced = exact(pooled, wr[...], (1, 1)) + vec[0:1, 0:32]
    sig_r = sigmoid(reduced)
    squeezed = reduced * sig_r * live
    gate = sigmoid(exact(squeezed, wx[...], (1, 0)) + bx)

    def of_blocks(rows, b):
        return row_sum(member[:, b : b + 1] * rows)

    for b in range(BLOCKS):
        gates[b : b + 1, :] = of_blocks(gate, b)

    def project(b, carry):
        rows = pl.ds(pl.multiple_of(b * CHUNK, CHUNK), CHUNK)
        hi, lo = split(wp[...] * gates[pl.ds(b, 1), :])
        wp_b[b, 0:128, :] = hi
        wp_b[b, 128:256, :] = lo
        r = mm_nt(act_hi[rows, :], wp_b[b])
        r = r[:, 0:128] + r[:, 128:256] + mm_nt(act_lo[rows, :], wp_b[b, 0:128, :])
        r = r.reshape(48, 8, LANE)
        q = q_rows[pl.ds(b * 48, 48)]
        p_rows[pl.ds(b * 48, 48)] = r
        return tuple(old + jnp.sum(new, axis=0) for old, new in zip(carry, (r, r * r, q, q * r)))

    zero = jnp.zeros((8, LANE), F32)
    four = lax.fori_loop(0, BLOCKS * REPS.get("proj", 1), lambda i, v: project(lax.rem(i, BLOCKS), v), (zero,) * 4)
    for i in range(4):
        vec[i : i + 1, :] = row_sum(four[i])
    sum3.start(vec[...])

    @rloop("slopes", GROUPS)
    def _(g):
        cols = lanes_of(g)

        @pl.loop(0, BLOCKS)
        def _(b):
            scale, shift = par[0, :, cols], par[1, :, cols]
            scale2, shift2 = par[2, :, cols], par[3, :, cols]
            for cell in range(CELLS):
                at = pl.ds(b * 48 + 2 * cell, 2)
                h, th = half_gate(e_ref[at, :, cols], scale, shift)
                e_ref[at, :, cols] = slope_of(h, th)
                q2[at, :, cols] = slope_of(dv[at, :, cols] * scale2 + shift2, q2[at, :, cols])

        @pl.when(g == 4)
        def _():
            sum3.middle()

    got = sum3.finish() * (1.0 / TOTAL)
    vec[...] = jnp.zeros((8, LANE), F32)
    vec[0:1, 0:D] = ga3_in[...]
    vec[1:2, 0:D] = bi3_in[...]
    gain3, bias3 = vec[0:1, :], vec[1:2, :]
    mean3 = got[0:1]
    inv3 = lax.rsqrt(got[1:2] - mean3 * mean3 + EPSILON)
    b3 = got[2:3]
    g3 = (got[3:4] - mean3 * got[2:3]) * inv3
    o_panel[OUT_SMALL : OUT_SMALL + 1, 0:LANE] = g3 * TOTAL
    o_panel[OUT_SMALL + 1 : OUT_SMALL + 2, 0:LANE] = b3 * TOTAL
    s3 = gain3 * inv3
    t3 = bias3 - mean3 * s3
    pg_p = -s3 * inv3 * g3
    pg_0 = -s3 * b3 - pg_p * mean3

    @rloop("pgs", 18)
    def _(i):
        at = pl.ds(i * 16, 16)
        v = (q_rows[at] * s3 + (p_rows[at] * pg_p + pg_0)).reshape(128, LANE)
        rows = pl.ds(pl.multiple_of(i * 128, 128), 128)
        hi, lo = split(v)
        pg3[rows, 0:128] = hi
        pg3[rows, 128:256] = hi
        pg3[rows, 256:384] = lo
        hi, lo = split(v.T)
        pgt[0:128, rows] = hi
        pgt[128:256, rows] = lo

    @rep("mm")
    def _():
        gp_panel[...] = jnp.zeros_like(gp_panel)
        for b in range(BLOCKS):
            rows = slice(b * CHUNK, (b + 1) * CHUNK)
            for n in range(3):
                cols = slice(n * GROUP, (n + 1) * GROUP)
                m = mm(pgt[:, rows], act_hi[rows, cols])
                m = m[0:128] + m[128:256] + mm(pgt[0:128, rows], act_lo[rows, cols])
                gg[b : b + 1, cols] = row_sum(m * wp[:, cols])
                gp_panel[n] += (m * gates[b : b + 1, cols]).reshape(16, 8, GROUP)

    for n in range(3):
        reduce_p.start(n)

    gate_grad = jnp.zeros((8, WIDE), F32)
    for b in range(BLOCKS):
        gate_grad = gate_grad + member[:, b : b + 1] * gg[b : b + 1, :]
    excite_in = gate_grad * gate * (1.0 - gate)
    misc[...] = jnp.zeros_like(misc)

    def put_misc(row, values):
        for n in range(3):
            part = values[:, n * GROUP : (n + 1) * GROUP]
            misc[n, row // 8 : (row + values.shape[0]) // 8] = part.reshape(values.shape[0] // 8, 8, GROUP)

    put_misc(AT_X, exact(squeezed, excite_in, (0, 0)))
    reduced_grad = exact(excite_in, wx[...], (1, 1)) * (sig_r * (1.0 + reduced * (1.0 - sig_r))) * live
    put_misc(AT_R, exact(reduced_grad, pooled, (0, 0)))
    for n in range(3):
        misc[n, AT_B // 8, 0:1, :] = row_sum(excite_in)[:, n * GROUP : (n + 1) * GROUP]
    for k in range(4):
        half = (k % 2) * LANE
        misc[k // 2, AT_B // 8, 1:2, half : half + 32] = row_sum(reduced_grad)
    pooled_grad = exact(reduced_grad, wr[...], (1, 0)) * per_count
    for b in range(BLOCKS):
        spread[b : b + 1, :] = of_blocks(pooled_grad, b)

    @rloop("a2g", 3)
    def _(n):
        cols = pl.ds(pl.multiple_of(n * GROUP, GROUP), GROUP)

        def block(b, carry):
            rows = pl.ds(pl.multiple_of(b * CHUNK, CHUNK), CHUNK)
            at = pl.ds(b * 48, 48)
            r = mm(pg3[rows, 0:256], wp_b[b, :, cols]) + mm(pg3[rows, 256:384], wp_b[b, 0:128, cols])
            r = (r.reshape(48, 8, GROUP) + spread[pl.ds(b, 1), cols]) * q2[at, :, cols]
            q2[at, :, cols] = r
            return carry[0] + jnp.sum(r, axis=0), carry[1] + jnp.sum(r * dv[at, :, cols], axis=0)

        zero = jnp.zeros((8, GROUP), F32)
        total, product = lax.fori_loop(0, BLOCKS, block, (zero, zero))
        size = jnp.where(n == 0, 2, 4)
        low = jnp.where(n == 0, 0, 2)
        for half in range(2):
            put_sums(
                total[:, half * LANE : (half + 1) * LANE], product[:, half * LANE : (half + 1) * LANE],
                n * 2 + half, low, size,
            )

        @pl.when(n == 0)
        def _():
            sum4a.start(sums[...])

        @pl.when(n == 2)
        def _():
            sum4b.start(sums[...])

    @rloop("tq", GROUPS)
    def _(g):
        cols = lanes_of(g)

        @pl.loop(0, BLOCKS)
        def _(b):
            products(tq, q2, a1, b * 48, cols)

        @pl.when(g == 1)
        def _():
            sum4a.middle()

        @pl.when(g == 2)
        def _():
            sum4b.middle()

    def second_norm_grad(got, lo, hi):
        count = (hi - lo) // LANE
        mean, inv, scale = [par[i, 0:1, lo:hi] for i in (9, 10, 11)]
        bias = wide(got, 0, count)
        gain = (wide(got, count, count) - mean * bias) * inv
        c3 = -scale * inv * gain * (1.0 / TOTAL)
        put(4, scale, lo, hi)
        put(5, -scale * bias * (1.0 / TOTAL) - c3 * mean, lo, hi)
        put(6, c3, lo, hi)
        put(7, gain, lo, hi)
        put(8, bias, lo, hi)

    def own_lanes(rows):
        first = rows[:, 0:LANE]
        rest = rows[:, LANE:GROUP]
        return first, jnp.where(odd, pltpu.roll(rest, 64, 1), rest)

    def own_wide(rows):
        first = jnp.zeros((rows.shape[0], LANE), F32)
        rest = jnp.zeros((rows.shape[0], LANE), F32)
        for k in range(4):
            first = jnp.where(z == k, rows[:, k * LANE : (k + 1) * LANE], first)
        for k in range(2):
            rest = jnp.where(z // 2 == k, rows[:, (4 + k) * LANE : (5 + k) * LANE], rest)
        return jnp.concatenate([first, rest], axis=1)

    def emit(row, values):
        first, rest = own_lanes(values)
        o_panel[row : row + values.shape[0], 0:LANE] = first
        o_panel[row : row + values.shape[0], LANE:GROUP] = rest

    def emit_vector(i, row):
        emit(OUT_VECS + i, own_wide(row))

    @rloop("conv2", GROUPS)
    def _(g):
        @pl.when(g == 0)
        def _():
            second_norm_grad(sum4a.finish(), 0, GROUP)
            reduce_p.middle()

        @pl.when(g == 2)
        def _():
            second_norm_grad(sum4b.finish(), GROUP, WIDE)
            for t in range(TAPS):
                a, k = t // 5, t % 5
                plain = None
                for i in range(H):
                    for j in range(W):
                        ii, jj = i + a - 2, j + k - 2
                        if 0 <= ii < H and 0 <= jj < W:
                            v = cells[ii * W + jj]
                            plain = v if plain is None else plain + v
                row = row_sum(tq[t] * par[4] + td[t] * par[6] + plain * par[5])
                for n in range(3):
                    misc[n, t // 8, t % 8 : t % 8 + 1, :] = row[:, n * GROUP : (n + 1) * GROUP]
            for n in range(3):
                reduce_m.start(n)
            reduce_p.last()

        @pl.when(g == 5)
        def _():
            reduce_m.middle()

        cols = lanes_of(g)

        @pl.loop(0, BLOCKS)
        def _(b):
            base = b * 48
            k1, k2, k3 = par[4, :, cols], par[5, :, cols], par[6, :, cols]
            for cell in range(CELLS):
                at = pl.ds(base + 2 * cell, 2)
                q2[at, :, cols] = q2[at, :, cols] * k1 + (dv[at, :, cols] * k3 + k2)
            for ip in range(H):
                acc = [None] * W
                for a in range(5):
                    i = ip - a + 2
                    if not 0 <= i < H:
                        continue
                    w = [wd[a * 5 + k, :, cols] for k in range(5)]
                    for j in range(W):
                        v = q2[pl.ds(base + 2 * (i * W + j), 2), :, cols]
                        for jp in range(W):
                            k = jp - j + 2
                            if 0 <= k < 5:
                                term = v * w[k]
                                acc[jp] = term if acc[jp] is None else acc[jp] + term
                for jp in range(W):
                    at = pl.ds(base + 2 * (ip * W + jp), 2)
                    hi, lo = split((acc[jp] * e_ref[at, :, cols]).reshape(16, LANE))
                    rows = pl.ds(b * CHUNK + 16 * (ip * W + jp), 16)
                    act_hi[rows, cols] = hi
                    act_lo[rows, cols] = lo

        @pl.when(lax.rem(g, 2) == 1)
        def _():
            n = g // 2
            cols = pl.ds(pl.multiple_of(n * GROUP, GROUP), GROUP)
            m = mm(ft[...], act_hi[:, cols])
            m = m[0:128] + m[128:256] + mm(ft[0:128, :], act_lo[:, cols])
            ge_panel[n] = m.reshape(16, 8, GROUP)
            product = row_sum(m * we[:, cols])
            size = jnp.where(n < 2, 4, 2)
            low = jnp.where(n < 2, 0, 4)
            for half in range(2):
                sums[pl.ds(g - 1 + half - low, 1), :] = m[D : D + 1, half * LANE : (half + 1) * LANE]
                sums[pl.ds(g - 1 + half - low + size, 1), :] = product[:, half * LANE : (half + 1) * LANE]

            @pl.when(g == 3)
            def _():
                sum5a.start(sums[...])

            @pl.when(g == 5)
            def _():
                sum5a.middle()
                sum5b.start(sums[...])

            reduce_e.start(n)

    hi, lo = split(we[...] * s1)
    we_b[0:128, :] = hi
    we_b[128:256, :] = lo

    @rloop("ig", BLOCKS)
    def _(b):
        rows = pl.ds(pl.multiple_of(b * CHUNK, CHUNK), CHUNK)
        at = pl.ds(b * 48, 48)
        r = mm_nt(act_hi[rows, :], we_b[...])
        r = r[:, 0:128] + r[:, 128:256] + mm_nt(act_lo[rows, :], we_b[0:128, :])
        igrad[at] = q_rows[at] + r.reshape(48, 8, LANE)
        out[at] = f_rows[at] + (p_rows[at] * s3 + t3)

    sum5b.middle()
    reduce_m.last()
    emit(OUT_PROJECT, reduce_p.finish())
    reduce_e.middle()
    emit_vector(2, par[7, 0:1, :])
    emit_vector(3, par[8, 0:1, :])
    first = sum5a.finish()
    reduce_e.last()
    second = sum5b.finish()
    b1 = jnp.concatenate([wide(first, 0, 4), wide(second, 0, 2)], axis=1)
    g1 = (jnp.concatenate([wide(first, 4, 4), wide(second, 2, 2)], axis=1) - mean1 * b1) * inv1
    k3 = -s1 * inv1 * g1 * (1.0 / TOTAL)
    k2 = -s1 * b1 * (1.0 / TOTAL) - k3 * mean1
    mix = exact(we[...] * k3, we[...], (1, 1))
    const = exact(jnp.broadcast_to(k2, (8, WIDE)), we[...], (1, 1))[0:1, :]
    mix = jnp.where(lax.broadcasted_iota(jnp.int32, (128, LANE), 0) == D, const, mix)
    mix_hi, mix_lo = split(mix)
    mix_all = jnp.concatenate([mix_hi, mix_lo], axis=0)

    @rloop("ig2", BLOCKS)
    def _(b):
        rows = pl.ds(pl.multiple_of(b * CHUNK, CHUNK), CHUNK)
        r = mm(f3[rows, 0:256], mix_all) + mm(f3[rows, 256:384], mix_hi)
        igrad[pl.ds(b * 48, 48)] += r.reshape(48, 8, LANE)

    emit_vector(0, g1)
    emit_vector(1, b1)
    emit(OUT_MISC, reduce_m.finish())
    total_e = reduce_e.finish()
    emit(0, own_wide(s1) * (total_e - f_mean * own_wide(b1) - own_wide(cov_we[...]) * own_wide(inv1 * g1)))

    for s in range(3):
        section(s, 0)
    for item in vectors + [reduce_g, reduce_p, reduce_m, reduce_e]:
        item.close()


def finish_kernel(
    out_in, igrad_in, panel,
    out, igrad, expand, gain1, bias1, depth, gain2, bias2, reduce, b_reduce, excite, b_excite, project, gain3, bias3,
    stage,
):
    for source, target in ((out_in, out), (igrad_in, igrad)):
        for cell in range(CELLS):
            stage[pl.ds(cell, BLOCK, stride=CELLS), :] = source[2 * cell : 2 * cell + 2].reshape(16, LANE)
        for i in range(3):
            target[:, i * LANE : (i + 1) * LANE] = stage[i * LANE : (i + 1) * LANE, :].T[0:D]

    @pl.when(pl.program_id(0) == 0)
    def _():
        expand[...] = panel[0:LANE, :].T[0:OWN, 0:D]
        project[...] = panel[OUT_PROJECT : OUT_PROJECT + LANE, :].T[0:OWN, 0:D]
        for a in range(5):
            depth[a] = panel[OUT_MISC + 5 * a : OUT_MISC + 5 * a + 5, 0:OWN]
        reduce[...] = panel[OUT_MISC + AT_R : OUT_MISC + AT_R + SQZ, 0:OWN]
        excite[...] = panel[OUT_MISC + AT_X : OUT_MISC + AT_X + SQZ, 0:OWN]
        b_excite[...] = panel[OUT_MISC + AT_B : OUT_MISC + AT_B + 1, 0:OWN]
        b_reduce[...] = panel[OUT_MISC + AT_B + 1 : OUT_MISC + AT_B + 2, 0:SQZ]
        for i, ref in enumerate((gain1, bias1, gain2, bias2)):
            ref[...] = panel[OUT_VECS + i : OUT_VECS + i + 1, 0:OWN]
        gain3[...] = panel[OUT_SMALL : OUT_SMALL + 1, 0:D]
        bias3[...] = panel[OUT_SMALL + 1 : OUT_SMALL + 2, 0:D]


def body(
    features, seg_units, w_expand, gain_one, bias_one, w_depth, gain_two, bias_two,
    w_reduce, b_reduce, w_excite, b_excite, w_project, gain_three, bias_three, cotangent,
):
    vm = pl.BlockSpec(memory_space=pltpu.VMEM)
    big = pltpu.VMEM((288, 8, WIDE), F32)
    rows128 = pltpu.VMEM((288, 8, LANE), F32)
    half = pltpu.VMEM((ROWS, WIDE), BF16)

    def f32(*shape):
        return pltpu.VMEM(shape, F32)

    def b16(*shape):
        return pltpu.VMEM(shape, BF16)

    def shape(*dims):
        return jax.ShapeDtypeStruct(dims, F32)

    def row(vector):
        return vector.reshape(1, vector.shape[0])

    dma = pltpu.SemaphoreType.DMA
    slots = [f32(3, 16, 8, GROUP), f32(4, 8, GROUP), f32(8, 8, GROUP), f32(16, 8, GROUP)]
    out, igrad, panel = pl.pallas_call(
        kernel,
        out_shape=(shape(288, 8, LANE), shape(288, 8, LANE), shape(RESULTS, GROUP)),
        in_specs=[vm] * 15 + [pl.BlockSpec(memory_space=pltpu.SMEM)],
        out_specs=(vm,) * 3,
        scratch_shapes=[
            f32(CHUNK, LANE), f32(GROUP, LANE),
            rows128, rows128, rows128, b16(ROWS, 384), b16(256, ROWS), b16(ROWS, 384), b16(256, ROWS),
            big, big, big, big, half, half,
            f32(4, PANEL, GROUP), f32(128, WIDE), f32(128, WIDE), f32(32, WIDE), f32(32, WIDE),
            b16(256, WIDE), b16(BLOCKS, 256, WIDE), f32(TAPS, 8, WIDE), f32(12, 8, WIDE),
            f32(TAPS, 8, WIDE), f32(TAPS, 8, WIDE), f32(CELLS, 8, WIDE), f32(128, WIDE),
            f32(BLOCKS, 8, WIDE), f32(8, WIDE), f32(8, WIDE), f32(8, WIDE), f32(8, LANE), f32(8, LANE),
            f32(3, 16, 8, GROUP), f32(3, 16, 8, GROUP), f32(3, 16, 8, GROUP), f32(8, 16, LANE),
            f32(7, 8, 8, LANE), f32(7, 16, 8, LANE),
            f32(8, 16, LANE), f32(16, 16, LANE), f32(8, 16, LANE),
        ]
        + slots * 3
        + [dma((2, 3)), dma((7, 4)), dma((6,)), dma((3, 8))],
        compiler_params=pltpu.CompilerParams(
            collective_id=0, has_side_effects=True, vmem_limit_bytes=64 * 1024 * 1024 - 65536
        ),
    )(
        features.T, cotangent.T, w_expand.T, w_project, w_reduce.T, w_excite, w_depth,
        row(gain_one), row(bias_one), row(gain_two), row(bias_two), row(b_excite), row(b_reduce), row(gain_three), row(bias_three),
        seg_units,
    )

    def whole(*dims):
        return pl.BlockSpec(dims, lambda b: (0,) * len(dims))

    small = [
        (OWN, D), (1, OWN), (1, OWN), (5, 5, OWN), (1, OWN), (1, OWN),
        (SQZ, OWN), (1, SQZ), (SQZ, OWN), (1, OWN), (OWN, D), (1, D), (1, D),
    ]
    rows_in = pl.BlockSpec((48, 8, LANE), lambda b: (b, 0, 0))
    rows_out = pl.BlockSpec((D, CHUNK), lambda b: (0, b))
    results = pl.pallas_call(
        finish_kernel,
        grid=(BLOCKS,),
        out_shape=(shape(D, ROWS), shape(D, ROWS)) + tuple(shape(*dims) for dims in small),
        in_specs=[rows_in, rows_in, whole(RESULTS, GROUP)],
        out_specs=(rows_out, rows_out) + tuple(whole(*dims) for dims in small),
        scratch_shapes=[f32(CHUNK, LANE)],
    )(out, igrad, panel)
    (out, igrad, expand, gain1, bias1, depth, gain2, bias2, reduce, small_b, excite, b_x, project, gain3, bias3) = results
    return (
        out.T, igrad.T, expand.T, gain1[0], bias1[0], depth, gain2[0], bias2[0],
        reduce.T, small_b[0], excite, b_x[0], project, gain3[0], bias3[0],
    )


def solution(mesh):
    placed = (
        P(("dp", "chan"), None),
        P("dp", None),
        P(None, "chan"),
        P("chan"),
        P("chan"),
        P(None, None, "chan"),
        P("chan"),
        P("chan"),
        P("chan", None),
        P(),
        P(None, "chan"),
        P("chan"),
        P("chan", None),
        P(),
        P(),
        P(("dp", "chan"), None),
    )
    return jax.shard_map(
        body,
        mesh=mesh,
        in_specs=placed,
        out_specs=(
            P(("dp", "chan"), None),
            P(("dp", "chan"), None),
            P(None, "chan"),
            P("chan"),
            P("chan"),
            P(None, None, "chan"),
            P("chan"),
            P("chan"),
            P("chan", None),
            P(),
            P(None, "chan"),
            P("chan"),
            P("chan", None),
            P(),
            P(),
        ),
        check_vma=False,
    )
```

```python
import jax
import jax.numpy as jnp
from jax import lax
from jax.experimental import pallas as pl
from jax.experimental.pallas import tpu as pltpu
from jax.sharding import PartitionSpec as P

MESH = pl.DeviceIdType.MESH
F32 = jnp.float32
BF16 = jnp.bfloat16
EPSILON = 0.001
PRECISE = lax.Precision.HIGHEST
D = 112
SQZ = 28
EXP = 672
H, W, CELLS = 6, 4, 24
TAPS = 25
BLOCK, BLOCKS = 16, 6
ROWS = 2304
CHUNK = BLOCK * CELLS
LANE = 128
WIDE = 768
GROUPS = WIDE // LANE
TOTAL = 294912.0
OWN = 168
REST = OWN - LANE

AT_EXPAND, AT_DEPTH, AT_VECS, AT_PROJECT, AT_REDUCE, AT_EXCITE, PANEL = 0, 112, 137, 144, 256, 288, 320
AT_DD, AT_PLAIN, AT_R, AT_X = TAPS, 2 * TAPS, 3 * TAPS, 3 * TAPS + SQZ
IN_THIRD = 128 - AT_X
OUT_PROJECT, OUT_MISC, OUT_VECS, OUT_SMALL, RESULTS = 128, 256, 384, 392, 400
GROUP = 2 * LANE


REPS = {}


def rep(name):
    count = REPS.get(name, 1)

    def run(fn):
        if count == 1:
            fn()
        else:
            lax.fori_loop(0, count, lambda i, carry: (fn(), carry)[1], 0)

    return run


def rloop(name, size):
    count = REPS.get(name, 1)

    def run(fn):
        if count == 1:
            pl.loop(0, size)(fn)
        else:
            pl.loop(0, size * count)(lambda i: fn(lax.rem(i, size)))

    return run


def split(values):
    high = values.astype(BF16)
    return high, (values - high.astype(F32)).astype(BF16)


def mm(a, b):
    return lax.dot_general(a, b, (((1,), (0,)), ((), ())), preferred_element_type=F32)


def mm_nt(a, b):
    return lax.dot_general(a, b, (((1,), (1,)), ((), ())), preferred_element_type=F32)


def exact(a, b, dims):
    return lax.dot_general(a, b, ((dims[:1], dims[1:]), ((), ())), precision=PRECISE, preferred_element_type=F32)


def pair(values):
    return jnp.concatenate(split(values), axis=0)


def pair_nt(a, b, rows, cols):
    r = mm_nt(a, b)
    return (r[0:rows, 0:cols] + r[rows:, cols:]) + (r[0:rows, cols:] + r[rows:, 0:cols])


def place():
    dp = lax.axis_index("dp")
    z = lax.axis_index("chan")
    return dp // 8, lax.rem(dp // 2, 4), lax.rem(dp, 2), z


def ring(step):
    return min(step, 4 - step)


def column_peers():
    x, y, c, z = place()
    moves = [(dz, dc) for dz in range(4) for dc in range(2) if dz or dc]
    moves.sort(key=lambda m: -10 * ring(m[0]) - m[1])
    base = x * 8 + y * 2
    zs = [lax.rem(z + dz, 4) for dz in range(4)]
    cs = [c, 1 - c]
    return z * 2 + c, [(zs[dz] * 2 + cs[dc], (base + cs[dc], zs[dz])) for dz, dc in moves]


def plane_peers():
    x, y, c, z = place()
    moves = [(dx, dy) for dx in range(4) for dy in range(4) if dx or dy]
    moves.sort(key=lambda m: -ring(m[0]) - ring(m[1]))
    xs = [lax.rem(x + dx, 4) for dx in range(4)]
    ys = [lax.rem(y + dy, 4) for dy in range(4)]
    peers = []
    for dx, dy in moves:
        rank = xs[dx] * 4 + ys[dy]
        peers.append((rank, (rank * 2 + c, z)))
    return x * 4 + y, peers


def push(sources, slots, mine, peers, send, recv):
    for rank, device in peers:
        pltpu.make_async_remote_copy(
            src_ref=sources(rank),
            dst_ref=slots.at[mine],
            send_sem=send,
            recv_sem=recv,
            device_id=device,
            device_id_type=MESH,
        ).start()


def drain(view, sem):
    pltpu.make_async_copy(view, view, sem).wait()


def add_slots(slots, count):
    total = slots[0]
    for k in range(1, count):
        total = total + slots[k]
    return total


class Vector:
    def __init__(self, column, plane, near, far, sems):
        self.column, self.plane, self.near, self.far, self.sems = column, plane, near, far, sems

    def start(self, value):
        mine, peers = self.column
        self.near[mine] = value
        push(lambda rank: self.near.at[mine], self.near, mine, peers, self.sems.at[0], self.sems.at[1])

    def middle(self):
        drain(self.near.at[pl.ds(0, 7)], self.sems.at[1])
        mine, peers = self.plane
        self.far[mine] = add_slots(self.near, 8)
        push(lambda rank: self.far.at[mine], self.far, mine, peers, self.sems.at[2], self.sems.at[3])

    def finish(self):
        drain(self.far.at[pl.ds(0, 15)], self.sems.at[3])
        return add_slots(self.far, 16)

    def close(self):
        drain(self.near.at[pl.ds(0, 7)], self.sems.at[0])
        drain(self.far.at[pl.ds(0, 15)], self.sems.at[2])


class Square:
    def __init__(self, column, plane, source, first, second, third, sems):
        self.column, self.plane = column, plane
        self.source, self.first, self.second, self.third, self.sems = source, first, second, third, sems

    def start(self):
        mine, peers = self.column
        self.first[mine] = self.source[mine]
        push(lambda rank: self.source.at[rank], self.first, mine, peers, self.sems.at[0], self.sems.at[1])

    def middle(self):
        drain(self.first.at[pl.ds(0, 7)], self.sems.at[1])
        mine, peers = self.plane
        self.second[mine] = add_slots(self.first, 8)
        push(lambda rank: self.second.at[mine], self.second, mine, peers, self.sems.at[2], self.sems.at[3])

    def last(self):
        drain(self.second.at[pl.ds(0, 15)], self.sems.at[3])
        mine, peers = self.column
        self.third[mine] = add_slots(self.second, 16)
        push(lambda rank: self.third.at[mine], self.third, mine, peers, self.sems.at[4], self.sems.at[5])

    def finish(self):
        drain(self.third.at[pl.ds(0, 7)], self.sems.at[5])
        return self.third[...].reshape(128, LANE)

    def close(self):
        drain(self.first.at[pl.ds(0, 7)], self.sems.at[0])
        drain(self.second.at[pl.ds(0, 15)], self.sems.at[2])
        drain(self.third.at[pl.ds(0, 7)], self.sems.at[4])


class Panel:
    def __init__(self, column, plane, ranges, source, first, parts, second, third, sems):
        self.column, self.plane, self.ranges = column, plane, ranges
        self.source, self.first, self.parts, self.second, self.third, self.sems = source, first, parts, second, third, sems

    def start(self, index):
        mine, peers = self.plane
        lo, hi = self.ranges[index]
        lanes = pl.ds(lo, hi - lo)
        self.first[mine, :, lo:hi] = self.source[mine, :, lo:hi]
        for rank, device in peers:
            pltpu.make_async_remote_copy(
                src_ref=self.source.at[rank, :, lanes],
                dst_ref=self.first.at[mine, :, lanes],
                send_sem=self.sems.at[0],
                recv_sem=self.sems.at[1 + index],
                device_id=device,
                device_id_type=MESH,
            ).start()

    def scattered(self, index, sem):
        lo, hi = self.ranges[index]
        drain(self.first.at[pl.ds(0, 15), :, pl.ds(lo, hi - lo)], self.sems.at[sem])

    def middle(self):
        for index in range(len(self.ranges)):
            self.scattered(index, 1 + index)
        total = add_slots(self.first, 16)
        mine, peers = self.column
        for z in range(4):
            self.parts[z, :, 0:LANE] = total[:, z * LANE : (z + 1) * LANE]
            rest = 4 + z // 2
            self.parts[z, :, LANE:GROUP] = total[:, rest * LANE : (rest + 1) * LANE]
        self.second[mine] = self.parts[mine // 2]
        push(lambda rank: self.parts.at[rank // 2], self.second, mine, peers, self.sems.at[4], self.sems.at[5])

    def last(self):
        drain(self.second.at[pl.ds(0, 7)], self.sems.at[5])
        mine, peers = self.plane
        self.third[mine] = add_slots(self.second, 8)
        push(lambda rank: self.third.at[mine], self.third, mine, peers, self.sems.at[6], self.sems.at[7])

    def finish(self):
        drain(self.third.at[pl.ds(0, 15)], self.sems.at[7])
        return self.third[...].reshape(128, GROUP)

    def close(self):
        for index in range(len(self.ranges)):
            self.scattered(index, 0)
        drain(self.second.at[pl.ds(0, 7)], self.sems.at[4])
        drain(self.third.at[pl.ds(0, 15)], self.sems.at[6])


def half_gate(values, scale, shift):
    h = values * scale + shift
    return h, jnp.tanh(h)


def slope_of(h, th):
    return (0.5 + 0.5 * th) * (1.0 + (h - h * th))


def sigmoid(v):
    return 1.0 / (1.0 + jnp.exp(-v))


def lanes_of(g):
    return pl.ds(pl.multiple_of(g * LANE, LANE), LANE)


def fold(v):
    return v[0] + v[1]


def row_sum(v):
    return jnp.sum(v, axis=0, keepdims=True)


def row_pairs():
    return [(i, i + a - 2, a) for a in range(5) for i in range(H) if 0 <= i + a - 2 < H]


def nine_weights(w):
    m2, m1, w0, p1, p2 = w
    return [
        w0, p1 - w0, m1 - w0,
        p2 - w0, w0 - p1 - p2, (p1 - m1) + (w0 - p2),
        m2 - w0, (m1 - p1) + (w0 - m2), w0 - m1 - m2,
    ]


def five_taps(g):
    return [
        g[6] - g[7] - g[8],
        (g[2] - g[5]) + (g[7] - g[8]),
        (g[0] - g[1]) - (g[2] + g[3]) + (g[4] + g[5]) - (g[6] - g[7] - g[8]),
        (g[1] - g[4]) + (g[5] - g[7]),
        g[3] - g[4] - g[5],
    ]


def nine_inputs(x):
    x02, x13 = x[0] + x[2], x[1] + x[3]
    return [x02 + x13, x13, x02, x[2] + x[3], x[3], x[2], x[0] + x[1], x[1], x[0]]


def nine_outputs(y):
    y02, y13 = y[0] + y[2], y[1] + y[3]
    return [y02 + y13, y02, y13, y[0] + y[1], y[0], y[1], y[2] + y[3], y[2], y[3]]


def expand_rows(target, expand, cell):
    for i in range(H):
        for m, v in enumerate(expand([cell(i * W + j) for j in range(W)])):
            target[i * 9 + m] = v


def convolve(inputs, outputs, weights, cols):
    for m in range(9):
        x = [inputs[i * 9 + m] for i in range(H)]
        w = [jnp.broadcast_to(weights[a * 9 + m : a * 9 + m + 1, cols], (8, LANE)) for a in range(5)]
        acc = [None] * H
        for i, ii, a in row_pairs():
            term = x[ii] * w[a]
            acc[i] = term if acc[i] is None else acc[i] + term
        for i in range(H):
            outputs[i * 9 + m] = acc[i]


def four_cells(outputs, i):
    m = [outputs[i * 9 + k] for k in range(9)]
    a, b, c, d, e, f = m[0] + m[1], m[0] + m[2], m[3] + m[4], m[3] + m[5], m[6] + m[7], m[6] + m[8]
    return [a + c, b + d, a + e, b + f]


def correlate(target, left, right):
    for m in range(9):
        x = [right[i * 9 + m] for i in range(H)]
        y = [left[i * 9 + m] for i in range(H)]
        acc = [None] * 5
        for i, ii, a in row_pairs():
            term = y[i] * x[ii]
            acc[a] = term if acc[a] is None else acc[a] + term
        for a in range(5):
            target[a * 9 + m] += fold(acc[a])


def row_sums(target, source, cols):
    for t in range(45):
        target[t : t + 1, cols] = row_sum(source[t])


def kernel(
    f_hbm, q_hbm, we_in, wp_in, wr_in, wx_in, wd_in, ga1_in, bi1_in, ga2_in, bi2_in, bx_in, br_in, ga3_in, bi3_in, units,
    out, igrad, o_panel,
    f_in, q_in, copy_sems, stage, wide_stage,
    f_rows, q_rows, p_rows, f3, ft, pg3, qpt, qa,
    e_ref, a1, dv, q2, act_hi, act_lo,
    gathered, we, wp, wr, wx, we_b, ws_b, wp_b, wd, wt, par, tq, td, acc45, cells, cov_we, nine_a, nine_b,
    pool, gates, spread, vec, sums, gp_panel, misc, ge_panel, g_panel,
    near, far, near2, far2,
    g_first, g_second, g_third,
    p_first, p_parts, p_second, p_third,
    m_first, m_parts, m_second, m_third,
    e_first, e_parts, e_second, e_third,
    w_sems, v_sems, g_sems, s_sems,
):
    fetch_f = pltpu.make_async_copy(f_hbm, f_in, copy_sems.at[13])
    fetch_f.start()
    fetch_q = pltpu.make_async_copy(q_hbm, q_in, copy_sems.at[0])
    fetch_q.start()
    x, y, c, z = place()
    column, plane = column_peers(), plane_peers()
    barrier = pltpu.get_barrier_semaphore()
    for _, device in column[1] + plane[1]:
        pl.semaphore_signal(barrier, inc=1, device_id=device, device_id_type=MESH)

    sum2a = Vector(column, plane, near2.at[0], far2.at[0], v_sems.at[0])
    sum2b = Vector(column, plane, near2.at[1], far2.at[1], v_sems.at[1])
    sum3 = Vector(column, plane, near2.at[2], far2.at[2], v_sems.at[2])
    sum4 = Vector(column, plane, near.at[0], far.at[0], v_sems.at[3])
    sum5 = Vector(column, plane, near.at[1], far.at[1], v_sems.at[4])
    vectors = [sum2a, sum2b, sum3, sum4, sum5]
    reduce_g = Square(column, plane, g_panel, g_first, g_second, g_third, g_sems)
    whole = [(0, WIDE)]
    reduce_p = Panel(column, plane, whole, gp_panel, p_first, p_parts, p_second, p_third, s_sems.at[0])
    reduce_m = Panel(column, plane, whole, misc, m_first, m_parts, m_second, m_third, s_sems.at[1])
    early_late = [(0, 2 * GROUP), (2 * GROUP, WIDE)]
    reduce_e = Panel(column, plane, early_late, ge_panel, e_first, e_parts, e_second, e_third, s_sems.at[2])

    fetch_f.wait()

    ones = jnp.where(lax.broadcasted_iota(jnp.int32, (16, ROWS), 0) == 0, 1.0, 0.0)
    hi, lo = split(jnp.concatenate([f_in[...], ones], axis=0))
    ft[0:128, :] = hi
    ft[128:256, :] = lo
    gram = mm_nt(ft[...], ft[...])
    gram = gram[0:128, 0:128] + (gram[0:128, 128:256] + gram[128:256, 0:128]) + gram[128:256, 128:256]
    g_panel[...] = gram.reshape(8, 16, LANE)
    pl.semaphore_wait(barrier, 22)
    reduce_g.start()

    sections = ((0, AT_DEPTH), (AT_DEPTH, AT_PROJECT), (AT_PROJECT, PANEL))
    odd = lax.rem(z, 2) == 1

    across = [(lax.rem(z + k, 4), {"chan": lax.rem(z + k, 4)}) for k in (2, 1, 3)]

    def halves(s):
        lo, hi = sections[s]
        size = (hi - lo) // 2
        return size, pl.ds(pl.multiple_of(lo + c * size, 8), size), pl.ds(lo, size)

    def send_section(s):
        lo, hi = sections[s]
        rest = gathered[z, lo:hi, LANE:GROUP]
        gathered[z, lo:hi, LANE:GROUP] = jnp.where(odd, pltpu.roll(rest, 64, 1), rest)
        size, rows, _ = halves(s)
        for _, device in across:
            pltpu.make_async_remote_copy(
                src_ref=gathered.at[z, rows],
                dst_ref=gathered.at[z, rows],
                send_sem=w_sems.at[0, s],
                recv_sem=w_sems.at[1, s],
                device_id=device,
                device_id_type=MESH,
            ).start()

    def forward_section(s):
        size, rows, some = halves(s)
        drain(gathered.at[pl.ds(0, 3), some], w_sems.at[1, s])
        for other, _ in across:
            pltpu.make_async_remote_copy(
                src_ref=gathered.at[other, rows],
                dst_ref=gathered.at[other, rows],
                send_sem=w_sems.at[0, s],
                recv_sem=w_sems.at[2, s],
                device_id=(x * 8 + y * 2 + 1 - c, z),
                device_id_type=MESH,
            ).start()

    def section(s):
        size, rows, some = halves(s)
        drain(gathered.at[pl.ds(0, 3), some], w_sems.at[2, s])

    def close_section(s):
        size, rows, some = halves(s)
        for _ in range(2):
            drain(gathered.at[pl.ds(0, 3), some], w_sems.at[0, s])

    def assembled(lo, rows):
        parts = [gathered[k, lo : lo + rows, 0:LANE] for k in range(4)]
        for k in (0, 2):
            parts.append(gathered[k, lo : lo + rows, LANE:GROUP] + gathered[k + 1, lo : lo + rows, LANE:GROUP])
        return jnp.concatenate(parts, axis=1)

    gathered[z] = jnp.zeros((PANEL, GROUP), F32)
    wide_stage[...] = jnp.zeros_like(wide_stage)
    wide_stage[0:OWN, 0:D] = we_in[...]
    gathered[z, 0:D, :] = wide_stage[...].T[0:D]
    send_section(0)
    for a in range(5):
        gathered[z, AT_DEPTH + 5 * a : AT_DEPTH + 5 * a + 5, 0:OWN] = wd_in[a]
    for i, row in enumerate((ga1_in, bi1_in, ga2_in, bi2_in, bx_in)):
        gathered[z, AT_VECS + i : AT_VECS + i + 1, 0:OWN] = row[...]
    send_section(1)

    tail = jnp.where(lax.broadcasted_iota(jnp.int32, (16, LANE), 0) == 0, 1.0, 0.0)

    def rows_of(source, tail, target):
        @pl.loop(0, BLOCKS)
        def _(b):
            for i in range(3):
                v = source[:, pl.ds(pl.multiple_of(b * CHUNK + i * LANE, LANE), LANE)]
                stage[i * LANE : (i + 1) * LANE, :] = jnp.concatenate([v, tail], axis=0).T
            for cell in range(CELLS):
                v = stage[pl.ds(cell, BLOCK, stride=CELLS), :]
                target[pl.ds((b * CELLS + cell) * 2, 2)] = v.reshape(2, 8, LANE)

    rows_of(f_in, tail, f_rows)

    @rloop("ft", 18)
    def _(i):
        v = f_rows[pl.ds(i * 16, 16)].reshape(128, LANE)
        rows = pl.ds(pl.multiple_of(i * 128, 128), 128)
        hi, lo = split(v)
        f3[rows, 0:128] = hi
        f3[rows, 128:256] = hi
        f3[rows, 256:384] = lo
        hi, lo = split(v.T)
        ft[0:128, rows] = hi
        ft[128:256, rows] = lo

    def parts_of(source, row):
        @pl.loop(0, 18)
        def _(i):
            hi, lo = split(source[pl.ds(i * 16, 16)].reshape(128, LANE).T)
            rows = pl.ds(pl.multiple_of(i * 128, 128), 128)
            qpt[row : row + 128, rows] = hi
            qpt[256 + row : 384 + row, rows] = lo

    reduce_g.middle()
    fetch_q.wait()
    rows_of(q_in, jnp.zeros((16, LANE), F32), q_rows)
    parts_of(q_rows, 0)
    sums[...] = jnp.zeros_like(sums)
    cells[...] = jnp.zeros_like(cells)
    qa[...] = jnp.zeros_like(qa)

    forward_section(0)
    forward_section(1)
    section(0)
    we[0:D, :] = assembled(0, D)
    we[D:128, :] = jnp.zeros((128 - D, WIDE), F32)
    hi, lo = split(we[...])
    we_b[0:128, :] = hi
    we_b[128:256, :] = lo

    @rloop("E", BLOCKS)
    def _(b):
        @pl.when(b == 3)
        def _():
            reduce_g.last()

        rows = pl.ds(pl.multiple_of(b * CHUNK, CHUNK), CHUNK)
        for n in range(3):
            cols = slice(n * GROUP, (n + 1) * GROUP)
            r = mm(f3[rows, 0:256], we_b[:, cols]) + mm(f3[rows, 256:384], we_b[0:128, cols])
            e_ref[pl.ds(b * 48, 48), :, cols] = r.reshape(48, 8, GROUP)

    section(1)
    taps = assembled(AT_DEPTH, 32)
    for a in range(5):
        row = [taps[5 * a + k : 5 * a + k + 1] for k in range(5)]
        for m, v in enumerate(nine_weights(row)):
            wd[a * 9 + m : a * 9 + m + 1, :] = v
        for m, v in enumerate(nine_weights(row[::-1])):
            wt[(4 - a) * 9 + m : (4 - a) * 9 + m + 1, :] = v
    gain1, bias1, gain2, bias2, bx = [taps[TAPS + i : TAPS + i + 1] for i in range(5)]
    wide_stage[0:OWN, 0:D] = wp_in[...]
    gathered[z, AT_PROJECT : AT_PROJECT + D, :] = wide_stage[...].T[0:D]
    gathered[z, AT_REDUCE : AT_REDUCE + SQZ, 0:OWN] = wr_in[...]
    gathered[z, AT_EXCITE : AT_EXCITE + SQZ, 0:OWN] = wx_in[...]

    gram = reduce_g.finish() * (1.0 / TOTAL)
    send_section(2)
    f_mean_row = gram[D : D + 1, :]
    f_mean = gram[:, D : D + 1]
    cov = gram - f_mean * f_mean_row
    hi, lo = split(cov)
    cov_we[...] = mm(jnp.concatenate([hi, hi], axis=1), we_b[...]) + mm(jnp.concatenate([lo, lo], axis=1), we_b[...])
    mean1 = row_sum(we[...] * f_mean)
    inv1 = lax.rsqrt(row_sum(we[...] * cov_we[...]) + EPSILON)
    s1 = gain1 * inv1
    t1 = bias1 - mean1 * s1

    def put(i, row, lo=0, hi=WIDE):
        par[i, :, lo:hi] = jnp.broadcast_to(row, (8, hi - lo))

    put(0, 0.5 * s1)
    put(1, 0.5 * t1)

    def put_sums(first, second, g, low, size):
        sums[pl.ds(g - low, 1), :] = row_sum(first)
        sums[pl.ds(g - low + size, 1), :] = row_sum(second)

    @rloop("conv1", GROUPS)
    def _(g):
        cols = lanes_of(g)

        def block(b, carry):
            total, square = carry
            base = b * 48
            scale, shift = par[0, :, cols], par[1, :, cols]

            def activate(cell):
                at = pl.ds(base + 2 * cell, 2)
                h, th = half_gate(e_ref[at, :, cols], scale, shift)
                act = h + h * th
                a1[at, :, cols] = act
                return act

            expand_rows(nine_a, nine_inputs, activate)
            convolve(nine_a, nine_b, wd, cols)
            for i in range(H):
                for j, v in enumerate(four_cells(nine_b, i)):
                    dv[pl.ds(base + 2 * (i * W + j), 2), :, cols] = v
                    total = total + fold(v)
                    square = square + fold(v * v)
            return total, square

        zero = jnp.zeros((8, LANE), F32)
        total, square = lax.fori_loop(0, BLOCKS, block, (zero, zero))
        put_sums(total, square, g, jnp.where(g < 3, 0, 3), 3)

        @pl.when(g == 2)
        def _():
            sum2a.start(sums[0:8, :])

        @pl.when(g == 4)
        def _():
            forward_section(2)

        @pl.when(g == 5)
        def _():
            sum2a.middle()
            sum2b.start(sums[0:8, :])

    def wide(rows, first, count):
        return jnp.concatenate([rows[first + g : first + g + 1, :] for g in range(count)], axis=1)

    mean2, inv2 = [None] * 2, [None] * 2

    def second_norm(got, lo, hi):
        count = (hi - lo) // LANE
        mean = wide(got, 0, count) * (1.0 / TOTAL)
        inv = lax.rsqrt(wide(got, count, count) * (1.0 / TOTAL) - mean * mean + EPSILON)
        scale = par[7, 0:1, lo:hi] * inv
        put(2, 0.5 * scale, lo, hi)
        put(3, 0.5 * (par[8, 0:1, lo:hi] - mean * scale), lo, hi)
        put(9, mean, lo, hi)
        put(10, inv, lo, hi)
        put(11, scale, lo, hi)

    put(7, gain2)
    put(8, bias2)

    def one_products(g):
        cols = lanes_of(g)
        acc45[...] = jnp.zeros_like(acc45)

        @pl.loop(0, BLOCKS)
        def _(b):
            def act(cell):
                v = a1[pl.ds(b * 48 + 2 * cell, 2), :, cols]
                cells[cell, :, cols] += fold(v)
                return v

            expand_rows(nine_a, nine_inputs, act)
            expand_rows(nine_b, nine_outputs, lambda cell: dv[pl.ds(b * 48 + 2 * cell, 2), :, cols])
            correlate(acc45, nine_b, nine_a)

        row_sums(td, acc45, cols)

    def one_activation(g):
        cols = lanes_of(g)

        @pl.loop(0, BLOCKS)
        def _(b):
            scale, shift = par[2, :, cols], par[3, :, cols]
            pooled = jnp.zeros((8, LANE), F32)
            for cell in range(CELLS):
                at = pl.ds(b * 48 + 2 * cell, 2)
                h, th = half_gate(dv[at, :, cols], scale, shift)
                q2[at, :, cols] = th
                act = h + h * th
                pooled = pooled + fold(act)
                hi, lo = split(act.reshape(16, LANE))
                rows = pl.ds(b * CHUNK + 16 * cell, 16)
                act_hi[rows, cols] = hi
                act_lo[rows, cols] = lo
            pool[b, :, cols] = pooled

    @pl.loop(0, 12)
    def _(step):
        @pl.when(step == 3)
        def _():
            sum2b.middle()

        @pl.when(step == 5)
        def _():
            second_norm(sum2a.finish(), 0, 3 * LANE)

        @pl.when(step == 9)
        def _():
            second_norm(sum2b.finish(), 3 * LANE, WIDE)

        early = (step < 5) | (step == 8)

        @pl.when(early)
        def _():
            one_products(jnp.where(step == 8, 5, step))

        @pl.when(jnp.logical_not(early))
        def _():
            one_activation(jnp.where(step < 8, step - 5, step - 6))

    section(2)
    wp[0:D, :] = assembled(AT_PROJECT, D)
    wp[D:128, :] = jnp.zeros((128 - D, WIDE), F32)
    hi, lo = split(assembled(AT_REDUCE, 32))
    wr[...] = jnp.concatenate([hi, lo, hi, lo], axis=0)
    hi, lo = split(assembled(AT_EXCITE, 32))
    wx[...] = jnp.concatenate([hi, lo, hi, lo], axis=0)
    seg = lax.broadcasted_iota(jnp.int32, (8, LANE), 0)
    blk = lax.broadcasted_iota(jnp.int32, (8, LANE), 1)
    u0, u1, u2 = units[z, 0], units[z, 1], units[z, 2]
    lower = jnp.where(seg == 0, 0, jnp.where(seg == 1, u0, u0 + u1))
    length = jnp.where(seg == 0, u0, jnp.where(seg == 1, u1, u2))
    member = jnp.where((seg < 3) & (blk >= lower) & (blk < lower + length), 1.0, 0.0)
    per_count = jnp.where(seg < 3, 1.0 / (length * (BLOCK * CELLS)).astype(F32), 0.0)[:, 0:1]
    live = jnp.where(seg < 3, 1.0, 0.0)[:, 0:1]

    vec[...] = jnp.zeros((8, LANE), F32)
    vec[0:1, 0:SQZ] = br_in[...]
    pooled = jnp.zeros((8, WIDE), F32)
    for b in range(BLOCKS):
        pooled = pooled + member[:, b : b + 1] * row_sum(pool[b])
    plain_sums = pooled
    pooled = pooled * per_count
    pooled_pair = pair(pooled)
    reduced = pair_nt(pooled_pair, wr[0:64, :], 8, 32) + vec[0:1, 0:32]
    sig_r = sigmoid(reduced)
    squeezed = reduced * sig_r * live

    def quad(values):
        hi, lo = split(values)
        return jnp.concatenate([hi, hi, lo, lo], axis=1)

    gate = sigmoid(mm(quad(squeezed), wx[...]) + bx)

    def of_blocks(rows, b):
        return row_sum(member[:, b : b + 1] * rows)

    for b in range(BLOCKS):
        gates[b : b + 1, :] = of_blocks(gate, b)

    def project(b, carry):
        rows = pl.ds(pl.multiple_of(b * CHUNK, CHUNK), CHUNK)
        hi, lo = split(wp[...] * gates[pl.ds(b, 1), :])
        wp_b[b, 0:128, :] = hi
        wp_b[b, 128:256, :] = lo
        r = mm_nt(act_hi[rows, :], wp_b[b])
        r = r[:, 0:128] + r[:, 128:256] + mm_nt(act_lo[rows, :], wp_b[b, 0:128, :])
        r = r.reshape(48, 8, LANE)
        q = q_rows[pl.ds(b * 48, 48)]
        p_rows[pl.ds(b * 48, 48)] = r
        return tuple(old + jnp.sum(new, axis=0) for old, new in zip(carry, (r, r * r, q, q * r)))

    zero = jnp.zeros((8, LANE), F32)
    four = lax.fori_loop(0, BLOCKS * REPS.get("proj", 1), lambda i, v: project(lax.rem(i, BLOCKS), v), (zero,) * 4)
    for i in range(4):
        vec[i : i + 1, :] = row_sum(four[i])
    sum3.start(vec[...])

    parts_of(p_rows, 128)

    @rloop("qa", BLOCKS)
    def _(b):
        rows = pl.ds(pl.multiple_of(b * CHUNK, CHUNK), CHUNK)
        inside = [jnp.where((b >= low) & (b < high), 1.0, 0.0) for low, high in ((0, u0), (u0, u0 + u1), (u0 + u1, 6))]
        for n in range(3):
            cols = slice(n * GROUP, (n + 1) * GROUP)
            m = mm(qpt[:, rows], act_hi[rows, cols])
            m = m[0:256] + m[256:512] + mm(qpt[0:256, rows], act_lo[rows, cols])
            for k in range(3):
                qa[k, :, cols] += m * inside[k]

        @pl.when(b == 3)
        def _():
            sum3.middle()

    @rloop("slope2", GROUPS)
    def _(g):
        cols = lanes_of(g)

        @pl.loop(0, BLOCKS)
        def _(b):
            scale, shift = par[2, :, cols], par[3, :, cols]
            for cell in range(CELLS):
                at = pl.ds(b * 48 + 2 * cell, 2)
                q2[at, :, cols] = slope_of(dv[at, :, cols] * scale + shift, q2[at, :, cols])

    got = sum3.finish() * (1.0 / TOTAL)
    vec[...] = jnp.zeros((8, LANE), F32)
    vec[0:1, 0:D] = ga3_in[...]
    vec[1:2, 0:D] = bi3_in[...]
    gain3, bias3 = vec[0:1, :], vec[1:2, :]
    mean3 = got[0:1]
    inv3 = lax.rsqrt(got[1:2] - mean3 * mean3 + EPSILON)
    b3 = got[2:3]
    g3 = (got[3:4] - mean3 * got[2:3]) * inv3
    o_panel[OUT_SMALL : OUT_SMALL + 1, 0:LANE] = g3 * TOTAL
    o_panel[OUT_SMALL + 1 : OUT_SMALL + 2, 0:LANE] = b3 * TOTAL
    s3 = gain3 * inv3
    t3 = bias3 - mean3 * s3
    pg_p = -s3 * inv3 * g3
    pg_0 = -s3 * b3 - pg_p * mean3

    columns = jnp.concatenate([s3, pg_p, pg_0, jnp.zeros((5, LANE), F32)], axis=0).T
    by_q, by_p, by_1 = columns[:, 0:1], columns[:, 1:2], columns[:, 2:3]
    base = row_sum(wp[...] * by_1)
    w_q, w_p = wp[...] * by_q, wp[...] * by_p
    gate_grad = jnp.concatenate(
        [row_sum(w_q * qa[k, 0:128] + w_p * qa[k, 128:256]) + base * plain_sums[k : k + 1] for k in range(3)]
        + [jnp.zeros((5, WIDE), F32)],
        axis=0,
    )
    excite_in = gate_grad * gate * (1.0 - gate)
    reduced_grad = pair_nt(pair(excite_in), wx[0:64, :], 8, 32) * (sig_r * (1.0 + reduced * (1.0 - sig_r))) * live
    pooled_grad = mm(quad(reduced_grad), wr[...]) * per_count
    for b in range(BLOCKS):
        spread[b : b + 1, :] = of_blocks(pooled_grad, b)

    @rloop("pgs", BLOCKS)
    def _(b):
        at = pl.ds(b * 48, 48)
        hi, lo = split((q_rows[at] * s3 + (p_rows[at] * pg_p + pg_0)).reshape(CHUNK, LANE))
        rows = pl.ds(pl.multiple_of(b * CHUNK, CHUNK), CHUNK)
        pg3[rows, 0:128] = hi
        pg3[rows, 128:256] = hi
        pg3[rows, 256:384] = lo

    @rloop("a2g", 3)
    def _(n):
        cols = pl.ds(pl.multiple_of(n * GROUP, GROUP), GROUP)

        def block(b, carry):
            rows = pl.ds(pl.multiple_of(b * CHUNK, CHUNK), CHUNK)
            at = pl.ds(b * 48, 48)
            r = mm(pg3[rows, 0:256], wp_b[b, :, cols]) + mm(pg3[rows, 256:384], wp_b[b, 0:128, cols])
            r = (r.reshape(48, 8, GROUP) + spread[pl.ds(b, 1), cols]) * q2[at, :, cols]
            q2[at, :, cols] = r
            return carry[0] + jnp.sum(r, axis=0), carry[1] + jnp.sum(r * dv[at, :, cols], axis=0)

        zero = jnp.zeros((8, GROUP), F32)
        total, product = lax.fori_loop(0, BLOCKS, block, (zero, zero))
        for half in range(2):
            lanes = slice(half * LANE, (half + 1) * LANE)
            put_sums(total[:, lanes], product[:, lanes], n * 2 + half, 0, 8)

    sum4.start(sums[...])

    gp = jnp.zeros((128, WIDE), F32)
    for k in range(3):
        gp = gp + gate[k : k + 1] * (by_q * qa[k, 0:128] + by_p * qa[k, 128:256] + by_1 * plain_sums[k : k + 1])
    gp_panel[...] = gp.reshape(16, 8, WIDE)
    g_excite = exact(squeezed, excite_in, (0, 0))
    gp_panel[14, 0:1, :] = row_sum(excite_in)
    gp_panel[15, 0:1, :] = jnp.zeros((1, WIDE), F32)
    for k in range(4):
        gp_panel[15, 0:1, k * LANE : k * LANE + 32] = row_sum(reduced_grad)
    for i in range(IN_THIRD, SQZ):
        gp_panel[14, 1 + i - IN_THIRD : 2 + i - IN_THIRD, :] = g_excite[i : i + 1]
    reduce_p.start(0)

    def put_misc(row, values):
        for i in range(values.shape[0]):
            misc[(row + i) // 8, (row + i) % 8 : (row + i) % 8 + 1, :] = values[i : i + 1]

    put_misc(AT_R, exact(reduced_grad, pooled, (0, 0))[0:SQZ])
    put_misc(AT_X, g_excite[0:IN_THIRD])

    @rloop("tq", GROUPS)
    def _(g):
        cols = lanes_of(g)
        acc45[...] = jnp.zeros_like(acc45)

        @pl.loop(0, BLOCKS)
        def _(b):
            expand_rows(nine_a, nine_inputs, lambda cell: a1[pl.ds(b * 48 + 2 * cell, 2), :, cols])
            expand_rows(nine_b, nine_outputs, lambda cell: q2[pl.ds(b * 48 + 2 * cell, 2), :, cols])
            correlate(acc45, nine_b, nine_a)
            scale, shift = par[0, :, cols], par[1, :, cols]
            for cell in range(CELLS):
                at = pl.ds(b * 48 + 2 * cell, 2)
                e_ref[at, :, cols] = slope_of(*half_gate(e_ref[at, :, cols], scale, shift))

        row_sums(tq, acc45, cols)

        @pl.when(g == 2)
        def _():
            sum4.middle()

        @pl.when(g == 4)
        def _():
            reduce_p.middle()

    def own_lanes(rows):
        first = rows[:, 0:LANE]
        rest = rows[:, LANE:GROUP]
        return first, jnp.where(odd, pltpu.roll(rest, 64, 1), rest)

    def own_wide(rows):
        first = jnp.zeros((rows.shape[0], LANE), F32)
        rest = jnp.zeros((rows.shape[0], LANE), F32)
        for k in range(4):
            first = jnp.where(z == k, rows[:, k * LANE : (k + 1) * LANE], first)
        for k in range(2):
            rest = jnp.where(z // 2 == k, rows[:, (4 + k) * LANE : (5 + k) * LANE], rest)
        return jnp.concatenate([first, rest], axis=1)

    def emit(row, values):
        first, rest = own_lanes(values)
        o_panel[row : row + values.shape[0], 0:LANE] = first
        o_panel[row : row + values.shape[0], LANE:GROUP] = rest

    def emit_vector(i, row):
        emit(OUT_VECS + i, own_wide(row))

    for t in range(TAPS):
        a, k = t // 5, t % 5
        plain = None
        for i in range(H):
            for j in range(W):
                ii, jj = i + a - 2, j + k - 2
                if 0 <= ii < H and 0 <= jj < W:
                    v = cells[ii * W + jj]
                    plain = v if plain is None else plain + v
        put_misc(AT_PLAIN + t, row_sum(plain))
    for first, source in ((0, tq), (AT_DD, td)):
        for a in range(5):
            for k, v in enumerate(five_taps([source[a * 9 + m : a * 9 + m + 1, :] for m in range(9)])):
                put_misc(first + 5 * a + k, v)
    reduce_m.start(0)

    got = sum4.finish()
    mean2, inv2, s2 = [par[i, 0:1, :] for i in (9, 10, 11)]
    b2 = wide(got, 0, GROUPS)
    g2 = (wide(got, 8, GROUPS) - mean2 * b2) * inv2
    c3 = -s2 * inv2 * g2 * (1.0 / TOTAL)
    c2 = -s2 * b2 * (1.0 / TOTAL) - c3 * mean2
    put(4, s2)
    put(5, c2)
    put(6, c3)
    emit_vector(2, g2)
    emit_vector(3, b2)

    @rloop("conv2", GROUPS)
    def _(g):
        @pl.when(g == 1)
        def _():
            reduce_p.last()

        @pl.when(g == 4)
        def _():
            reduce_m.middle()

        cols = lanes_of(g)

        @pl.loop(0, BLOCKS)
        def _(b):
            base = b * 48
            k1, k2, k3 = par[4, :, cols], par[5, :, cols], par[6, :, cols]

            def grad(cell):
                at = pl.ds(base + 2 * cell, 2)
                return q2[at, :, cols] * k1 + (dv[at, :, cols] * k3 + k2)

            expand_rows(nine_a, nine_inputs, grad)
            convolve(nine_a, nine_b, wt, cols)
            for i in range(H):
                for j, v in enumerate(four_cells(nine_b, i)):
                    at = pl.ds(base + 2 * (i * W + j), 2)
                    hi, lo = split((v * e_ref[at, :, cols]).reshape(16, LANE))
                    rows = pl.ds(b * CHUNK + 16 * (i * W + j), 16)
                    act_hi[rows, cols] = hi
                    act_lo[rows, cols] = lo

        @pl.when(lax.rem(g, 2) == 1)
        def _():
            n = g // 2
            cols = pl.ds(pl.multiple_of(n * GROUP, GROUP), GROUP)
            m = mm(ft[...], act_hi[:, cols])
            m = m[0:128] + m[128:256] + mm(ft[0:128, :], act_lo[:, cols])
            ge_panel[:, :, cols] = m.reshape(16, 8, GROUP)
            product = row_sum(m * we[:, cols])
            for half in range(2):
                lanes = slice(half * LANE, (half + 1) * LANE)
                sums[pl.ds(g - 1 + half, 1), :] = m[D : D + 1, lanes]
                sums[pl.ds(g + 7 + half, 1), :] = product[:, lanes]

            @pl.when(g == 3)
            def _():
                reduce_e.start(0)

    reduce_e.start(1)
    sum5.start(sums[...])

    hi, lo = split(we[...] * s1)
    ws_b[0:128, :] = hi
    ws_b[128:256, :] = lo

    @rloop("ig", BLOCKS)
    def _(b):
        rows = pl.ds(pl.multiple_of(b * CHUNK, CHUNK), CHUNK)
        at = pl.ds(b * 48, 48)
        r = mm_nt(act_hi[rows, :], ws_b[...])
        r = r[:, 0:128] + r[:, 128:256] + mm_nt(act_lo[rows, :], ws_b[0:128, :])
        q_rows[at] += r.reshape(48, 8, LANE)

    sum5.middle()

    def write(target, b, rows_of_cell):
        for cell in range(CELLS):
            stage[pl.ds(cell, BLOCK, stride=CELLS), :] = rows_of_cell(pl.ds(b * 48 + 2 * cell, 2)).reshape(16, LANE)
        for i in range(3):
            at = pl.ds(pl.multiple_of(b * CHUNK + i * LANE, LANE), LANE)
            target[:, at] = stage[i * LANE : (i + 1) * LANE, :].T[0:D]

    def store(source, target, sem, b):
        at = pl.ds(pl.multiple_of(b * CHUNK, CHUNK), CHUNK)
        return pltpu.make_async_copy(source.at[:, at], target.at[:, at], sem)

    @rloop("out", BLOCKS)
    def _(b):
        write(f_in, b, lambda at: f_rows[at] + (p_rows[at] * s3 + t3))
        store(f_in, out, copy_sems.at[1 + b], b).start()

    reduce_e.middle()
    reduce_m.last()
    emit(OUT_PROJECT, reduce_p.finish())
    got = sum5.finish()
    b1 = wide(got, 0, GROUPS)
    g1 = (wide(got, 8, GROUPS) - mean1 * b1) * inv1
    k3 = -s1 * inv1 * g1 * (1.0 / TOTAL)
    k2 = -s1 * b1 * (1.0 / TOTAL) - k3 * mean1
    reduce_e.last()
    left = jnp.where(lax.broadcasted_iota(jnp.int32, (128, WIDE), 0) == D, k2, we[...] * k3)
    mix = pair_nt(pair(left), we_b[...], 128, 128)
    mix_hi, mix_lo = split(mix)
    mix_all = jnp.concatenate([mix_hi, mix_lo], axis=0)

    @rloop("ig2", BLOCKS)
    def _(b):
        rows = pl.ds(pl.multiple_of(b * CHUNK, CHUNK), CHUNK)
        r = mm(f3[rows, 0:256], mix_all) + mm(f3[rows, 256:384], mix_hi)
        q_rows[pl.ds(b * 48, 48)] += r.reshape(48, 8, LANE)
        write(q_in, b, lambda at: q_rows[at])
        store(q_in, igrad, copy_sems.at[7 + b], b).start()

    emit_vector(0, g1)
    emit_vector(1, b1)
    total_m = reduce_m.finish()
    emit(OUT_MISC, total_m)
    by = [own_wide(v) for v in (s2, c2, c3)]
    taps_grad = total_m[0:TAPS] * by[0] + total_m[AT_DD : AT_DD + TAPS] * by[2] + total_m[AT_PLAIN : AT_PLAIN + TAPS] * by[1]
    emit(OUT_MISC, taps_grad)
    total_e = reduce_e.finish()
    emit(0, own_wide(s1) * (total_e - f_mean * own_wide(b1) - own_wide(cov_we[...]) * own_wide(inv1 * g1)))

    for b in range(BLOCKS):
        store(f_in, out, copy_sems.at[1 + b], b).wait()
        store(q_in, igrad, copy_sems.at[7 + b], b).wait()
    for s in range(3):
        close_section(s)
    for item in vectors + [reduce_g, reduce_p, reduce_m, reduce_e]:
        item.close()


def finish_kernel(
    out_in, igrad_in, panel,
    out, igrad, expand, gain1, bias1, depth, gain2, bias2, reduce, b_reduce, excite, b_excite, project, gain3, bias3,
    held, sems,
):
    pieces = []
    for i in range(6):
        source, target = ((out_in, out), (igrad_in, igrad))[i // 3]
        at = pl.ds((i % 3) * (ROWS // 3), ROWS // 3)
        pieces.append((
            pltpu.make_async_copy(source.at[:, at], held.at[i], sems.at[0, i]),
            pltpu.make_async_copy(held.at[i], target.at[:, at], sems.at[1, i]),
        ))
    for arrive, _ in pieces:
        arrive.start()
    expand[...] = panel[0:LANE, :].T[0:OWN, 0:D]
    project[...] = panel[OUT_PROJECT : OUT_PROJECT + LANE, :].T[0:OWN, 0:D]
    for arrive, leave in pieces:
        arrive.wait()
        leave.start()
    for a in range(5):
        depth[a] = panel[OUT_MISC + 5 * a : OUT_MISC + 5 * a + 5, 0:OWN]
    reduce[...] = panel[OUT_MISC + AT_R : OUT_MISC + AT_R + SQZ, 0:OWN]
    excite[0:IN_THIRD, :] = panel[OUT_MISC + AT_X : OUT_MISC + 128, 0:OWN]
    excite[IN_THIRD:SQZ, :] = panel[OUT_PROJECT + D + 1 : OUT_PROJECT + D + 1 + SQZ - IN_THIRD, 0:OWN]
    b_excite[...] = panel[OUT_PROJECT + D : OUT_PROJECT + D + 1, 0:OWN]
    b_reduce[...] = panel[OUT_PROJECT + D + 8 : OUT_PROJECT + D + 9, 0:SQZ]
    for i, ref in enumerate((gain1, bias1, gain2, bias2)):
        ref[...] = panel[OUT_VECS + i : OUT_VECS + i + 1, 0:OWN]
    gain3[...] = panel[OUT_SMALL : OUT_SMALL + 1, 0:D]
    bias3[...] = panel[OUT_SMALL + 1 : OUT_SMALL + 2, 0:D]
    for _, leave in pieces:
        leave.wait()


def body(
    features, seg_units, w_expand, gain_one, bias_one, w_depth, gain_two, bias_two,
    w_reduce, b_reduce, w_excite, b_excite, w_project, gain_three, bias_three, cotangent,
):
    vm = pl.BlockSpec(memory_space=pltpu.VMEM)
    anywhere = pl.BlockSpec(memory_space=pl.ANY)
    big = pltpu.VMEM((288, 8, WIDE), F32)
    rows128 = pltpu.VMEM((288, 8, LANE), F32)
    half = pltpu.VMEM((ROWS, WIDE), BF16)

    def f32(*shape):
        return pltpu.VMEM(shape, F32)

    def b16(*shape):
        return pltpu.VMEM(shape, BF16)

    def shape(*dims):
        return jax.ShapeDtypeStruct(dims, F32)

    def row(vector):
        return vector.reshape(1, vector.shape[0])

    dma = pltpu.SemaphoreType.DMA
    slots = [f32(16, 8, WIDE), f32(4, 8, GROUP), f32(8, 8, GROUP), f32(16, 8, GROUP)]
    out, igrad, panel = pl.pallas_call(
        kernel,
        out_shape=(shape(D, ROWS), shape(D, ROWS), shape(RESULTS, GROUP)),
        in_specs=[anywhere, anywhere] + [vm] * 13 + [pl.BlockSpec(memory_space=pltpu.SMEM)],
        out_specs=(anywhere, anywhere, vm),
        scratch_shapes=[
            f32(D, ROWS), f32(D, ROWS), dma((14,)), f32(CHUNK, LANE), f32(GROUP, LANE),
            rows128, rows128, rows128, b16(ROWS, 384), b16(256, ROWS), b16(ROWS, 384), b16(512, ROWS), f32(3, 256, WIDE),
            big, big, big, big, half, half,
            f32(4, PANEL, GROUP), f32(128, WIDE), f32(128, WIDE), b16(128, WIDE), b16(128, WIDE),
            b16(256, WIDE), b16(256, WIDE), b16(BLOCKS, 256, WIDE), f32(48, WIDE), f32(48, WIDE), f32(12, 8, WIDE),
            f32(48, WIDE), f32(48, WIDE), f32(45, 8, LANE), f32(CELLS, 8, WIDE), f32(128, WIDE), f32(54, 2, 8, LANE), f32(54, 2, 8, LANE),
            f32(BLOCKS, 8, WIDE), f32(8, WIDE), f32(8, WIDE), f32(8, LANE), f32(16, LANE),
            f32(16, 8, WIDE), f32(16, 8, WIDE), f32(16, 8, WIDE), f32(8, 16, LANE),
            f32(2, 8, 16, LANE), f32(2, 16, 16, LANE), f32(3, 8, 8, LANE), f32(3, 16, 8, LANE),
            f32(8, 16, LANE), f32(16, 16, LANE), f32(8, 16, LANE),
        ]
        + slots * 3
        + [dma((3, 3)), dma((5, 4)), dma((6,)), dma((3, 8))],
        compiler_params=pltpu.CompilerParams(
            collective_id=0, has_side_effects=True, vmem_limit_bytes=64 * 1024 * 1024 - 65536
        ),
    )(
        features.T, cotangent.T, w_expand.T, w_project, w_reduce.T, w_excite, w_depth,
        row(gain_one), row(bias_one), row(gain_two), row(bias_two), row(b_excite), row(b_reduce), row(gain_three), row(bias_three),
        seg_units,
    )

    small = [
        (OWN, D), (1, OWN), (1, OWN), (5, 5, OWN), (1, OWN), (1, OWN),
        (SQZ, OWN), (1, SQZ), (SQZ, OWN), (1, OWN), (OWN, D), (1, D), (1, D),
    ]
    results = pl.pallas_call(
        finish_kernel,
        out_shape=(shape(D, ROWS), shape(D, ROWS)) + tuple(shape(*dims) for dims in small),
        in_specs=[anywhere, anywhere, vm],
        out_specs=(anywhere, anywhere) + (vm,) * 13,
        scratch_shapes=[f32(6, D, ROWS // 3), dma((2, 6))],
    )(out, igrad, panel)
    (out, igrad, expand, gain1, bias1, depth, gain2, bias2, reduce, small_b, excite, b_x, project, gain3, bias3) = results
    return (
        out.T, igrad.T, expand.T, gain1[0], bias1[0], depth, gain2[0], bias2[0],
        reduce.T, small_b[0], excite, b_x[0], project, gain3[0], bias3[0],
    )


def solution(mesh):
    placed = (
        P(("dp", "chan"), None),
        P("dp", None),
        P(None, "chan"),
        P("chan"),
        P("chan"),
        P(None, None, "chan"),
        P("chan"),
        P("chan"),
        P("chan", None),
        P(),
        P(None, "chan"),
        P("chan"),
        P("chan", None),
        P(),
        P(),
        P(("dp", "chan"), None),
    )
    return jax.shard_map(
        body,
        mesh=mesh,
        in_specs=placed,
        out_specs=(
            P(("dp", "chan"), None),
            P(("dp", "chan"), None),
            P(None, "chan"),
            P("chan"),
            P("chan"),
            P(None, None, "chan"),
            P("chan"),
            P("chan"),
            P("chan", None),
            P(),
            P(None, "chan"),
            P("chan"),
            P("chan", None),
            P(),
            P(),
        ),
        check_vma=False,
    )
```

```python
import jax
import jax.numpy as jnp
from jax import lax
from jax.experimental import pallas as pl
from jax.experimental.pallas import tpu as pltpu
from jax.sharding import PartitionSpec as P

MESH = pl.DeviceIdType.MESH
F32 = jnp.float32
BF16 = jnp.bfloat16
EPSILON = 0.001
PRECISE = lax.Precision.HIGHEST
D = 112
SQZ = 28
EXP = 672
H, W, CELLS = 6, 4, 24
TAPS = 25
BLOCK, BLOCKS = 16, 6
ROWS = 2304
CHUNK = BLOCK * CELLS
LANE = 128
WIDE = 768
GROUPS = WIDE // LANE
TOTAL = 294912.0
OWN = 168
REST = OWN - LANE

AT_EXPAND, AT_DEPTH, AT_VECS, AT_PROJECT, AT_REDUCE, AT_EXCITE, PANEL = 0, 112, 137, 144, 256, 288, 320
AT_DD, AT_PLAIN, AT_R, AT_X = TAPS, 2 * TAPS, 3 * TAPS, 3 * TAPS + SQZ
IN_THIRD = 128 - AT_X
OUT_PROJECT, OUT_MISC, OUT_VECS, OUT_SMALL, RESULTS = 128, 256, 384, 392, 400
GROUP = 2 * LANE


REPS = {}


def rep(name):
    count = REPS.get(name, 1)

    def run(fn):
        if count == 1:
            fn()
        else:
            lax.fori_loop(0, count, lambda i, carry: (fn(), carry)[1], 0)

    return run


def rloop(name, size):
    count = REPS.get(name, 1)

    def run(fn):
        if count == 1:
            pl.loop(0, size)(fn)
        else:
            pl.loop(0, size * count)(lambda i: fn(lax.rem(i, size)))

    return run


def split(values):
    high = values.astype(BF16)
    return high, (values - high.astype(F32)).astype(BF16)


def mm(a, b):
    return lax.dot_general(a, b, (((1,), (0,)), ((), ())), preferred_element_type=F32)


def mm_nt(a, b):
    return lax.dot_general(a, b, (((1,), (1,)), ((), ())), preferred_element_type=F32)


def exact(a, b, dims):
    return lax.dot_general(a, b, ((dims[:1], dims[1:]), ((), ())), precision=PRECISE, preferred_element_type=F32)


def pair(values):
    return jnp.concatenate(split(values), axis=0)


def pair_nt(a, b, rows, cols):
    r = mm_nt(a, b)
    return (r[0:rows, 0:cols] + r[rows:, cols:]) + (r[0:rows, cols:] + r[rows:, 0:cols])


def place():
    dp = lax.axis_index("dp")
    z = lax.axis_index("chan")
    return dp // 8, lax.rem(dp // 2, 4), lax.rem(dp, 2), z


def ring(step):
    return min(step, 4 - step)


def column_peers():
    x, y, c, z = place()
    moves = [(dz, dc) for dz in range(4) for dc in range(2) if dz or dc]
    moves.sort(key=lambda m: -10 * ring(m[0]) - m[1])
    base = x * 8 + y * 2
    zs = [lax.rem(z + dz, 4) for dz in range(4)]
    cs = [c, 1 - c]
    return z * 2 + c, [(zs[dz] * 2 + cs[dc], (base + cs[dc], zs[dz])) for dz, dc in moves]


def plane_peers():
    x, y, c, z = place()
    moves = [(dx, dy) for dx in range(4) for dy in range(4) if dx or dy]
    moves.sort(key=lambda m: -ring(m[0]) - ring(m[1]))
    xs = [lax.rem(x + dx, 4) for dx in range(4)]
    ys = [lax.rem(y + dy, 4) for dy in range(4)]
    peers = []
    for dx, dy in moves:
        rank = xs[dx] * 4 + ys[dy]
        peers.append((rank, (rank * 2 + c, z)))
    return x * 4 + y, peers


def push(sources, slots, mine, peers, send, recv):
    for rank, device in peers:
        pltpu.make_async_remote_copy(
            src_ref=sources(rank),
            dst_ref=slots.at[mine],
            send_sem=send,
            recv_sem=recv,
            device_id=device,
            device_id_type=MESH,
        ).start()


def drain(view, sem):
    pltpu.make_async_copy(view, view, sem).wait()


def add_slots(slots, count):
    total = slots[0]
    for k in range(1, count):
        total = total + slots[k]
    return total


class Vector:
    def __init__(self, column, plane, near, far, sems):
        self.column, self.plane, self.near, self.far, self.sems = column, plane, near, far, sems

    def start(self, value):
        mine, peers = self.column
        self.near[mine] = value
        push(lambda rank: self.near.at[mine], self.near, mine, peers, self.sems.at[0], self.sems.at[1])

    def middle(self):
        drain(self.near.at[pl.ds(0, 7)], self.sems.at[1])
        mine, peers = self.plane
        self.far[mine] = add_slots(self.near, 8)
        push(lambda rank: self.far.at[mine], self.far, mine, peers, self.sems.at[2], self.sems.at[3])

    def finish(self):
        drain(self.far.at[pl.ds(0, 15)], self.sems.at[3])
        return add_slots(self.far, 16)

    def close(self):
        drain(self.near.at[pl.ds(0, 7)], self.sems.at[0])
        drain(self.far.at[pl.ds(0, 15)], self.sems.at[2])


class Square:
    def __init__(self, column, plane, source, first, second, third, sems):
        self.column, self.plane = column, plane
        self.source, self.first, self.second, self.third, self.sems = source, first, second, third, sems

    def start(self):
        mine, peers = self.column
        self.first[mine] = self.source[mine]
        push(lambda rank: self.source.at[rank], self.first, mine, peers, self.sems.at[0], self.sems.at[1])

    def middle(self):
        drain(self.first.at[pl.ds(0, 7)], self.sems.at[1])
        mine, peers = self.plane
        self.second[mine] = add_slots(self.first, 8)
        push(lambda rank: self.second.at[mine], self.second, mine, peers, self.sems.at[2], self.sems.at[3])

    def last(self):
        drain(self.second.at[pl.ds(0, 15)], self.sems.at[3])
        mine, peers = self.column
        self.third[mine] = add_slots(self.second, 16)
        push(lambda rank: self.third.at[mine], self.third, mine, peers, self.sems.at[4], self.sems.at[5])

    def finish(self):
        drain(self.third.at[pl.ds(0, 7)], self.sems.at[5])
        return self.third[...].reshape(128, LANE)

    def close(self):
        drain(self.first.at[pl.ds(0, 7)], self.sems.at[0])
        drain(self.second.at[pl.ds(0, 15)], self.sems.at[2])
        drain(self.third.at[pl.ds(0, 7)], self.sems.at[4])


class Panel:
    def __init__(self, column, plane, ranges, source, first, parts, second, third, sems):
        self.column, self.plane, self.ranges = column, plane, ranges
        self.source, self.first, self.parts, self.second, self.third, self.sems = source, first, parts, second, third, sems

    def start(self, index):
        mine, peers = self.plane
        lo, hi = self.ranges[index]
        lanes = pl.ds(lo, hi - lo)
        self.first[mine, :, lo:hi] = self.source[mine, :, lo:hi]
        for rank, device in peers:
            pltpu.make_async_remote_copy(
                src_ref=self.source.at[rank, :, lanes],
                dst_ref=self.first.at[mine, :, lanes],
                send_sem=self.sems.at[0],
                recv_sem=self.sems.at[1 + index],
                device_id=device,
                device_id_type=MESH,
            ).start()

    def scattered(self, index, sem):
        lo, hi = self.ranges[index]
        drain(self.first.at[pl.ds(0, 15), :, pl.ds(lo, hi - lo)], self.sems.at[sem])

    def middle(self):
        for index in range(len(self.ranges)):
            self.scattered(index, 1 + index)
        total = add_slots(self.first, 16)
        mine, peers = self.column
        for z in range(4):
            self.parts[z, :, 0:LANE] = total[:, z * LANE : (z + 1) * LANE]
            rest = 4 + z // 2
            self.parts[z, :, LANE:GROUP] = total[:, rest * LANE : (rest + 1) * LANE]
        self.second[mine] = self.parts[mine // 2]
        push(lambda rank: self.parts.at[rank // 2], self.second, mine, peers, self.sems.at[4], self.sems.at[5])

    def last(self):
        drain(self.second.at[pl.ds(0, 7)], self.sems.at[5])
        mine, peers = self.plane
        self.third[mine] = add_slots(self.second, 8)
        push(lambda rank: self.third.at[mine], self.third, mine, peers, self.sems.at[6], self.sems.at[7])

    def finish(self):
        drain(self.third.at[pl.ds(0, 15)], self.sems.at[7])
        return self.third[...].reshape(128, GROUP)

    def sent(self):
        for index in range(len(self.ranges)):
            self.scattered(index, 0)

    def close(self):
        drain(self.second.at[pl.ds(0, 7)], self.sems.at[4])
        drain(self.third.at[pl.ds(0, 15)], self.sems.at[6])


def half_gate(values, scale, shift):
    h = values * scale + shift
    return h, jnp.tanh(h)


def slope_of(h, th):
    return (0.5 + 0.5 * th) * (1.0 + (h - h * th))


def sigmoid(v):
    return 1.0 / (1.0 + jnp.exp(-v))


def lanes_of(g):
    return pl.ds(pl.multiple_of(g * LANE, LANE), LANE)


def fold(v):
    return v[0] + v[1]


def row_sum(v):
    return jnp.sum(v, axis=0, keepdims=True)


def row_pairs():
    return [(i, i + a - 2, a) for a in range(5) for i in range(H) if 0 <= i + a - 2 < H]


def nine_weights(w):
    m2, m1, w0, p1, p2 = w
    return [
        w0, p1 - w0, m1 - w0,
        p2 - w0, w0 - p1 - p2, (p1 - m1) + (w0 - p2),
        m2 - w0, (m1 - p1) + (w0 - m2), w0 - m1 - m2,
    ]


def five_taps(g):
    return [
        g[6] - g[7] - g[8],
        (g[2] - g[5]) + (g[7] - g[8]),
        (g[0] - g[1]) - (g[2] + g[3]) + (g[4] + g[5]) - (g[6] - g[7] - g[8]),
        (g[1] - g[4]) + (g[5] - g[7]),
        g[3] - g[4] - g[5],
    ]


def nine_inputs(x):
    x02, x13 = x[0] + x[2], x[1] + x[3]
    return [x02 + x13, x13, x02, x[2] + x[3], x[3], x[2], x[0] + x[1], x[1], x[0]]


def nine_outputs(y):
    y02, y13 = y[0] + y[2], y[1] + y[3]
    return [y02 + y13, y02, y13, y[0] + y[1], y[0], y[1], y[2] + y[3], y[2], y[3]]


def expand_rows(target, expand, cell):
    for i in range(H):
        for m, v in enumerate(expand([cell(i * W + j) for j in range(W)])):
            target[i * 9 + m] = v


def convolve(inputs, outputs, weights, cols):
    for m in range(9):
        x = [inputs[i * 9 + m] for i in range(H)]
        w = [jnp.broadcast_to(weights[a * 9 + m : a * 9 + m + 1, cols], (8, LANE)) for a in range(5)]
        acc = [None] * H
        for i, ii, a in row_pairs():
            term = x[ii] * w[a]
            acc[i] = term if acc[i] is None else acc[i] + term
        for i in range(H):
            outputs[i * 9 + m] = acc[i]


def four_cells(outputs, i):
    m = [outputs[i * 9 + k] for k in range(9)]
    a, b, c, d, e, f = m[0] + m[1], m[0] + m[2], m[3] + m[4], m[3] + m[5], m[6] + m[7], m[6] + m[8]
    return [a + c, b + d, a + e, b + f]


def correlate(target, left, right):
    for m in range(9):
        x = [right[i * 9 + m] for i in range(H)]
        y = [left[i * 9 + m] for i in range(H)]
        acc = [None] * 5
        for i, ii, a in row_pairs():
            term = y[i] * x[ii]
            acc[a] = term if acc[a] is None else acc[a] + term
        for a in range(5):
            target[a * 9 + m] += fold(acc[a])


def row_sums(target, source, cols):
    for t in range(45):
        target[t : t + 1, cols] = row_sum(source[t])


def kernel(
    f_hbm, q_hbm, we_in, wp_in, wr_in, wx_in, wd_in, ga1_in, bi1_in, ga2_in, bi2_in, bx_in, br_in, ga3_in, bi3_in, units,
    f_in, q_in, o_panel,
    copy_sems, stage, wide_stage,
    f_rows, q_rows, p_rows, f3, ft, pg3, qpt, qa,
    e_ref, a1, dv, q2, act_hi, act_lo,
    gathered, we, wp, wr, wx, we_b, ws_b, wp_b, wd, wt, par, tq, td, acc45, acc24, cells, cov_we, nine_a, nine_b,
    pool, gates, spread, vec, sums, gp_panel, misc, g_panel,
    near, far, near2, far2,
    g_first, g_second, g_third,
    p_first, p_parts, p_second, p_third,
    m_first, m_parts, m_second, m_third,
    e_first, e_parts, e_second, e_third,
    w_sems, v_sems, g_sems, s_sems,
):
    fetch_f = pltpu.make_async_copy(f_hbm, f_in, copy_sems.at[1])
    fetch_f.start()
    fetch_q = pltpu.make_async_copy(q_hbm, q_in, copy_sems.at[0])
    fetch_q.start()
    x, y, c, z = place()
    column, plane = column_peers(), plane_peers()
    barrier = pltpu.get_barrier_semaphore()
    for _, device in column[1] + plane[1]:
        pl.semaphore_signal(barrier, inc=1, device_id=device, device_id_type=MESH)

    sum2a = Vector(column, plane, near2.at[0], far2.at[0], v_sems.at[0])
    sum2b = Vector(column, plane, near2.at[1], far2.at[1], v_sems.at[1])
    sum3 = Vector(column, plane, near2.at[2], far2.at[2], v_sems.at[2])
    sum4 = Vector(column, plane, near.at[0], far.at[0], v_sems.at[3])
    sum5 = Vector(column, plane, near.at[1], far.at[1], v_sems.at[4])
    vectors = [sum2a, sum2b, sum3, sum4, sum5]
    reduce_g = Square(column, plane, g_panel, g_first, g_second, g_third, g_sems)
    whole = [(0, WIDE)]
    reduce_p = Panel(column, plane, whole, gp_panel, p_first, p_parts, p_second, p_third, s_sems.at[0])
    reduce_m = Panel(column, plane, whole, misc, m_first, m_parts, m_second, m_third, s_sems.at[1])
    early_late = [(0, 2 * GROUP), (2 * GROUP, WIDE)]
    reduce_e = Panel(column, plane, early_late, gp_panel, e_first, e_parts, e_second, e_third, s_sems.at[2])

    fetch_f.wait()

    ones = jnp.where(lax.broadcasted_iota(jnp.int32, (16, ROWS), 0) == 0, 1.0, 0.0)
    hi, lo = split(jnp.concatenate([f_in[...], ones], axis=0))
    ft[0:128, :] = hi
    ft[128:256, :] = lo
    gram = mm_nt(ft[...], ft[...])
    gram = gram[0:128, 0:128] + (gram[0:128, 128:256] + gram[128:256, 0:128]) + gram[128:256, 128:256]
    g_panel[...] = gram.reshape(8, 16, LANE)
    pl.semaphore_wait(barrier, 22)
    reduce_g.start()

    sections = ((0, AT_DEPTH), (AT_DEPTH, AT_PROJECT), (AT_PROJECT, PANEL))
    odd = lax.rem(z, 2) == 1

    across = [(lax.rem(z + k, 4), {"chan": lax.rem(z + k, 4)}) for k in (2, 1, 3)]

    def halves(s):
        lo, hi = sections[s]
        size = (hi - lo) // 2
        return size, pl.ds(pl.multiple_of(lo + c * size, 8), size), pl.ds(lo, size)

    def send_section(s):
        lo, hi = sections[s]
        rest = gathered[z, lo:hi, LANE:GROUP]
        gathered[z, lo:hi, LANE:GROUP] = jnp.where(odd, pltpu.roll(rest, 64, 1), rest)
        size, rows, _ = halves(s)
        for _, device in across:
            pltpu.make_async_remote_copy(
                src_ref=gathered.at[z, rows],
                dst_ref=gathered.at[z, rows],
                send_sem=w_sems.at[0, s],
                recv_sem=w_sems.at[1, s],
                device_id=device,
                device_id_type=MESH,
            ).start()

    def forward_section(s):
        size, rows, some = halves(s)
        drain(gathered.at[pl.ds(0, 3), some], w_sems.at[1, s])
        for other, _ in across:
            pltpu.make_async_remote_copy(
                src_ref=gathered.at[other, rows],
                dst_ref=gathered.at[other, rows],
                send_sem=w_sems.at[0, s],
                recv_sem=w_sems.at[2, s],
                device_id=(x * 8 + y * 2 + 1 - c, z),
                device_id_type=MESH,
            ).start()

    def section(s):
        size, rows, some = halves(s)
        drain(gathered.at[pl.ds(0, 3), some], w_sems.at[2, s])

    def close_section(s):
        size, rows, some = halves(s)
        for _ in range(2):
            drain(gathered.at[pl.ds(0, 3), some], w_sems.at[0, s])

    def assembled(lo, rows):
        parts = [gathered[k, lo : lo + rows, 0:LANE] for k in range(4)]
        for k in (0, 2):
            parts.append(gathered[k, lo : lo + rows, LANE:GROUP] + gathered[k + 1, lo : lo + rows, LANE:GROUP])
        return jnp.concatenate(parts, axis=1)

    gathered[z] = jnp.zeros((PANEL, GROUP), F32)
    wide_stage[...] = jnp.zeros_like(wide_stage)
    wide_stage[0:OWN, 0:D] = we_in[...]
    gathered[z, 0:D, :] = wide_stage[...].T[0:D]
    send_section(0)
    for a in range(5):
        gathered[z, AT_DEPTH + 5 * a : AT_DEPTH + 5 * a + 5, 0:OWN] = wd_in[a]
    for i, row in enumerate((ga1_in, bi1_in, ga2_in, bi2_in, bx_in)):
        gathered[z, AT_VECS + i : AT_VECS + i + 1, 0:OWN] = row[...]
    send_section(1)

    tail = jnp.where(lax.broadcasted_iota(jnp.int32, (16, LANE), 0) == 0, 1.0, 0.0)

    def rows_of(source, tail, target):
        @pl.loop(0, BLOCKS)
        def _(b):
            for i in range(3):
                v = source[:, pl.ds(pl.multiple_of(b * CHUNK + i * LANE, LANE), LANE)]
                stage[i * LANE : (i + 1) * LANE, :] = jnp.concatenate([v, tail], axis=0).T
            for cell in range(CELLS):
                v = stage[pl.ds(cell, BLOCK, stride=CELLS), :]
                target[pl.ds((b * CELLS + cell) * 2, 2)] = v.reshape(2, 8, LANE)

    rows_of(f_in, tail, f_rows)

    @rloop("ft", 18)
    def _(i):
        v = f_rows[pl.ds(i * 16, 16)].reshape(128, LANE)
        rows = pl.ds(pl.multiple_of(i * 128, 128), 128)
        hi, lo = split(v)
        f3[rows, 0:128] = hi
        f3[rows, 128:256] = hi
        f3[rows, 256:384] = lo
        hi, lo = split(v.T)
        ft[0:128, rows] = hi
        ft[128:256, rows] = lo

    def parts_of(source, row):
        @pl.loop(0, 18)
        def _(i):
            hi, lo = split(source[pl.ds(i * 16, 16)].reshape(128, LANE).T)
            rows = pl.ds(pl.multiple_of(i * 128, 128), 128)
            qpt[row : row + 128, rows] = hi
            qpt[256 + row : 384 + row, rows] = lo

    reduce_g.middle()
    fetch_q.wait()
    rows_of(q_in, jnp.zeros((16, LANE), F32), q_rows)
    parts_of(q_rows, 0)
    sums[...] = jnp.zeros_like(sums)
    qa[...] = jnp.zeros_like(qa)

    forward_section(0)
    forward_section(1)
    section(0)
    we[0:D, :] = assembled(0, D)
    we[D:128, :] = jnp.zeros((128 - D, WIDE), F32)
    hi, lo = split(we[...])
    we_b[0:128, :] = hi
    we_b[128:256, :] = lo

    @rloop("E", BLOCKS)
    def _(b):
        @pl.when(b == 3)
        def _():
            reduce_g.last()

        rows = pl.ds(pl.multiple_of(b * CHUNK, CHUNK), CHUNK)
        for n in range(3):
            cols = slice(n * GROUP, (n + 1) * GROUP)
            r = mm(f3[rows, 0:256], we_b[:, cols]) + mm(f3[rows, 256:384], we_b[0:128, cols])
            e_ref[pl.ds(b * 48, 48), :, cols] = r.reshape(48, 8, GROUP)

    section(1)
    taps = assembled(AT_DEPTH, 32)
    for a in range(5):
        row = [taps[5 * a + k : 5 * a + k + 1] for k in range(5)]
        for m, v in enumerate(nine_weights(row)):
            wd[a * 9 + m : a * 9 + m + 1, :] = v
        for m, v in enumerate(nine_weights(row[::-1])):
            wt[(4 - a) * 9 + m : (4 - a) * 9 + m + 1, :] = v
    gain1, bias1, gain2, bias2, bx = [taps[TAPS + i : TAPS + i + 1] for i in range(5)]
    wide_stage[0:OWN, 0:D] = wp_in[...]
    gathered[z, AT_PROJECT : AT_PROJECT + D, :] = wide_stage[...].T[0:D]
    gathered[z, AT_REDUCE : AT_REDUCE + SQZ, 0:OWN] = wr_in[...]
    gathered[z, AT_EXCITE : AT_EXCITE + SQZ, 0:OWN] = wx_in[...]

    gram = reduce_g.finish() * (1.0 / TOTAL)
    send_section(2)
    f_mean_row = gram[D : D + 1, :]
    f_mean = gram[:, D : D + 1]
    cov = gram - f_mean * f_mean_row
    hi, lo = split(cov)
    cov_we[...] = mm(jnp.concatenate([hi, hi], axis=1), we_b[...]) + mm(jnp.concatenate([lo, lo], axis=1), we_b[...])
    mean1 = row_sum(we[...] * f_mean)
    inv1 = lax.rsqrt(row_sum(we[...] * cov_we[...]) + EPSILON)
    s1 = gain1 * inv1
    t1 = bias1 - mean1 * s1

    def put(i, row, lo=0, hi=WIDE):
        par[i, :, lo:hi] = jnp.broadcast_to(row, (8, hi - lo))

    put(0, 0.5 * s1)
    put(1, 0.5 * t1)

    def put_sums(first, second, g, low, size):
        sums[pl.ds(g - low, 1), :] = row_sum(first)
        sums[pl.ds(g - low + size, 1), :] = row_sum(second)

    @rloop("conv1", GROUPS)
    def _(g):
        cols = lanes_of(g)

        def block(b, carry):
            total, square = carry
            base = b * 48
            scale, shift = par[0, :, cols], par[1, :, cols]

            def activate(cell):
                at = pl.ds(base + 2 * cell, 2)
                h, th = half_gate(e_ref[at, :, cols], scale, shift)
                act = h + h * th
                a1[at, :, cols] = act
                return act

            expand_rows(nine_a, nine_inputs, activate)
            convolve(nine_a, nine_b, wd, cols)
            for i in range(H):
                for j, v in enumerate(four_cells(nine_b, i)):
                    dv[pl.ds(base + 2 * (i * W + j), 2), :, cols] = v
                    total = total + fold(v)
                    square = square + fold(v * v)
            return total, square

        zero = jnp.zeros((8, LANE), F32)
        total, square = lax.fori_loop(0, BLOCKS, block, (zero, zero))
        put_sums(total, square, g, jnp.where(g < 3, 0, 3), 3)

        @pl.when(g == 2)
        def _():
            sum2a.start(sums[0:8, :])

        @pl.when(g == 4)
        def _():
            forward_section(2)

        @pl.when(g == 5)
        def _():
            sum2a.middle()
            sum2b.start(sums[0:8, :])

    def wide(rows, first, count):
        return jnp.concatenate([rows[first + g : first + g + 1, :] for g in range(count)], axis=1)

    mean2, inv2 = [None] * 2, [None] * 2

    def second_norm(got, lo, hi):
        count = (hi - lo) // LANE
        mean = wide(got, 0, count) * (1.0 / TOTAL)
        inv = lax.rsqrt(wide(got, count, count) * (1.0 / TOTAL) - mean * mean + EPSILON)
        scale = par[7, 0:1, lo:hi] * inv
        put(2, 0.5 * scale, lo, hi)
        put(3, 0.5 * (par[8, 0:1, lo:hi] - mean * scale), lo, hi)
        put(9, mean, lo, hi)
        put(10, inv, lo, hi)
        put(11, scale, lo, hi)

    put(7, gain2)
    put(8, bias2)

    def one_products(g):
        cols = lanes_of(g)
        acc45[...] = jnp.zeros_like(acc45)
        acc24[...] = jnp.zeros_like(acc24)

        @pl.loop(0, BLOCKS)
        def _(b):
            def act(cell):
                v = a1[pl.ds(b * 48 + 2 * cell, 2), :, cols]
                acc24[cell] += fold(v)
                return v

            expand_rows(nine_a, nine_inputs, act)
            expand_rows(nine_b, nine_outputs, lambda cell: dv[pl.ds(b * 48 + 2 * cell, 2), :, cols])
            correlate(acc45, nine_b, nine_a)

        row_sums(td, acc45, cols)
        for cell in range(CELLS):
            cells[cell : cell + 1, cols] = row_sum(acc24[cell])

    def one_activation(g):
        cols = lanes_of(g)

        @pl.loop(0, BLOCKS)
        def _(b):
            scale, shift = par[2, :, cols], par[3, :, cols]
            pooled = jnp.zeros((8, LANE), F32)
            for cell in range(CELLS):
                at = pl.ds(b * 48 + 2 * cell, 2)
                h, th = half_gate(dv[at, :, cols], scale, shift)
                q2[at, :, cols] = th
                act = h + h * th
                pooled = pooled + fold(act)
                hi, lo = split(act.reshape(16, LANE))
                rows = pl.ds(b * CHUNK + 16 * cell, 16)
                act_hi[rows, cols] = hi
                act_lo[rows, cols] = lo
            pool[b, :, cols] = pooled

    @pl.loop(0, 12)
    def _(step):
        @pl.when(step == 3)
        def _():
            sum2b.middle()

        @pl.when(step == 5)
        def _():
            second_norm(sum2a.finish(), 0, 3 * LANE)

        @pl.when(step == 9)
        def _():
            second_norm(sum2b.finish(), 3 * LANE, WIDE)

        early = (step < 5) | (step == 8)

        @pl.when(early)
        def _():
            one_products(jnp.where(step == 8, 5, step))

        @pl.when(jnp.logical_not(early))
        def _():
            one_activation(jnp.where(step < 8, step - 5, step - 6))

    section(2)
    wp[0:D, :] = assembled(AT_PROJECT, D)
    wp[D:128, :] = jnp.zeros((128 - D, WIDE), F32)
    hi, lo = split(assembled(AT_REDUCE, 32))
    wr[...] = jnp.concatenate([hi, lo, hi, lo], axis=0)
    hi, lo = split(assembled(AT_EXCITE, 32))
    wx[...] = jnp.concatenate([hi, lo, hi, lo], axis=0)
    seg = lax.broadcasted_iota(jnp.int32, (8, LANE), 0)
    blk = lax.broadcasted_iota(jnp.int32, (8, LANE), 1)
    u0, u1, u2 = units[z, 0], units[z, 1], units[z, 2]
    lower = jnp.where(seg == 0, 0, jnp.where(seg == 1, u0, u0 + u1))
    length = jnp.where(seg == 0, u0, jnp.where(seg == 1, u1, u2))
    member = jnp.where((seg < 3) & (blk >= lower) & (blk < lower + length), 1.0, 0.0)
    per_count = jnp.where(seg < 3, 1.0 / (length * (BLOCK * CELLS)).astype(F32), 0.0)[:, 0:1]
    live = jnp.where(seg < 3, 1.0, 0.0)[:, 0:1]

    vec[...] = jnp.zeros((8, LANE), F32)
    vec[0:1, 0:SQZ] = br_in[...]
    pooled = jnp.zeros((8, WIDE), F32)
    for b in range(BLOCKS):
        pooled = pooled + member[:, b : b + 1] * row_sum(pool[b])
    plain_sums = pooled
    pooled = pooled * per_count
    pooled_pair = pair(pooled)
    reduced = pair_nt(pooled_pair, wr[0:64, :], 8, 32) + vec[0:1, 0:32]
    sig_r = sigmoid(reduced)
    squeezed = reduced * sig_r * live

    def quad(values):
        hi, lo = split(values)
        return jnp.concatenate([hi, hi, lo, lo], axis=1)

    gate = sigmoid(mm(quad(squeezed), wx[...]) + bx)

    def of_blocks(rows, b):
        return row_sum(member[:, b : b + 1] * rows)

    for b in range(BLOCKS):
        gates[b : b + 1, :] = of_blocks(gate, b)

    def project(b, carry):
        rows = slice(b * CHUNK, (b + 1) * CHUNK)
        hi, lo = split(wp[...] * gates[b : b + 1, :])
        wp_b[b, 0:128, :] = hi
        wp_b[b, 128:256, :] = lo
        r = mm_nt(act_hi[rows, :], wp_b[b])
        r = r[:, 0:128] + r[:, 128:256] + mm_nt(act_lo[rows, :], wp_b[b, 0:128, :])
        r = r.reshape(48, 8, LANE)
        q = q_rows[pl.ds(b * 48, 48)]
        p_rows[pl.ds(b * 48, 48)] = r
        return tuple(old + jnp.sum(new, axis=0) for old, new in zip(carry, (r, r * r, q, q * r)))

    zero = jnp.zeros((8, LANE), F32)
    four = (zero,) * 4
    for b in range(BLOCKS):
        four = project(b, four)
    for i in range(4):
        vec[i : i + 1, :] = row_sum(four[i])
    sum3.start(vec[...])

    parts_of(p_rows, 128)

    @rloop("qa", 3)
    def _(i):
        for b in (2 * i, 2 * i + 1):
            rows = pl.ds(pl.multiple_of(b * CHUNK, CHUNK), CHUNK)
            inside = [jnp.where((b >= low) & (b < high), 1.0, 0.0) for low, high in ((0, u0), (u0, u0 + u1), (u0 + u1, 6))]
            m = mm(qpt[:, rows], act_hi[rows, :])
            m = m[0:256] + m[256:512] + mm(qpt[0:256, rows], act_lo[rows, :])
            for k in range(3):
                qa[k] += m * inside[k]

        @pl.when(i == 1)
        def _():
            sum3.middle()

    @rloop("slope2", GROUPS)
    def _(g):
        cols = lanes_of(g)

        @pl.loop(0, BLOCKS)
        def _(b):
            scale, shift = par[2, :, cols], par[3, :, cols]
            for cell in range(CELLS):
                at = pl.ds(b * 48 + 2 * cell, 2)
                q2[at, :, cols] = slope_of(dv[at, :, cols] * scale + shift, q2[at, :, cols])

    got = sum3.finish() * (1.0 / TOTAL)
    vec[...] = jnp.zeros((8, LANE), F32)
    vec[0:1, 0:D] = ga3_in[...]
    vec[1:2, 0:D] = bi3_in[...]
    gain3, bias3 = vec[0:1, :], vec[1:2, :]
    mean3 = got[0:1]
    inv3 = lax.rsqrt(got[1:2] - mean3 * mean3 + EPSILON)
    b3 = got[2:3]
    g3 = (got[3:4] - mean3 * got[2:3]) * inv3
    o_panel[OUT_SMALL : OUT_SMALL + 1, 0:LANE] = g3 * TOTAL
    o_panel[OUT_SMALL + 1 : OUT_SMALL + 2, 0:LANE] = b3 * TOTAL
    s3 = gain3 * inv3
    t3 = bias3 - mean3 * s3
    pg_p = -s3 * inv3 * g3
    pg_0 = -s3 * b3 - pg_p * mean3

    columns = jnp.concatenate([s3, pg_p, pg_0, jnp.zeros((5, LANE), F32)], axis=0).T
    by_q, by_p, by_1 = columns[:, 0:1], columns[:, 1:2], columns[:, 2:3]
    base = row_sum(wp[...] * by_1)
    w_q, w_p = wp[...] * by_q, wp[...] * by_p
    gate_grad = jnp.concatenate(
        [row_sum(w_q * qa[k, 0:128] + w_p * qa[k, 128:256]) + base * plain_sums[k : k + 1] for k in range(3)]
        + [jnp.zeros((5, WIDE), F32)],
        axis=0,
    )
    excite_in = gate_grad * gate * (1.0 - gate)
    reduced_grad = pair_nt(pair(excite_in), wx[0:64, :], 8, 32) * (sig_r * (1.0 + reduced * (1.0 - sig_r))) * live
    pooled_grad = mm(quad(reduced_grad), wr[...]) * per_count
    for b in range(BLOCKS):
        spread[b : b + 1, :] = of_blocks(pooled_grad, b)

    @rloop("pgs", BLOCKS)
    def _(b):
        at = pl.ds(b * 48, 48)
        hi, lo = split((q_rows[at] * s3 + (p_rows[at] * pg_p + pg_0)).reshape(CHUNK, LANE))
        rows = pl.ds(pl.multiple_of(b * CHUNK, CHUNK), CHUNK)
        pg3[rows, 0:128] = hi
        pg3[rows, 128:256] = hi
        pg3[rows, 256:384] = lo

    def backward(i, carry):
        total, product = carry
        for b in (2 * i, 2 * i + 1):
            rows = pl.ds(pl.multiple_of(b * CHUNK, CHUNK), CHUNK)
            at = pl.ds(b * 48, 48)
            r = mm(pg3[rows, 0:256], wp_b[b]) + mm(pg3[rows, 256:384], wp_b[b, 0:128, :])
            r = (r.reshape(48, 8, WIDE) + spread[pl.ds(b, 1), :]) * q2[at]
            q2[at] = r
            total, product = total + jnp.sum(r, axis=0), product + jnp.sum(r * dv[at], axis=0)
        return total, product

    zero = jnp.zeros((8, WIDE), F32)
    total, product = lax.fori_loop(0, 3, backward, (zero, zero))
    total, product = row_sum(total), row_sum(product)
    for g in range(GROUPS):
        lanes = slice(g * LANE, (g + 1) * LANE)
        sums[g : g + 1, :] = total[:, lanes]
        sums[8 + g : 9 + g, :] = product[:, lanes]
    sum4.start(sums[...])

    gp = jnp.zeros((128, WIDE), F32)
    for k in range(3):
        gp = gp + gate[k : k + 1] * (by_q * qa[k, 0:128] + by_p * qa[k, 128:256] + by_1 * plain_sums[k : k + 1])
    gp_panel[...] = gp.reshape(16, 8, WIDE)
    g_excite = exact(squeezed, excite_in, (0, 0))
    gp_panel[14, 0:1, :] = row_sum(excite_in)
    gp_panel[15, 0:1, :] = jnp.zeros((1, WIDE), F32)
    for k in range(4):
        gp_panel[15, 0:1, k * LANE : k * LANE + 32] = row_sum(reduced_grad)
    for i in range(IN_THIRD, SQZ):
        gp_panel[14, 1 + i - IN_THIRD : 2 + i - IN_THIRD, :] = g_excite[i : i + 1]
    reduce_p.start(0)

    def put_misc(row, values):
        for i in range(values.shape[0]):
            misc[(row + i) // 8, (row + i) % 8 : (row + i) % 8 + 1, :] = values[i : i + 1]

    put_misc(AT_R, exact(reduced_grad, pooled, (0, 0))[0:SQZ])
    put_misc(AT_X, g_excite[0:IN_THIRD])

    @rloop("tq", GROUPS)
    def _(g):
        cols = lanes_of(g)
        acc45[...] = jnp.zeros_like(acc45)

        @pl.loop(0, BLOCKS)
        def _(b):
            expand_rows(nine_a, nine_inputs, lambda cell: a1[pl.ds(b * 48 + 2 * cell, 2), :, cols])
            expand_rows(nine_b, nine_outputs, lambda cell: q2[pl.ds(b * 48 + 2 * cell, 2), :, cols])
            correlate(acc45, nine_b, nine_a)
            scale, shift = par[0, :, cols], par[1, :, cols]
            for cell in range(CELLS):
                at = pl.ds(b * 48 + 2 * cell, 2)
                e_ref[at, :, cols] = slope_of(*half_gate(e_ref[at, :, cols], scale, shift))

        row_sums(tq, acc45, cols)

        @pl.when(g == 2)
        def _():
            sum4.middle()

    def own_lanes(rows):
        first = rows[:, 0:LANE]
        rest = rows[:, LANE:GROUP]
        return first, jnp.where(odd, pltpu.roll(rest, 64, 1), rest)

    def own_wide(rows):
        first = jnp.zeros((rows.shape[0], LANE), F32)
        rest = jnp.zeros((rows.shape[0], LANE), F32)
        for k in range(4):
            first = jnp.where(z == k, rows[:, k * LANE : (k + 1) * LANE], first)
        for k in range(2):
            rest = jnp.where(z // 2 == k, rows[:, (4 + k) * LANE : (5 + k) * LANE], rest)
        return jnp.concatenate([first, rest], axis=1)

    def emit(row, values):
        first, rest = own_lanes(values)
        o_panel[row : row + values.shape[0], 0:LANE] = first
        o_panel[row : row + values.shape[0], LANE:GROUP] = rest

    def emit_vector(i, row):
        emit(OUT_VECS + i, own_wide(row))

    for t in range(TAPS):
        a, k = t // 5, t % 5
        plain = None
        for i in range(H):
            for j in range(W):
                ii, jj = i + a - 2, j + k - 2
                if 0 <= ii < H and 0 <= jj < W:
                    v = cells[ii * W + jj : ii * W + jj + 1, :]
                    plain = v if plain is None else plain + v
        put_misc(AT_PLAIN + t, plain)
    for first, source in ((0, tq), (AT_DD, td)):
        for a in range(5):
            for k, v in enumerate(five_taps([source[a * 9 + m : a * 9 + m + 1, :] for m in range(9)])):
                put_misc(first + 5 * a + k, v)
    reduce_m.start(0)

    got = sum4.finish()
    mean2, inv2, s2 = [par[i, 0:1, :] for i in (9, 10, 11)]
    b2 = wide(got, 0, GROUPS)
    g2 = (wide(got, 8, GROUPS) - mean2 * b2) * inv2
    c3 = -s2 * inv2 * g2 * (1.0 / TOTAL)
    c2 = -s2 * b2 * (1.0 / TOTAL) - c3 * mean2
    put(4, s2)
    put(5, c2)
    put(6, c3)
    emit_vector(2, g2)
    emit_vector(3, b2)

    @rloop("conv2", GROUPS)
    def _(g):
        @pl.when(g == 1)
        def _():
            reduce_p.middle()
            reduce_p.sent()

        @pl.when(g == 4)
        def _():
            reduce_p.last()

        cols = lanes_of(g)

        @pl.loop(0, BLOCKS)
        def _(b):
            base = b * 48
            k1, k2, k3 = par[4, :, cols], par[5, :, cols], par[6, :, cols]

            def grad(cell):
                at = pl.ds(base + 2 * cell, 2)
                return q2[at, :, cols] * k1 + (dv[at, :, cols] * k3 + k2)

            expand_rows(nine_a, nine_inputs, grad)
            convolve(nine_a, nine_b, wt, cols)
            for i in range(H):
                for j, v in enumerate(four_cells(nine_b, i)):
                    at = pl.ds(base + 2 * (i * W + j), 2)
                    hi, lo = split((v * e_ref[at, :, cols]).reshape(16, LANE))
                    rows = pl.ds(b * CHUNK + 16 * (i * W + j), 16)
                    act_hi[rows, cols] = hi
                    act_lo[rows, cols] = lo

        @pl.when(lax.rem(g, 2) == 1)
        def _():
            n = g // 2
            cols = pl.ds(pl.multiple_of(n * GROUP, GROUP), GROUP)
            m = mm(ft[...], act_hi[:, cols])
            m = m[0:128] + m[128:256] + mm(ft[0:128, :], act_lo[:, cols])
            gp_panel[:, :, cols] = m.reshape(16, 8, GROUP)
            product = row_sum(m * we[:, cols])
            for half in range(2):
                lanes = slice(half * LANE, (half + 1) * LANE)
                sums[pl.ds(g - 1 + half, 1), :] = m[D : D + 1, lanes]
                sums[pl.ds(g + 7 + half, 1), :] = product[:, lanes]

            @pl.when(g == 3)
            def _():
                reduce_e.start(0)

    reduce_e.start(1)
    sum5.start(sums[...])
    reduce_m.middle()

    hi, lo = split(we[...] * s1)
    ws_b[0:128, :] = hi
    ws_b[128:256, :] = lo

    @rloop("ig", 3)
    def _(i):
        rows = pl.ds(pl.multiple_of(i * 2 * CHUNK, 2 * CHUNK), 2 * CHUNK)
        r = mm_nt(act_hi[rows, :], ws_b[...])
        r = r[:, 0:128] + r[:, 128:256] + mm_nt(act_lo[rows, :], ws_b[0:128, :])
        q_rows[pl.ds(i * 96, 96)] += r.reshape(96, 8, LANE)

    sum5.middle()

    def write(target, b, rows_of_cell):
        for cell in range(CELLS):
            stage[pl.ds(cell, BLOCK, stride=CELLS), :] = rows_of_cell(pl.ds(b * 48 + 2 * cell, 2)).reshape(16, LANE)
        for i in range(3):
            at = pl.ds(pl.multiple_of(b * CHUNK + i * LANE, LANE), LANE)
            target[:, at] = stage[i * LANE : (i + 1) * LANE, :].T[0:D]

    @rloop("out", BLOCKS)
    def _(b):
        write(f_in, b, lambda at: f_rows[at] + (p_rows[at] * s3 + t3))

    reduce_e.middle()
    reduce_m.last()
    emit(OUT_PROJECT, reduce_p.finish())
    reduce_e.last()
    got = sum5.finish()
    b1 = wide(got, 0, GROUPS)
    g1 = (wide(got, 8, GROUPS) - mean1 * b1) * inv1
    k3 = -s1 * inv1 * g1 * (1.0 / TOTAL)
    k2 = -s1 * b1 * (1.0 / TOTAL) - k3 * mean1
    left = jnp.where(lax.broadcasted_iota(jnp.int32, (128, WIDE), 0) == D, k2, we[...] * k3)
    mix = pair_nt(pair(left), we_b[...], 128, 128)
    mix_hi, mix_lo = split(mix)
    mix_all = jnp.concatenate([mix_hi, mix_lo], axis=0)

    @rloop("ig2", BLOCKS)
    def _(b):
        rows = pl.ds(pl.multiple_of(b * CHUNK, CHUNK), CHUNK)
        r = mm(f3[rows, 0:256], mix_all) + mm(f3[rows, 256:384], mix_hi)
        q_rows[pl.ds(b * 48, 48)] += r.reshape(48, 8, LANE)
        write(q_in, b, lambda at: q_rows[at])

    emit_vector(0, g1)
    emit_vector(1, b1)
    total_m = reduce_m.finish()
    emit(OUT_MISC, total_m)
    by = [own_wide(v) for v in (s2, c2, c3)]
    taps_grad = total_m[0:TAPS] * by[0] + total_m[AT_DD : AT_DD + TAPS] * by[2] + total_m[AT_PLAIN : AT_PLAIN + TAPS] * by[1]
    emit(OUT_MISC, taps_grad)
    total_e = reduce_e.finish()
    emit(0, own_wide(s1) * (total_e - f_mean * own_wide(b1) - own_wide(cov_we[...]) * own_wide(inv1 * g1)))

    for s in range(3):
        close_section(s)
    reduce_m.sent()
    reduce_e.sent()
    for item in vectors + [reduce_g, reduce_p, reduce_m, reduce_e]:
        item.close()


def finish_kernel(
    out_in, igrad_in, panel,
    out, igrad, expand, gain1, bias1, depth, gain2, bias2, reduce, b_reduce, excite, b_excite, project, gain3, bias3,
    sems,
):
    large = [pltpu.make_async_copy(out_in, out, sems.at[0]), pltpu.make_async_copy(igrad_in, igrad, sems.at[1])]
    for copy in large:
        copy.start()
    expand[...] = panel[0:LANE, :].T[0:OWN, 0:D]
    project[...] = panel[OUT_PROJECT : OUT_PROJECT + LANE, :].T[0:OWN, 0:D]
    for a in range(5):
        depth[a] = panel[OUT_MISC + 5 * a : OUT_MISC + 5 * a + 5, 0:OWN]
    reduce[...] = panel[OUT_MISC + AT_R : OUT_MISC + AT_R + SQZ, 0:OWN]
    excite[0:IN_THIRD, :] = panel[OUT_MISC + AT_X : OUT_MISC + 128, 0:OWN]
    excite[IN_THIRD:SQZ, :] = panel[OUT_PROJECT + D + 1 : OUT_PROJECT + D + 1 + SQZ - IN_THIRD, 0:OWN]
    b_excite[...] = panel[OUT_PROJECT + D : OUT_PROJECT + D + 1, 0:OWN]
    b_reduce[...] = panel[OUT_PROJECT + D + 8 : OUT_PROJECT + D + 9, 0:SQZ]
    for i, ref in enumerate((gain1, bias1, gain2, bias2)):
        ref[...] = panel[OUT_VECS + i : OUT_VECS + i + 1, 0:OWN]
    gain3[...] = panel[OUT_SMALL : OUT_SMALL + 1, 0:D]
    bias3[...] = panel[OUT_SMALL + 1 : OUT_SMALL + 2, 0:D]
    for copy in large:
        copy.wait()


def body(
    features, seg_units, w_expand, gain_one, bias_one, w_depth, gain_two, bias_two,
    w_reduce, b_reduce, w_excite, b_excite, w_project, gain_three, bias_three, cotangent,
):
    vm = pl.BlockSpec(memory_space=pltpu.VMEM)
    anywhere = pl.BlockSpec(memory_space=pl.ANY)
    big = pltpu.VMEM((288, 8, WIDE), F32)
    rows128 = pltpu.VMEM((288, 8, LANE), F32)
    half = pltpu.VMEM((ROWS, WIDE), BF16)

    def f32(*shape):
        return pltpu.VMEM(shape, F32)

    def b16(*shape):
        return pltpu.VMEM(shape, BF16)

    def shape(*dims):
        return jax.ShapeDtypeStruct(dims, F32)

    def row(vector):
        return vector.reshape(1, vector.shape[0])

    dma = pltpu.SemaphoreType.DMA
    slots = [f32(16, 8, WIDE), f32(4, 8, GROUP), f32(8, 8, GROUP), f32(16, 8, GROUP)]
    out, igrad, panel = pl.pallas_call(
        kernel,
        out_shape=(f32(D, ROWS), f32(D, ROWS), f32(RESULTS, GROUP)),
        in_specs=[anywhere, anywhere] + [vm] * 13 + [pl.BlockSpec(memory_space=pltpu.SMEM)],
        out_specs=(vm,) * 3,
        scratch_shapes=[
            dma((2,)), f32(CHUNK, LANE), f32(GROUP, LANE),
            rows128, rows128, rows128, b16(ROWS, 384), b16(256, ROWS), b16(ROWS, 384), b16(512, ROWS), f32(3, 256, WIDE),
            big, big, big, big, half, half,
            f32(4, PANEL, GROUP), f32(128, WIDE), f32(128, WIDE), b16(128, WIDE), b16(128, WIDE),
            b16(256, WIDE), b16(256, WIDE), b16(BLOCKS, 256, WIDE), f32(48, WIDE), f32(48, WIDE), f32(12, 8, WIDE),
            f32(48, WIDE), f32(48, WIDE), f32(45, 8, LANE), f32(CELLS, 8, LANE), f32(CELLS, WIDE), f32(128, WIDE), f32(54, 2, 8, LANE), f32(54, 2, 8, LANE),
            f32(BLOCKS, 8, WIDE), f32(8, WIDE), f32(8, WIDE), f32(8, LANE), f32(16, LANE),
            f32(16, 8, WIDE), f32(16, 8, WIDE), f32(8, 16, LANE),
            f32(2, 8, 16, LANE), f32(2, 16, 16, LANE), f32(3, 8, 8, LANE), f32(3, 16, 8, LANE),
            f32(8, 16, LANE), f32(16, 16, LANE), f32(8, 16, LANE),
        ]
        + slots * 3
        + [dma((3, 3)), dma((5, 4)), dma((6,)), dma((3, 8))],
        compiler_params=pltpu.CompilerParams(
            collective_id=0, has_side_effects=True, vmem_limit_bytes=61 * 1024 * 1024 + 256 * 1024
        ),
    )(
        features.T, cotangent.T, w_expand.T, w_project, w_reduce.T, w_excite, w_depth,
        row(gain_one), row(bias_one), row(gain_two), row(bias_two), row(b_excite), row(b_reduce), row(gain_three), row(bias_three),
        seg_units,
    )

    small = [
        (OWN, D), (1, OWN), (1, OWN), (5, 5, OWN), (1, OWN), (1, OWN),
        (SQZ, OWN), (1, SQZ), (SQZ, OWN), (1, OWN), (OWN, D), (1, D), (1, D),
    ]
    results = pl.pallas_call(
        finish_kernel,
        out_shape=(shape(D, ROWS), shape(D, ROWS)) + tuple(shape(*dims) for dims in small),
        in_specs=[vm] * 3,
        out_specs=(anywhere, anywhere) + (vm,) * 13,
        scratch_shapes=[dma((2,))],
        compiler_params=pltpu.CompilerParams(vmem_limit_bytes=8 * 1024 * 1024),
    )(*(pltpu.with_memory_space_constraint(v, pltpu.VMEM) for v in (out, igrad, panel)))
    (out, igrad, expand, gain1, bias1, depth, gain2, bias2, reduce, small_b, excite, b_x, project, gain3, bias3) = results
    return (
        out.T, igrad.T, expand.T, gain1[0], bias1[0], depth, gain2[0], bias2[0],
        reduce.T, small_b[0], excite, b_x[0], project, gain3[0], bias3[0],
    )


def solution(mesh):
    placed = (
        P(("dp", "chan"), None),
        P("dp", None),
        P(None, "chan"),
        P("chan"),
        P("chan"),
        P(None, None, "chan"),
        P("chan"),
        P("chan"),
        P("chan", None),
        P(),
        P(None, "chan"),
        P("chan"),
        P("chan", None),
        P(),
        P(),
        P(("dp", "chan"), None),
    )
    return jax.shard_map(
        body,
        mesh=mesh,
        in_specs=placed,
        out_specs=(
            P(("dp", "chan"), None),
            P(("dp", "chan"), None),
            P(None, "chan"),
            P("chan"),
            P("chan"),
            P(None, None, "chan"),
            P("chan"),
            P("chan"),
            P("chan", None),
            P(),
            P(None, "chan"),
            P("chan"),
            P("chan", None),
            P(),
            P(),
        ),
        check_vma=False,
    )
```

```python
import jax
import jax.numpy as jnp
import numpy as np
from jax import lax
from jax.experimental import pallas as pl
from jax.experimental.pallas import tpu as pltpu
from jax.sharding import PartitionSpec as P

MESH = pl.DeviceIdType.MESH
F32 = jnp.float32
BF16 = jnp.bfloat16
EPSILON = 0.001
PRECISE = lax.Precision.HIGHEST
D = 112
SQZ = 28
EXP = 672
H, W, CELLS = 6, 4, 24
TAPS = 25
BLOCK, BLOCKS = 16, 6
ROWS = 2304
CHUNK = BLOCK * CELLS
LANE = 128
WIDE = 768
GROUPS = WIDE // LANE
TOTAL = 294912.0
OWN = 168
REST = OWN - LANE

AT_EXPAND, AT_DEPTH, AT_VECS, AT_PROJECT, AT_REDUCE, AT_EXCITE, PANEL = 0, 112, 137, 144, 256, 288, 320
AT_DD, AT_PLAIN, AT_R, AT_X = TAPS, 2 * TAPS, 3 * TAPS, 3 * TAPS + SQZ
IN_THIRD = 128 - AT_X
OUT_PROJECT, OUT_MISC, OUT_VECS, OUT_SMALL, RESULTS = 128, 256, 384, 392, 400
GROUP = 2 * LANE


REPS = {}


def rep(name):
    count = REPS.get(name, 1)

    def run(fn):
        if count == 1:
            fn()
        else:
            lax.fori_loop(0, count, lambda i, carry: (fn(), carry)[1], 0)

    return run


def rloop(name, size):
    count = REPS.get(name, 1)

    def run(fn):
        if count == 1:
            pl.loop(0, size)(fn)
        else:
            pl.loop(0, size * count)(lambda i: fn(lax.rem(i, size)))

    return run


def split(values):
    high = values.astype(BF16)
    return high, (values - high.astype(F32)).astype(BF16)


def mm(a, b):
    return lax.dot_general(a, b, (((1,), (0,)), ((), ())), preferred_element_type=F32)


def mm_nt(a, b):
    return lax.dot_general(a, b, (((1,), (1,)), ((), ())), preferred_element_type=F32)


def exact(a, b, dims):
    return lax.dot_general(a, b, ((dims[:1], dims[1:]), ((), ())), precision=PRECISE, preferred_element_type=F32)


def pair(values):
    return jnp.concatenate(split(values), axis=0)


def pair_nt(a, b, rows, cols):
    r = mm_nt(a, b)
    return (r[0:rows, 0:cols] + r[rows:, cols:]) + (r[0:rows, cols:] + r[rows:, 0:cols])


def place():
    dp = lax.axis_index("dp")
    z = lax.axis_index("chan")
    return dp // 8, lax.rem(dp // 2, 4), lax.rem(dp, 2), z


def ring(step):
    return min(step, 4 - step)


def column_peers():
    x, y, c, z = place()
    moves = [(dz, dc) for dz in range(4) for dc in range(2) if dz or dc]
    moves.sort(key=lambda m: -10 * ring(m[0]) - m[1])
    base = x * 8 + y * 2
    zs = [lax.rem(z + dz, 4) for dz in range(4)]
    cs = [c, 1 - c]
    return z * 2 + c, [(zs[dz] * 2 + cs[dc], (base + cs[dc], zs[dz])) for dz, dc in moves]


def plane_peers():
    x, y, c, z = place()
    moves = [(dx, dy) for dx in range(4) for dy in range(4) if dx or dy]
    moves.sort(key=lambda m: -ring(m[0]) - ring(m[1]))
    xs = [lax.rem(x + dx, 4) for dx in range(4)]
    ys = [lax.rem(y + dy, 4) for dy in range(4)]
    peers = []
    for dx, dy in moves:
        rank = xs[dx] * 4 + ys[dy]
        peers.append((rank, (rank * 2 + c, z)))
    return x * 4 + y, peers


def push(sources, slots, mine, peers, send, recv):
    for rank, device in peers:
        pltpu.make_async_remote_copy(
            src_ref=sources(rank),
            dst_ref=slots.at[mine],
            send_sem=send,
            recv_sem=recv,
            device_id=device,
            device_id_type=MESH,
        ).start()


def drain(view, sem):
    pltpu.make_async_copy(view, view, sem).wait()


def add_slots(slots, count):
    total = slots[0]
    for k in range(1, count):
        total = total + slots[k]
    return total


class Vector:
    def __init__(self, column, plane, near, far, sems):
        self.column, self.plane, self.near, self.far, self.sems = column, plane, near, far, sems

    def start(self, value):
        mine, peers = self.column
        self.near[mine] = value
        push(lambda rank: self.near.at[mine], self.near, mine, peers, self.sems.at[0], self.sems.at[1])

    def middle(self):
        drain(self.near.at[pl.ds(0, 7)], self.sems.at[1])
        mine, peers = self.plane
        self.far[mine] = add_slots(self.near, 8)
        push(lambda rank: self.far.at[mine], self.far, mine, peers, self.sems.at[2], self.sems.at[3])

    def finish(self):
        drain(self.far.at[pl.ds(0, 15)], self.sems.at[3])
        return add_slots(self.far, 16)

    def close(self):
        drain(self.near.at[pl.ds(0, 7)], self.sems.at[0])
        drain(self.far.at[pl.ds(0, 15)], self.sems.at[2])


class Square:
    def __init__(self, column, plane, source, first, second, third, sems):
        self.column, self.plane = column, plane
        self.source, self.first, self.second, self.third, self.sems = source, first, second, third, sems

    def start(self):
        mine, peers = self.column
        self.first[mine] = self.source[mine]
        push(lambda rank: self.source.at[rank], self.first, mine, peers, self.sems.at[0], self.sems.at[1])

    def middle(self):
        drain(self.first.at[pl.ds(0, 7)], self.sems.at[1])
        mine, peers = self.plane
        self.second[mine] = add_slots(self.first, 8)
        push(lambda rank: self.second.at[mine], self.second, mine, peers, self.sems.at[2], self.sems.at[3])

    def last(self):
        drain(self.second.at[pl.ds(0, 15)], self.sems.at[3])
        mine, peers = self.column
        self.third[mine] = add_slots(self.second, 16)
        push(lambda rank: self.third.at[mine], self.third, mine, peers, self.sems.at[4], self.sems.at[5])

    def finish(self):
        drain(self.third.at[pl.ds(0, 7)], self.sems.at[5])
        return self.third[...].reshape(128, LANE)

    def close(self):
        drain(self.first.at[pl.ds(0, 7)], self.sems.at[0])
        drain(self.second.at[pl.ds(0, 15)], self.sems.at[2])
        drain(self.third.at[pl.ds(0, 7)], self.sems.at[4])


class Panel:
    def __init__(self, column, plane, ranges, source, first, parts, second, third, sems):
        self.column, self.plane, self.ranges = column, plane, ranges
        self.source, self.first, self.parts, self.second, self.third, self.sems = source, first, parts, second, third, sems

    def start(self, index):
        mine, peers = self.plane
        lo, hi = self.ranges[index]
        lanes = pl.ds(lo, hi - lo)
        self.first[mine, :, lo:hi] = self.source[mine, :, lo:hi]
        for rank, device in peers:
            pltpu.make_async_remote_copy(
                src_ref=self.source.at[rank, :, lanes],
                dst_ref=self.first.at[mine, :, lanes],
                send_sem=self.sems.at[0],
                recv_sem=self.sems.at[1 + index],
                device_id=device,
                device_id_type=MESH,
            ).start()

    def scattered(self, index, sem):
        lo, hi = self.ranges[index]
        drain(self.first.at[pl.ds(0, 15), :, pl.ds(lo, hi - lo)], self.sems.at[sem])

    def middle(self):
        for index in range(len(self.ranges)):
            self.scattered(index, 1 + index)
        total = add_slots(self.first, 16)
        mine, peers = self.column
        for z in range(4):
            self.parts[z, :, 0:LANE] = total[:, z * LANE : (z + 1) * LANE]
            rest = 4 + z // 2
            self.parts[z, :, LANE:GROUP] = total[:, rest * LANE : (rest + 1) * LANE]
        self.second[mine] = self.parts[mine // 2]
        push(lambda rank: self.parts.at[rank // 2], self.second, mine, peers, self.sems.at[4], self.sems.at[5])

    def last(self):
        drain(self.second.at[pl.ds(0, 7)], self.sems.at[5])
        mine, peers = self.plane
        self.third[mine] = add_slots(self.second, 8)
        push(lambda rank: self.third.at[mine], self.third, mine, peers, self.sems.at[6], self.sems.at[7])

    def finish(self):
        drain(self.third.at[pl.ds(0, 15)], self.sems.at[7])
        return self.third[...].reshape(128, GROUP)

    def sent(self):
        for index in range(len(self.ranges)):
            self.scattered(index, 0)

    def close(self):
        drain(self.second.at[pl.ds(0, 7)], self.sems.at[4])
        drain(self.third.at[pl.ds(0, 15)], self.sems.at[6])


def half_gate(values, scale, shift):
    h = values * scale + shift
    return h, jnp.tanh(h)


def twice_slope_of(h, th):
    return (1.0 + th) * (1.0 + (h - h * th))


def sigmoid(v):
    return 1.0 / (1.0 + jnp.exp(-v))


def lanes_of(g):
    return pl.ds(pl.multiple_of(g * LANE, LANE), LANE)


def fold(v):
    return v[0] + v[1]


def row_sum(v):
    return jnp.sum(v, axis=0, keepdims=True)


def row_pairs():
    return [(i, i + a - 2, a) for a in range(5) for i in range(H) if 0 <= i + a - 2 < H]


def nine_weights(w):
    m2, m1, w0, p1, p2 = w
    return [
        w0, p1 - w0, m1 - w0,
        p2 - w0, w0 - p1 - p2, (p1 - m1) + (w0 - p2),
        m2 - w0, (m1 - p1) + (w0 - m2), w0 - m1 - m2,
    ]


FIVE = (
    (0, 0, 0, 0, 0, 0, 1, -1, -1),
    (0, 0, 1, 0, 0, -1, 0, 1, -1),
    (1, -1, -1, -1, 1, 1, -1, 1, 1),
    (0, 1, 0, 0, -1, 1, 0, -1, 0),
    (0, 0, 0, 1, -1, -1, 0, 0, 0),
)
IN_D, IN_CELLS, IN_R, IN_X, SUMS = 48, 96, 120, 152, 192


def combination():
    c = np.zeros((128, SUMS), np.float32)
    for a in range(5):
        for k in range(5):
            t = 5 * a + k
            for m in range(9):
                c[t, 9 * a + m] = FIVE[k][m]
                c[AT_DD + t, IN_D + 9 * a + m] = FIVE[k][m]
            for i in range(H):
                for j in range(W):
                    ii, jj = i + a - 2, j + k - 2
                    if 0 <= ii < H and 0 <= jj < W:
                        c[AT_PLAIN + t, IN_CELLS + ii * W + jj] = 1.0
    for i in range(SQZ):
        c[AT_R + i, IN_R + i] = 1.0
    for i in range(IN_THIRD):
        c[AT_X + i, IN_X + i] = 1.0
    return c


def over_rows(x, weights, m, cols):
    w = [jnp.broadcast_to(weights[a * 9 + m : a * 9 + m + 1, cols], (8, LANE)) for a in range(5)]
    acc = [None] * H
    for i, ii, a in row_pairs():
        term = x[ii] * w[a]
        acc[i] = term if acc[i] is None else acc[i] + term
    return acc


def plus(a, b):
    return [u + v for u, v in zip(a, b)]


def convolve(column, weights, cols, kept, put):
    x13 = plus(column(1), column(3))
    x02 = plus(column(0), column(2))
    m1 = over_rows(x13, weights, 1, cols)
    m2 = over_rows(x02, weights, 2, cols)
    m0 = over_rows(plus(x02, x13), weights, 0, cols)
    for i, v in enumerate(plus(m0, m1) + plus(m0, m2)):
        kept[i] = v
    for first, left, right in ((3, 2, 0), (6, 0, 2)):
        both = over_rows(plus(column(left), column(left + 1)), weights, first, cols)
        for k, j in ((0, left + 1), (1, left)):
            own = over_rows(column(j), weights, first + 1 + k, cols)
            for i in range(H):
                put(i, right + k, kept[k * H + i] + (both[i] + own[i]))


def correlate(target, left, right):
    def add(m, y, x):
        acc = [None] * 5
        for i, ii, a in row_pairs():
            term = y[i] * x[ii]
            acc[a] = term if acc[a] is None else acc[a] + term
        for a in range(5):
            target[a * 9 + m] += fold(acc[a])

    y02, x13 = plus(left(0), left(2)), plus(right(1), right(3))
    add(1, y02, x13)
    y13, x02 = plus(left(1), left(3)), plus(right(0), right(2))
    add(2, y13, x02)
    add(0, plus(y02, y13), plus(x02, x13))
    for first, j, k in ((3, 0, 2), (6, 2, 0)):
        add(first, plus(left(j), left(j + 1)), plus(right(k), right(k + 1)))
        add(first + 1, left(j), right(k + 1))
        add(first + 2, left(j + 1), right(k))


def column_of(ref, base, cols):
    return lambda j: [ref[pl.ds(base + 2 * (i * W + j), 2), :, cols] for i in range(H)]


def row_sums(target, first, source, cols):
    for t in range(source.shape[0]):
        target[first + t : first + t + 1, cols] = row_sum(source[t])


def kernel(
    f_hbm, q_hbm, we_hbm, wp_hbm, wr_hbm, wx_hbm, wd_hbm, ga1_hbm, bi1_hbm, ga2_hbm, bi2_hbm, bx_hbm, br_hbm, ga3_hbm, bi3_hbm,
    combine_hbm, units,
    f_in, q_in, o_panel,
    we_in, wp_in, wr_in, wx_in, wd_in, ga1_in, bi1_in, ga2_in, bi2_in, bx_in, br_in, ga3_in, bi3_in,
    copy_sems, stage, wide_stage,
    f_rows, q_rows, p_rows, f3, ft, pg3, qpt, qa,
    e_ref, a1, dv, q2, act_hi, act_lo,
    gathered, we, wp, wr, wx, we_b, ws_b, wp_b, wd, wt, par, parts, combine, acc45, acc24, cov_we, kept,
    pool, gates, spread, vec, sums, gp_panel, misc, g_panel,
    near, far, near2, far2,
    g_first, g_second, g_third,
    p_first, p_parts, p_second, p_third,
    m_first, m_parts, m_second, m_third,
    e_first, e_parts, e_second, e_third,
    w_sems, v_sems, g_sems, s_sems,
):
    third = ROWS // 3
    fetch_f = []
    for i in range(3):
        at = pl.ds(i * third, third)
        fetch_f.append(pltpu.make_async_copy(f_hbm.at[:, at], f_in.at[:, at], copy_sems.at[16 + i]))
        fetch_f[i].start()
    small_copies = [
        pltpu.make_async_copy(source, target, copy_sems.at[2 + i])
        for i, (source, target) in enumerate((
            (we_hbm, we_in), (wp_hbm, wp_in), (wr_hbm, wr_in), (wx_hbm, wx_in), (wd_hbm, wd_in),
            (ga1_hbm, ga1_in), (bi1_hbm, bi1_in), (ga2_hbm, ga2_in), (bi2_hbm, bi2_in), (bx_hbm, bx_in),
            (br_hbm, br_in), (ga3_hbm, ga3_in), (bi3_hbm, bi3_in), (combine_hbm, combine),
        ))
    ]
    for copy in small_copies:
        copy.start()
    fetch_q = pltpu.make_async_copy(q_hbm, q_in, copy_sems.at[0])
    fetch_q.start()
    x, y, c, z = place()
    column, plane = column_peers(), plane_peers()
    barrier = pltpu.get_barrier_semaphore()
    for _, device in column[1] + plane[1]:
        pl.semaphore_signal(barrier, inc=1, device_id=device, device_id_type=MESH)

    sum2a = Vector(column, plane, near2.at[0], far2.at[0], v_sems.at[0])
    sum2b = Vector(column, plane, near2.at[1], far2.at[1], v_sems.at[1])
    sum3 = Vector(column, plane, near2.at[2], far2.at[2], v_sems.at[2])
    sum4 = Vector(column, plane, near.at[0], far.at[0], v_sems.at[3])
    sum5 = Vector(column, plane, near.at[1], far.at[1], v_sems.at[4])
    vectors = [sum2a, sum2b, sum3, sum4, sum5]
    reduce_g = Square(column, plane, g_panel, g_first, g_second, g_third, g_sems)
    whole = [(0, WIDE)]
    reduce_p = Panel(column, plane, whole, gp_panel, p_first, p_parts, p_second, p_third, s_sems.at[0])
    reduce_m = Panel(column, plane, whole, misc, m_first, m_parts, m_second, m_third, s_sems.at[1])
    early_late = [(0, 2 * GROUP), (2 * GROUP, WIDE)]
    reduce_e = Panel(column, plane, early_late, gp_panel, e_first, e_parts, e_second, e_third, s_sems.at[2])

    ones = jnp.where(lax.broadcasted_iota(jnp.int32, (16, third), 0) == 0, 1.0, 0.0)
    gram = None
    for i in range(3):
        fetch_f[i].wait()
        at = slice(i * third, (i + 1) * third)
        hi, lo = split(jnp.concatenate([f_in[:, at], ones], axis=0))
        both = jnp.concatenate([hi, lo], axis=0)
        part = mm_nt(both, both)
        gram = part if gram is None else gram + part
    gram = gram[0:128, 0:128] + (gram[0:128, 128:256] + gram[128:256, 0:128]) + gram[128:256, 128:256]
    g_panel[...] = gram.reshape(8, 16, LANE)
    pl.semaphore_wait(barrier, 22)
    reduce_g.start()

    sections = ((0, AT_DEPTH), (AT_DEPTH, AT_PROJECT), (AT_PROJECT, PANEL))
    odd = lax.rem(z, 2) == 1

    across = [(lax.rem(z + k, 4), {"chan": lax.rem(z + k, 4)}) for k in (2, 1, 3)]

    def halves(s):
        lo, hi = sections[s]
        size = (hi - lo) // 2
        return size, pl.ds(pl.multiple_of(lo + c * size, 8), size), pl.ds(lo, size)

    def send_section(s):
        lo, hi = sections[s]
        rest = gathered[z, lo:hi, LANE:GROUP]
        gathered[z, lo:hi, LANE:GROUP] = jnp.where(odd, pltpu.roll(rest, 64, 1), rest)
        size, rows, _ = halves(s)
        for _, device in across:
            pltpu.make_async_remote_copy(
                src_ref=gathered.at[z, rows],
                dst_ref=gathered.at[z, rows],
                send_sem=w_sems.at[0, s],
                recv_sem=w_sems.at[1, s],
                device_id=device,
                device_id_type=MESH,
            ).start()

    def forward_section(s):
        size, rows, some = halves(s)
        drain(gathered.at[pl.ds(0, 3), some], w_sems.at[1, s])
        for other, _ in across:
            pltpu.make_async_remote_copy(
                src_ref=gathered.at[other, rows],
                dst_ref=gathered.at[other, rows],
                send_sem=w_sems.at[0, s],
                recv_sem=w_sems.at[2, s],
                device_id=(x * 8 + y * 2 + 1 - c, z),
                device_id_type=MESH,
            ).start()

    def section(s):
        size, rows, some = halves(s)
        drain(gathered.at[pl.ds(0, 3), some], w_sems.at[2, s])

    def close_section(s):
        size, rows, some = halves(s)
        for _ in range(2):
            drain(gathered.at[pl.ds(0, 3), some], w_sems.at[0, s])

    def assembled(lo, rows):
        parts = [gathered[k, lo : lo + rows, 0:LANE] for k in range(4)]
        for k in (0, 2):
            parts.append(gathered[k, lo : lo + rows, LANE:GROUP] + gathered[k + 1, lo : lo + rows, LANE:GROUP])
        return jnp.concatenate(parts, axis=1)

    for copy in small_copies:
        copy.wait()
    gathered[z] = jnp.zeros((PANEL, GROUP), F32)
    wide_stage[...] = jnp.zeros_like(wide_stage)
    wide_stage[0:OWN, 0:D] = we_in[...]
    gathered[z, 0:D, :] = wide_stage[...].T[0:D]
    send_section(0)
    for a in range(5):
        gathered[z, AT_DEPTH + 5 * a : AT_DEPTH + 5 * a + 5, 0:OWN] = wd_in[a]
    for i, row in enumerate((ga1_in, bi1_in, ga2_in, bi2_in, bx_in)):
        gathered[z, AT_VECS + i : AT_VECS + i + 1, 0:OWN] = row[...]
    send_section(1)
    wide_stage[0:OWN, 0:D] = wp_in[...]
    gathered[z, AT_PROJECT : AT_PROJECT + D, :] = wide_stage[...].T[0:D]
    gathered[z, AT_REDUCE : AT_REDUCE + SQZ, 0:OWN] = wr_in[...]
    gathered[z, AT_EXCITE : AT_EXCITE + SQZ, 0:OWN] = wx_in[...]
    send_section(2)

    tail = jnp.where(lax.broadcasted_iota(jnp.int32, (16, LANE), 0) == 0, 1.0, 0.0)

    def rows_of(source, tail, target):
        @pl.loop(0, BLOCKS)
        def _(b):
            for i in range(3):
                v = source[:, pl.ds(pl.multiple_of(b * CHUNK + i * LANE, LANE), LANE)]
                stage[i * LANE : (i + 1) * LANE, :] = jnp.concatenate([v, tail], axis=0).T
            for cell in range(CELLS):
                v = stage[pl.ds(cell, BLOCK, stride=CELLS), :]
                target[pl.ds((b * CELLS + cell) * 2, 2)] = v.reshape(2, 8, LANE)

    rows_of(f_in, tail, f_rows)

    @rloop("ft", 18)
    def _(i):
        v = f_rows[pl.ds(i * 16, 16)].reshape(128, LANE)
        rows = pl.ds(pl.multiple_of(i * 128, 128), 128)
        hi, lo = split(v)
        f3[rows, 0:128] = hi
        f3[rows, 128:256] = hi
        f3[rows, 256:384] = lo
        hi, lo = split(v.T)
        ft[0:128, rows] = hi
        ft[128:256, rows] = lo

    def parts_of(source, row):
        @pl.loop(0, 18)
        def _(i):
            hi, lo = split(source[pl.ds(i * 16, 16)].reshape(128, LANE).T)
            rows = pl.ds(pl.multiple_of(i * 128, 128), 128)
            qpt[row : row + 128, rows] = hi
            qpt[256 + row : 384 + row, rows] = lo

    reduce_g.middle()
    fetch_q.wait()
    rows_of(q_in, jnp.zeros((16, LANE), F32), q_rows)
    parts_of(q_rows, 0)
    sums[...] = jnp.zeros_like(sums)
    parts[...] = jnp.zeros_like(parts)
    qa[...] = jnp.zeros_like(qa)

    forward_section(0)
    forward_section(1)
    reduce_g.last()
    section(0)
    we[0:D, :] = assembled(0, D)
    we[D:128, :] = jnp.zeros((128 - D, WIDE), F32)
    hi, lo = split(we[...])
    we_b[0:128, :] = hi
    we_b[128:256, :] = lo

    @rloop("E", BLOCKS)
    def _(b):
        @pl.when(b == 3)
        def _():
            forward_section(2)

        rows = pl.ds(pl.multiple_of(b * CHUNK, CHUNK), CHUNK)
        for n in range(3):
            cols = slice(n * GROUP, (n + 1) * GROUP)
            r = mm(f3[rows, 0:256], we_b[:, cols]) + mm(f3[rows, 256:384], we_b[0:128, cols])
            e_ref[pl.ds(b * 48, 48), :, cols] = r.reshape(48, 8, GROUP)

    section(1)
    taps = assembled(AT_DEPTH, 32)
    for a in range(5):
        row = [taps[5 * a + k : 5 * a + k + 1] for k in range(5)]
        for m, v in enumerate(nine_weights(row)):
            wd[a * 9 + m : a * 9 + m + 1, :] = v
        for m, v in enumerate(nine_weights(row[::-1])):
            wt[(4 - a) * 9 + m : (4 - a) * 9 + m + 1, :] = v
    gain1, bias1, gain2, bias2, bx = [taps[TAPS + i : TAPS + i + 1] for i in range(5)]

    section(2)
    wp[0:D, :] = assembled(AT_PROJECT, D)
    wp[D:128, :] = jnp.zeros((128 - D, WIDE), F32)
    hi, lo = split(assembled(AT_REDUCE, 32))
    wr[...] = jnp.concatenate([hi, lo, hi, lo], axis=0)
    hi, lo = split(assembled(AT_EXCITE, 32))
    wx[...] = jnp.concatenate([hi, lo, hi, lo], axis=0)
    gram = reduce_g.finish() * (1.0 / TOTAL)
    f_mean_row = gram[D : D + 1, :]
    f_mean = gram[:, D : D + 1]
    cov = gram - f_mean * f_mean_row
    hi, lo = split(cov)
    cov_we[...] = mm(jnp.concatenate([hi, hi], axis=1), we_b[...]) + mm(jnp.concatenate([lo, lo], axis=1), we_b[...])
    mean1 = row_sum(we[...] * f_mean)
    inv1 = lax.rsqrt(row_sum(we[...] * cov_we[...]) + EPSILON)
    s1 = gain1 * inv1
    t1 = bias1 - mean1 * s1

    def put(i, row, lo=0, hi=WIDE):
        par[i, :, lo:hi] = jnp.broadcast_to(row, (8, hi - lo))

    put(0, 0.5 * s1)
    put(1, 0.5 * t1)

    def put_sums(first, second, g, low, size):
        sums[pl.ds(g - low, 1), :] = row_sum(first)
        sums[pl.ds(g - low + size, 1), :] = row_sum(second)

    @rloop("conv1", GROUPS)
    def _(g):
        cols = lanes_of(g)

        def block(b, carry):
            total, square = carry
            base = b * 48
            scale, shift = par[0, :, cols], par[1, :, cols]
            for cell in range(CELLS):
                at = pl.ds(base + 2 * cell, 2)
                h, th = half_gate(e_ref[at, :, cols], scale, shift)
                a1[at, :, cols] = h + h * th
            tally = [total, square]

            def put(i, j, v):
                dv[pl.ds(base + 2 * (i * W + j), 2), :, cols] = v
                tally[0] = tally[0] + fold(v)
                tally[1] = tally[1] + fold(v * v)

            convolve(column_of(a1, base, cols), wd, cols, kept, put)
            total, square = tally
            return total, square

        zero = jnp.zeros((8, LANE), F32)
        total, square = lax.fori_loop(0, BLOCKS, block, (zero, zero))
        put_sums(total, square, g, jnp.where(g < 4, 0, 4), jnp.where(g < 4, 4, 2))

        @pl.when(g == 3)
        def _():
            sum2a.start(sums[0:8, :])

        @pl.when(g == 5)
        def _():
            sum2b.start(sums[0:8, :])

    def wide(rows, first, count):
        return jnp.concatenate([rows[first + g : first + g + 1, :] for g in range(count)], axis=1)

    mean2, inv2 = [None] * 2, [None] * 2

    def second_norm(got, lo, hi):
        count = (hi - lo) // LANE
        mean = wide(got, 0, count) * (1.0 / TOTAL)
        inv = lax.rsqrt(wide(got, count, count) * (1.0 / TOTAL) - mean * mean + EPSILON)
        scale = par[7, 0:1, lo:hi] * inv
        put(2, 0.5 * scale, lo, hi)
        put(3, 0.5 * (par[8, 0:1, lo:hi] - mean * scale), lo, hi)
        put(9, mean, lo, hi)
        put(10, inv, lo, hi)
        put(11, scale, lo, hi)

    put(7, gain2)
    put(8, bias2)

    def one_products(g):
        cols = lanes_of(g)
        acc45[...] = jnp.zeros_like(acc45)
        acc24[...] = jnp.zeros_like(acc24)

        @pl.loop(0, BLOCKS)
        def _(b):
            for cell in range(CELLS):
                acc24[cell] += fold(a1[pl.ds(b * 48 + 2 * cell, 2), :, cols])
            correlate(acc45, column_of(dv, b * 48, cols), column_of(a1, b * 48, cols))

        row_sums(parts, IN_D, acc45, cols)
        row_sums(parts, IN_CELLS, acc24, cols)

    def one_activation(g):
        cols = lanes_of(g)

        @pl.loop(0, BLOCKS)
        def _(b):
            scale, shift = par[2, :, cols], par[3, :, cols]
            pooled = jnp.zeros((8, LANE), F32)
            for cell in range(CELLS):
                at = pl.ds(b * 48 + 2 * cell, 2)
                h, th = half_gate(dv[at, :, cols], scale, shift)
                q2[at, :, cols] = th
                act = h + h * th
                pooled = pooled + fold(act)
                hi, lo = split(act.reshape(16, LANE))
                rows = pl.ds(b * CHUNK + 16 * cell, 16)
                act_hi[rows, cols] = hi
                act_lo[rows, cols] = lo
            pool[b, :, cols] = pooled

    @pl.loop(0, 11)
    def _(step):
        @pl.when(step == 1)
        def _():
            sum2a.middle()

        @pl.when(step == 3)
        def _():
            sum2b.middle()

        @pl.when(step == 5)
        def _():
            second_norm(sum2a.finish(), 0, 4 * LANE)

        @pl.when(step == 9)
        def _():
            second_norm(sum2b.finish(), 4 * LANE, WIDE)

        @pl.when(step < 5)
        def _():
            one_products(step)

        @pl.when(step >= 5)
        def _():
            one_activation(step - 5)

    seg = lax.broadcasted_iota(jnp.int32, (8, LANE), 0)
    blk = lax.broadcasted_iota(jnp.int32, (8, LANE), 1)
    u0, u1, u2 = units[z, 0], units[z, 1], units[z, 2]
    lower = jnp.where(seg == 0, 0, jnp.where(seg == 1, u0, u0 + u1))
    length = jnp.where(seg == 0, u0, jnp.where(seg == 1, u1, u2))
    member = jnp.where((seg < 3) & (blk >= lower) & (blk < lower + length), 1.0, 0.0)
    per_count = jnp.where(seg < 3, 1.0 / (length * (BLOCK * CELLS)).astype(F32), 0.0)[:, 0:1]
    live = jnp.where(seg < 3, 1.0, 0.0)[:, 0:1]

    vec[...] = jnp.zeros((8, LANE), F32)
    vec[0:1, 0:SQZ] = br_in[...]
    pooled = jnp.zeros((8, WIDE), F32)
    for b in range(BLOCKS):
        pooled = pooled + member[:, b : b + 1] * row_sum(pool[b])
    plain_sums = pooled
    pooled = pooled * per_count
    pooled_pair = pair(pooled)
    reduced = pair_nt(pooled_pair, wr[0:64, :], 8, 32) + vec[0:1, 0:32]
    sig_r = sigmoid(reduced)
    squeezed = reduced * sig_r * live

    def quad(values):
        hi, lo = split(values)
        return jnp.concatenate([hi, hi, lo, lo], axis=1)

    gate = sigmoid(mm(quad(squeezed), wx[...]) + bx)

    def of_blocks(rows, b):
        return row_sum(member[:, b : b + 1] * rows)

    for b in range(BLOCKS):
        gates[b : b + 1, :] = of_blocks(gate, b)

    def project(b, carry):
        rows = slice(b * CHUNK, (b + 1) * CHUNK)
        hi, lo = split(wp[...] * gates[b : b + 1, :])
        wp_b[b, 0:128, :] = hi
        wp_b[b, 128:256, :] = lo
        r = mm_nt(act_hi[rows, :], wp_b[b])
        r = r[:, 0:128] + r[:, 128:256] + mm_nt(act_lo[rows, :], wp_b[b, 0:128, :])
        r = r.reshape(48, 8, LANE)
        q = q_rows[pl.ds(b * 48, 48)]
        p_rows[pl.ds(b * 48, 48)] = r
        return tuple(old + jnp.sum(new, axis=0) for old, new in zip(carry, (r, r * r, q, q * r)))

    zero = jnp.zeros((8, LANE), F32)
    four = (zero,) * 4
    for b in range(BLOCKS):
        four = project(b, four)
    for i in range(4):
        vec[i : i + 1, :] = row_sum(four[i])
    sum3.start(vec[...])

    parts_of(p_rows, 128)

    @rloop("qa", 3)
    def _(i):
        for b in (2 * i, 2 * i + 1):
            rows = pl.ds(pl.multiple_of(b * CHUNK, CHUNK), CHUNK)
            inside = [jnp.where((b >= low) & (b < high), 1.0, 0.0) for low, high in ((0, u0), (u0, u0 + u1), (u0 + u1, 6))]
            m = mm(qpt[:, rows], act_hi[rows, :])
            m = m[0:256] + m[256:512] + mm(qpt[0:256, rows], act_lo[rows, :])
            for k in range(3):
                qa[k] += m * inside[k]

        @pl.when(i == 1)
        def _():
            sum3.middle()

    @rloop("slope2", GROUPS)
    def _(g):
        cols = lanes_of(g)

        @pl.loop(0, BLOCKS)
        def _(b):
            scale, shift = par[2, :, cols], par[3, :, cols]
            for cell in range(CELLS):
                at = pl.ds(b * 48 + 2 * cell, 2)
                q2[at, :, cols] = twice_slope_of(dv[at, :, cols] * scale + shift, q2[at, :, cols])

    def one_slope(g):
        cols = lanes_of(g)

        @pl.loop(0, BLOCKS)
        def _(b):
            scale, shift = par[0, :, cols], par[1, :, cols]
            for cell in range(CELLS):
                at = pl.ds(b * 48 + 2 * cell, 2)
                e_ref[at, :, cols] = twice_slope_of(*half_gate(e_ref[at, :, cols], scale, shift))

    pl.loop(0, 2)(one_slope)
    got = sum3.finish() * (1.0 / TOTAL)
    vec[...] = jnp.zeros((8, LANE), F32)
    vec[0:1, 0:D] = ga3_in[...]
    vec[1:2, 0:D] = bi3_in[...]
    gain3, bias3 = vec[0:1, :], vec[1:2, :]
    mean3 = got[0:1]
    inv3 = lax.rsqrt(got[1:2] - mean3 * mean3 + EPSILON)
    b3 = got[2:3]
    g3 = (got[3:4] - mean3 * got[2:3]) * inv3
    o_panel[OUT_SMALL : OUT_SMALL + 1, 0:LANE] = g3 * TOTAL
    o_panel[OUT_SMALL + 1 : OUT_SMALL + 2, 0:LANE] = b3 * TOTAL
    s3 = gain3 * inv3
    t3 = bias3 - mean3 * s3
    pg_p = -s3 * inv3 * g3
    pg_0 = -s3 * b3 - pg_p * mean3

    columns = jnp.concatenate([s3, pg_p, pg_0, jnp.zeros((5, LANE), F32)], axis=0).T
    by_q, by_p, by_1 = columns[:, 0:1], columns[:, 1:2], columns[:, 2:3]
    base = row_sum(wp[...] * by_1)
    w_q, w_p = wp[...] * by_q, wp[...] * by_p
    gate_grad = jnp.concatenate(
        [row_sum(w_q * qa[k, 0:128] + w_p * qa[k, 128:256]) + base * plain_sums[k : k + 1] for k in range(3)]
        + [jnp.zeros((5, WIDE), F32)],
        axis=0,
    )
    excite_in = gate_grad * gate * (1.0 - gate)
    reduced_grad = pair_nt(pair(excite_in), wx[0:64, :], 8, 32) * (sig_r * (1.0 + reduced * (1.0 - sig_r))) * live
    pooled_grad = mm(quad(reduced_grad), wr[...]) * per_count
    for b in range(BLOCKS):
        spread[b : b + 1, :] = 0.5 * of_blocks(pooled_grad, b)

    @rloop("pgs", BLOCKS)
    def _(b):
        at = pl.ds(b * 48, 48)
        hi, lo = split((q_rows[at] * (0.5 * s3) + (p_rows[at] * (0.5 * pg_p) + 0.5 * pg_0)).reshape(CHUNK, LANE))
        rows = pl.ds(pl.multiple_of(b * CHUNK, CHUNK), CHUNK)
        pg3[rows, 0:128] = hi
        pg3[rows, 128:256] = hi
        pg3[rows, 256:384] = lo

    def backward(i, carry):
        total, product = carry
        for b in (2 * i, 2 * i + 1):
            rows = pl.ds(pl.multiple_of(b * CHUNK, CHUNK), CHUNK)
            at = pl.ds(b * 48, 48)
            r = mm(pg3[rows, 0:256], wp_b[b]) + mm(pg3[rows, 256:384], wp_b[b, 0:128, :])
            r = (r.reshape(48, 8, WIDE) + spread[pl.ds(b, 1), :]) * q2[at]
            q2[at] = r
            total, product = total + jnp.sum(r, axis=0), product + jnp.sum(r * dv[at], axis=0)
        return total, product

    zero = jnp.zeros((8, WIDE), F32)
    total, product = lax.fori_loop(0, 3, backward, (zero, zero))
    total, product = row_sum(total), row_sum(product)
    for g in range(GROUPS):
        lanes = slice(g * LANE, (g + 1) * LANE)
        sums[g : g + 1, :] = total[:, lanes]
        sums[8 + g : 9 + g, :] = product[:, lanes]
    sum4.start(sums[...])

    gp = jnp.zeros((128, WIDE), F32)
    for k in range(3):
        gp = gp + gate[k : k + 1] * (by_q * qa[k, 0:128] + by_p * qa[k, 128:256] + by_1 * plain_sums[k : k + 1])
    gp_panel[...] = gp.reshape(16, 8, WIDE)
    g_excite = exact(squeezed, excite_in, (0, 0))
    gp_panel[14, 0:1, :] = row_sum(excite_in)
    gp_panel[15, 0:1, :] = jnp.zeros((1, WIDE), F32)
    for k in range(4):
        gp_panel[15, 0:1, k * LANE : k * LANE + 32] = row_sum(reduced_grad)
    for i in range(IN_THIRD, SQZ):
        gp_panel[14, 1 + i - IN_THIRD : 2 + i - IN_THIRD, :] = g_excite[i : i + 1]
    reduce_p.start(0)

    parts[IN_R : IN_R + 32, :] = exact(reduced_grad, pooled, (0, 0))
    parts[IN_X : IN_X + 32, :] = g_excite

    @rloop("tq", GROUPS)
    def _(g):
        cols = lanes_of(g)
        acc45[...] = jnp.zeros_like(acc45)

        @pl.loop(0, BLOCKS)
        def _(b):
            correlate(acc45, column_of(q2, b * 48, cols), column_of(a1, b * 48, cols))

        @pl.when(g >= 2)
        def _():
            one_slope(g)

        row_sums(parts, 0, acc45, cols)

        @pl.when(g == 2)
        def _():
            sum4.middle()

    def own_lanes(rows):
        first = rows[:, 0:LANE]
        rest = rows[:, LANE:GROUP]
        return first, jnp.where(odd, pltpu.roll(rest, 64, 1), rest)

    def own_wide(rows):
        first = jnp.zeros((rows.shape[0], LANE), F32)
        rest = jnp.zeros((rows.shape[0], LANE), F32)
        for k in range(4):
            first = jnp.where(z == k, rows[:, k * LANE : (k + 1) * LANE], first)
        for k in range(2):
            rest = jnp.where(z // 2 == k, rows[:, (4 + k) * LANE : (5 + k) * LANE], rest)
        return jnp.concatenate([first, rest], axis=1)

    def emit(row, values):
        first, rest = own_lanes(values)
        o_panel[row : row + values.shape[0], 0:LANE] = first
        o_panel[row : row + values.shape[0], LANE:GROUP] = rest

    def emit_vector(i, row):
        emit(OUT_VECS + i, own_wide(row))

    one_products(5)

    hi, lo = split(parts[...])
    picks = combine[...].astype(BF16)
    misc[...] = (mm(picks, hi) + mm(picks, lo)).reshape(16, 8, WIDE)
    reduce_m.start(0)

    got = sum4.finish()
    mean2, inv2, s2 = [par[i, 0:1, :] for i in (9, 10, 11)]
    b2 = wide(got, 0, GROUPS)
    g2 = (wide(got, 8, GROUPS) - mean2 * b2) * inv2
    c3 = -s2 * inv2 * g2 * (1.0 / TOTAL)
    c2 = -s2 * b2 * (1.0 / TOTAL) - c3 * mean2
    shift3 = -inv2 * g2 * (1.0 / TOTAL)
    put(4, -b2 * (1.0 / TOTAL) - shift3 * mean2)
    put(5, shift3)
    wt[...] = wt[...] * (0.5 * s2)
    emit_vector(2, g2)
    emit_vector(3, b2)

    @rloop("conv2", GROUPS)
    def _(g):
        @pl.when(g == 1)
        def _():
            reduce_p.middle()
            reduce_p.sent()

        cols = lanes_of(g)

        @pl.loop(0, BLOCKS)
        def _(b):
            base = b * 48
            k2, k3 = par[4, :, cols], par[5, :, cols]

            for cell in range(CELLS):
                at = pl.ds(base + 2 * cell, 2)
                q2[at, :, cols] = q2[at, :, cols] + (dv[at, :, cols] * k3 + k2)

            def put(i, j, v):
                at = pl.ds(base + 2 * (i * W + j), 2)
                hi, lo = split((v * e_ref[at, :, cols]).reshape(16, LANE))
                rows = pl.ds(b * CHUNK + 16 * (i * W + j), 16)
                act_hi[rows, cols] = hi
                act_lo[rows, cols] = lo

            convolve(column_of(q2, base, cols), wt, cols, kept, put)

        @pl.when(lax.rem(g, 2) == 1)
        def _():
            n = g // 2
            cols = pl.ds(pl.multiple_of(n * GROUP, GROUP), GROUP)
            m = mm(ft[...], act_hi[:, cols])
            m = m[0:128] + m[128:256] + mm(ft[0:128, :], act_lo[:, cols])
            gp_panel[:, :, cols] = m.reshape(16, 8, GROUP)

            @pl.when(g == 5)
            def _():
                reduce_e.start(1)

            product = row_sum(m * we[:, cols])
            for half in range(2):
                lanes = slice(half * LANE, (half + 1) * LANE)
                sums[pl.ds(g - 1 + half, 1), :] = m[D : D + 1, lanes]
                sums[pl.ds(g + 7 + half, 1), :] = product[:, lanes]

            @pl.when(g == 3)
            def _():
                reduce_e.start(0)

    sum5.start(sums[...])
    reduce_p.last()
    reduce_m.middle()

    hi, lo = split(we[...] * s1)
    ws_b[0:128, :] = hi
    ws_b[128:256, :] = lo

    @rloop("ig", 3)
    def _(i):
        rows = pl.ds(pl.multiple_of(i * 2 * CHUNK, 2 * CHUNK), 2 * CHUNK)
        r = mm_nt(act_hi[rows, :], ws_b[...])
        r = r[:, 0:128] + r[:, 128:256] + mm_nt(act_lo[rows, :], ws_b[0:128, :])
        q_rows[pl.ds(i * 96, 96)] += r.reshape(96, 8, LANE)

    sum5.middle()

    def write(target, b, rows_of_cell):
        for cell in range(CELLS):
            stage[pl.ds(cell, BLOCK, stride=CELLS), :] = rows_of_cell(pl.ds(b * 48 + 2 * cell, 2)).reshape(16, LANE)
        for i in range(3):
            at = pl.ds(pl.multiple_of(b * CHUNK + i * LANE, LANE), LANE)
            target[:, at] = stage[i * LANE : (i + 1) * LANE, :].T[0:D]

    reduce_m.last()
    reduce_e.middle()

    @rloop("out", BLOCKS)
    def _(b):
        write(f_in, b, lambda at: f_rows[at] + (p_rows[at] * s3 + t3))

    reduce_e.last()
    got = sum5.finish()
    b1 = wide(got, 0, GROUPS)
    g1 = (wide(got, 8, GROUPS) - mean1 * b1) * inv1
    k3 = -s1 * inv1 * g1 * (1.0 / TOTAL)
    k2 = -s1 * b1 * (1.0 / TOTAL) - k3 * mean1
    left = jnp.where(lax.broadcasted_iota(jnp.int32, (128, WIDE), 0) == D, k2, we[...] * k3)
    mix = pair_nt(pair(left), we_b[...], 128, 128)
    mix_hi, mix_lo = split(mix)
    mix_all = jnp.concatenate([mix_hi, mix_lo], axis=0)

    @rloop("ig2", BLOCKS)
    def _(b):
        rows = pl.ds(pl.multiple_of(b * CHUNK, CHUNK), CHUNK)
        r = mm(f3[rows, 0:256], mix_all) + mm(f3[rows, 256:384], mix_hi)
        q_rows[pl.ds(b * 48, 48)] += r.reshape(48, 8, LANE)
        write(q_in, b, lambda at: q_rows[at])

    emit_vector(0, g1)
    emit_vector(1, b1)
    emit(OUT_PROJECT, reduce_p.finish())
    total_m = reduce_m.finish()
    emit(OUT_MISC, total_m)
    by = [own_wide(v) for v in (s2, c2, c3)]
    taps_grad = total_m[0:TAPS] * by[0] + total_m[AT_DD : AT_DD + TAPS] * by[2] + total_m[AT_PLAIN : AT_PLAIN + TAPS] * by[1]
    emit(OUT_MISC, taps_grad)
    scale_own = own_wide(s1)
    away = f_mean * own_wide(b1) + own_wide(cov_we[...]) * own_wide(inv1 * g1)
    for s in range(3):
        close_section(s)
    reduce_m.sent()
    reduce_e.sent()
    for item in vectors + [reduce_g, reduce_p, reduce_m, reduce_e]:
        item.close()
    emit(0, scale_own * (reduce_e.finish() - away))


def finish_kernel(
    out_in, igrad_in, panel,
    out, igrad, expand, gain1, bias1, depth, gain2, bias2, reduce, b_reduce, excite, b_excite, project, gain3, bias3,
    sems,
):
    large = [pltpu.make_async_copy(out_in, out, sems.at[0]), pltpu.make_async_copy(igrad_in, igrad, sems.at[1])]
    for copy in large:
        copy.start()
    expand[...] = panel[0:LANE, :].T[0:OWN, 0:D]
    project[...] = panel[OUT_PROJECT : OUT_PROJECT + LANE, :].T[0:OWN, 0:D]
    for a in range(5):
        depth[a] = panel[OUT_MISC + 5 * a : OUT_MISC + 5 * a + 5, 0:OWN]
    reduce[...] = panel[OUT_MISC + AT_R : OUT_MISC + AT_R + SQZ, 0:OWN]
    excite[0:IN_THIRD, :] = panel[OUT_MISC + AT_X : OUT_MISC + 128, 0:OWN]
    excite[IN_THIRD:SQZ, :] = panel[OUT_PROJECT + D + 1 : OUT_PROJECT + D + 1 + SQZ - IN_THIRD, 0:OWN]
    b_excite[...] = panel[OUT_PROJECT + D : OUT_PROJECT + D + 1, 0:OWN]
    b_reduce[...] = panel[OUT_PROJECT + D + 8 : OUT_PROJECT + D + 9, 0:SQZ]
    for i, ref in enumerate((gain1, bias1, gain2, bias2)):
        ref[...] = panel[OUT_VECS + i : OUT_VECS + i + 1, 0:OWN]
    gain3[...] = panel[OUT_SMALL : OUT_SMALL + 1, 0:D]
    bias3[...] = panel[OUT_SMALL + 1 : OUT_SMALL + 2, 0:D]
    for copy in large:
        copy.wait()


def body(
    features, seg_units, w_expand, gain_one, bias_one, w_depth, gain_two, bias_two,
    w_reduce, b_reduce, w_excite, b_excite, w_project, gain_three, bias_three, cotangent,
):
    vm = pl.BlockSpec(memory_space=pltpu.VMEM)
    anywhere = pl.BlockSpec(memory_space=pl.ANY)
    big = pltpu.VMEM((288, 8, WIDE), F32)
    rows128 = pltpu.VMEM((288, 8, LANE), F32)
    half = pltpu.VMEM((ROWS, WIDE), BF16)

    def f32(*shape):
        return pltpu.VMEM(shape, F32)

    def b16(*shape):
        return pltpu.VMEM(shape, BF16)

    def shape(*dims):
        return jax.ShapeDtypeStruct(dims, F32)

    def row(vector):
        return vector.reshape(1, vector.shape[0])

    dma = pltpu.SemaphoreType.DMA
    slots = [f32(16, 8, WIDE), f32(4, 8, GROUP), f32(8, 8, GROUP), f32(16, 8, GROUP)]
    out, igrad, panel = pl.pallas_call(
        kernel,
        out_shape=(f32(D, ROWS), f32(D, ROWS), f32(RESULTS, GROUP)),
        in_specs=[anywhere] * 16 + [pl.BlockSpec(memory_space=pltpu.SMEM)],
        out_specs=(vm,) * 3,
        scratch_shapes=[
            f32(OWN, D), f32(OWN, D), f32(SQZ, OWN), f32(SQZ, OWN), f32(5, 5, OWN),
            f32(1, OWN), f32(1, OWN), f32(1, OWN), f32(1, OWN), f32(1, OWN), f32(1, SQZ), f32(1, D), f32(1, D),
            dma((19,)), f32(CHUNK, LANE), f32(GROUP, LANE),
            rows128, rows128, rows128, b16(ROWS, 384), b16(256, ROWS), b16(ROWS, 384), b16(512, ROWS), f32(3, 256, WIDE),
            big, big, big, big, half, half,
            f32(4, PANEL, GROUP), f32(128, WIDE), f32(128, WIDE), b16(128, WIDE), b16(128, WIDE),
            b16(256, WIDE), b16(256, WIDE), b16(BLOCKS, 256, WIDE), f32(48, WIDE), f32(48, WIDE), f32(12, 8, WIDE),
            f32(SUMS, WIDE), f32(128, SUMS), f32(45, 8, LANE), f32(CELLS, 8, LANE), f32(128, WIDE), f32(2 * H, 2, 8, LANE),
            f32(BLOCKS, 8, WIDE), f32(8, WIDE), f32(8, WIDE), f32(8, LANE), f32(16, LANE),
            f32(16, 8, WIDE), f32(16, 8, WIDE), f32(8, 16, LANE),
            f32(2, 8, 16, LANE), f32(2, 16, 16, LANE), f32(3, 8, 8, LANE), f32(3, 16, 8, LANE),
            f32(8, 16, LANE), f32(16, 16, LANE), f32(8, 16, LANE),
        ]
        + slots * 3
        + [dma((3, 3)), dma((5, 4)), dma((6,)), dma((3, 8))],
        compiler_params=pltpu.CompilerParams(
            collective_id=0, has_side_effects=True, vmem_limit_bytes=61 * 1024 * 1024 + 256 * 1024
        ),
    )(
        features.T, cotangent.T, w_expand.T, w_project, w_reduce.T, w_excite, w_depth,
        row(gain_one), row(bias_one), row(gain_two), row(bias_two), row(b_excite), row(b_reduce), row(gain_three), row(bias_three),
        jnp.asarray(combination()), seg_units,
    )

    small = [
        (OWN, D), (1, OWN), (1, OWN), (5, 5, OWN), (1, OWN), (1, OWN),
        (SQZ, OWN), (1, SQZ), (SQZ, OWN), (1, OWN), (OWN, D), (1, D), (1, D),
    ]
    results = pl.pallas_call(
        finish_kernel,
        out_shape=(shape(D, ROWS), shape(D, ROWS)) + tuple(shape(*dims) for dims in small),
        in_specs=[vm] * 3,
        out_specs=(anywhere, anywhere) + (vm,) * 13,
        scratch_shapes=[dma((2,))],
        compiler_params=pltpu.CompilerParams(vmem_limit_bytes=8 * 1024 * 1024),
    )(*(pltpu.with_memory_space_constraint(v, pltpu.VMEM) for v in (out, igrad, panel)))
    (out, igrad, expand, gain1, bias1, depth, gain2, bias2, reduce, small_b, excite, b_x, project, gain3, bias3) = results
    return (
        out.T, igrad.T, expand.T, gain1[0], bias1[0], depth, gain2[0], bias2[0],
        reduce.T, small_b[0], excite, b_x[0], project, gain3[0], bias3[0],
    )


def solution(mesh):
    placed = (
        P(("dp", "chan"), None),
        P("dp", None),
        P(None, "chan"),
        P("chan"),
        P("chan"),
        P(None, None, "chan"),
        P("chan"),
        P("chan"),
        P("chan", None),
        P(),
        P(None, "chan"),
        P("chan"),
        P("chan", None),
        P(),
        P(),
        P(("dp", "chan"), None),
    )
    return jax.shard_map(
        body,
        mesh=mesh,
        in_specs=placed,
        out_specs=(
            P(("dp", "chan"), None),
            P(("dp", "chan"), None),
            P(None, "chan"),
            P("chan"),
            P("chan"),
            P(None, None, "chan"),
            P("chan"),
            P("chan"),
            P("chan", None),
            P(),
            P(None, "chan"),
            P("chan"),
            P("chan", None),
            P(),
            P(),
        ),
        check_vma=False,
    )
```

```python
import jax
import jax.numpy as jnp
import numpy as np
from jax import lax
from jax.experimental import pallas as pl
from jax.experimental.pallas import tpu as pltpu
from jax.sharding import PartitionSpec as P

MESH = pl.DeviceIdType.MESH
F32 = jnp.float32
BF16 = jnp.bfloat16
EPSILON = 0.001
PRECISE = lax.Precision.HIGHEST
D = 112
SQZ = 28
EXP = 672
H, W, CELLS = 6, 4, 24
TAPS = 25
BLOCK, BLOCKS = 16, 6
ROWS = 2304
CHUNK = BLOCK * CELLS
LANE = 128
WIDE = 768
GROUPS = WIDE // LANE
TOTAL = 294912.0
OWN = 168
REST = OWN - LANE

AT_EXPAND, AT_DEPTH, AT_VECS, AT_PROJECT, AT_REDUCE, AT_EXCITE, PANEL = 0, 112, 137, 144, 256, 288, 320
AT_DD, AT_PLAIN, AT_R, AT_X = TAPS, 2 * TAPS, 3 * TAPS, 3 * TAPS + SQZ
IN_THIRD = 128 - AT_X
OUT_PROJECT, OUT_MISC, OUT_VECS, OUT_SMALL, RESULTS = 128, 256, 384, 392, 400
GROUP = 2 * LANE


REPS = {}


def rep(name):
    count = REPS.get(name, 1)

    def run(fn):
        if count == 1:
            fn()
        else:
            lax.fori_loop(0, count, lambda i, carry: (fn(), carry)[1], 0)

    return run


def rloop(name, size):
    count = REPS.get(name, 1)

    def run(fn):
        if count == 1:
            pl.loop(0, size)(fn)
        else:
            pl.loop(0, size * count)(lambda i: fn(lax.rem(i, size)))

    return run


def split(values):
    high = values.astype(BF16)
    return high, (values - high.astype(F32)).astype(BF16)


def mm(a, b):
    return lax.dot_general(a, b, (((1,), (0,)), ((), ())), preferred_element_type=F32)


def mm_nt(a, b):
    return lax.dot_general(a, b, (((1,), (1,)), ((), ())), preferred_element_type=F32)


def exact(a, b, dims):
    return lax.dot_general(a, b, ((dims[:1], dims[1:]), ((), ())), precision=PRECISE, preferred_element_type=F32)


def pair(values):
    return jnp.concatenate(split(values), axis=0)


def pair_nt(a, b, rows, cols):
    r = mm_nt(a, b)
    return (r[0:rows, 0:cols] + r[rows:, cols:]) + (r[0:rows, cols:] + r[rows:, 0:cols])


def place():
    dp = lax.axis_index("dp")
    z = lax.axis_index("chan")
    return dp // 8, lax.rem(dp // 2, 4), lax.rem(dp, 2), z


def ring(step):
    return min(step, 4 - step)


def column_peers():
    x, y, c, z = place()
    moves = [(dz, dc) for dz in range(4) for dc in range(2) if dz or dc]
    moves.sort(key=lambda m: -10 * ring(m[0]) - m[1])
    base = x * 8 + y * 2
    zs = [lax.rem(z + dz, 4) for dz in range(4)]
    cs = [c, 1 - c]
    return z * 2 + c, [(zs[dz] * 2 + cs[dc], (base + cs[dc], zs[dz])) for dz, dc in moves]


def plane_peers():
    x, y, c, z = place()
    moves = [(dx, dy) for dx in range(4) for dy in range(4) if dx or dy]
    moves.sort(key=lambda m: -ring(m[0]) - ring(m[1]))
    xs = [lax.rem(x + dx, 4) for dx in range(4)]
    ys = [lax.rem(y + dy, 4) for dy in range(4)]
    peers = []
    for dx, dy in moves:
        rank = xs[dx] * 4 + ys[dy]
        peers.append((rank, (rank * 2 + c, z)))
    return x * 4 + y, peers


def push(sources, slots, mine, peers, send, recv):
    for rank, device in peers:
        pltpu.make_async_remote_copy(
            src_ref=sources(rank),
            dst_ref=slots.at[mine],
            send_sem=send,
            recv_sem=recv,
            device_id=device,
            device_id_type=MESH,
        ).start()


def drain(view, sem):
    pltpu.make_async_copy(view, view, sem).wait()


def add_slots(slots, count):
    total = slots[0]
    for k in range(1, count):
        total = total + slots[k]
    return total


class Vector:
    def __init__(self, column, plane, near, far, sems):
        self.column, self.plane, self.near, self.far, self.sems = column, plane, near, far, sems

    def start(self, value):
        mine, peers = self.column
        self.near[mine] = value
        push(lambda rank: self.near.at[mine], self.near, mine, peers, self.sems.at[0], self.sems.at[1])

    def middle(self):
        drain(self.near.at[pl.ds(0, 7)], self.sems.at[1])
        mine, peers = self.plane
        self.far[mine] = add_slots(self.near, 8)
        push(lambda rank: self.far.at[mine], self.far, mine, peers, self.sems.at[2], self.sems.at[3])

    def finish(self):
        drain(self.far.at[pl.ds(0, 15)], self.sems.at[3])
        return add_slots(self.far, 16)

    def close(self):
        drain(self.near.at[pl.ds(0, 7)], self.sems.at[0])
        drain(self.far.at[pl.ds(0, 15)], self.sems.at[2])


class Square:
    def __init__(self, column, plane, source, first, second, third, sems):
        self.column, self.plane = column, plane
        self.source, self.first, self.second, self.third, self.sems = source, first, second, third, sems

    def start(self):
        mine, peers = self.column
        self.first[mine] = self.source[mine]
        push(lambda rank: self.source.at[rank], self.first, mine, peers, self.sems.at[0], self.sems.at[1])

    def middle(self):
        drain(self.first.at[pl.ds(0, 7)], self.sems.at[1])
        mine, peers = self.plane
        self.second[mine] = add_slots(self.first, 8)
        push(lambda rank: self.second.at[mine], self.second, mine, peers, self.sems.at[2], self.sems.at[3])

    def last(self):
        drain(self.second.at[pl.ds(0, 15)], self.sems.at[3])
        mine, peers = self.column
        self.third[mine] = add_slots(self.second, 16)
        push(lambda rank: self.third.at[mine], self.third, mine, peers, self.sems.at[4], self.sems.at[5])

    def finish(self):
        drain(self.third.at[pl.ds(0, 7)], self.sems.at[5])
        return self.third[...].reshape(128, LANE)

    def close(self):
        drain(self.first.at[pl.ds(0, 7)], self.sems.at[0])
        drain(self.second.at[pl.ds(0, 15)], self.sems.at[2])
        drain(self.third.at[pl.ds(0, 7)], self.sems.at[4])


class Panel:
    def __init__(self, column, plane, ranges, source, first, parts, second, third, sems):
        self.column, self.plane, self.ranges = column, plane, ranges
        self.source, self.first, self.parts, self.second, self.third, self.sems = source, first, parts, second, third, sems

    def start(self, index):
        mine, peers = self.plane
        lo, hi = self.ranges[index]
        lanes = pl.ds(lo, hi - lo)
        self.first[mine, :, lo:hi] = self.source[mine, :, lo:hi]
        for rank, device in peers:
            pltpu.make_async_remote_copy(
                src_ref=self.source.at[rank, :, lanes],
                dst_ref=self.first.at[mine, :, lanes],
                send_sem=self.sems.at[0],
                recv_sem=self.sems.at[1 + index],
                device_id=device,
                device_id_type=MESH,
            ).start()

    def scattered(self, index, sem):
        lo, hi = self.ranges[index]
        drain(self.first.at[pl.ds(0, 15), :, pl.ds(lo, hi - lo)], self.sems.at[sem])

    def middle(self):
        for index in range(len(self.ranges)):
            self.scattered(index, 1 + index)
        total = add_slots(self.first, 16)
        mine, peers = self.column
        for z in range(4):
            self.parts[z, :, 0:LANE] = total[:, z * LANE : (z + 1) * LANE]
            rest = 4 + z // 2
            self.parts[z, :, LANE:GROUP] = total[:, rest * LANE : (rest + 1) * LANE]
        self.second[mine] = self.parts[mine // 2]
        push(lambda rank: self.parts.at[rank // 2], self.second, mine, peers, self.sems.at[4], self.sems.at[5])

    def last(self):
        drain(self.second.at[pl.ds(0, 7)], self.sems.at[5])
        mine, peers = self.plane
        self.third[mine] = add_slots(self.second, 8)
        push(lambda rank: self.third.at[mine], self.third, mine, peers, self.sems.at[6], self.sems.at[7])

    def finish(self):
        drain(self.third.at[pl.ds(0, 15)], self.sems.at[7])
        return self.third[...].reshape(128, GROUP)

    def sent(self):
        for index in range(len(self.ranges)):
            self.scattered(index, 0)

    def close(self):
        drain(self.second.at[pl.ds(0, 7)], self.sems.at[4])
        drain(self.third.at[pl.ds(0, 15)], self.sems.at[6])


def half_gate(values, scale, shift):
    h = values * scale + shift
    return h, jnp.tanh(h)


def twice_slope_of(h, th):
    return (1.0 + th) * (1.0 + (h - h * th))


def sigmoid(v):
    return 1.0 / (1.0 + jnp.exp(-v))


def lanes_of(g):
    return pl.ds(pl.multiple_of(g * LANE, LANE), LANE)


def fold(v):
    return v[0] + v[1]


def row_sum(v):
    return jnp.sum(v, axis=0, keepdims=True)


def row_pairs():
    return [(i, i + a - 2, a) for a in range(5) for i in range(H) if 0 <= i + a - 2 < H]


def nine_weights(w):
    m2, m1, w0, p1, p2 = w
    return [
        w0, p1 - w0, m1 - w0,
        p2 - w0, w0 - p1 - p2, (p1 - m1) + (w0 - p2),
        m2 - w0, (m1 - p1) + (w0 - m2), w0 - m1 - m2,
    ]


FIVE = (
    (0, 0, 0, 0, 0, 0, 1, -1, -1),
    (0, 0, 1, 0, 0, -1, 0, 1, -1),
    (1, -1, -1, -1, 1, 1, -1, 1, 1),
    (0, 1, 0, 0, -1, 1, 0, -1, 0),
    (0, 0, 0, 1, -1, -1, 0, 0, 0),
)
IN_D, IN_CELLS, IN_R, IN_X, SUMS = 48, 96, 120, 152, 192


def combination():
    c = np.zeros((128, SUMS), np.float32)
    for a in range(5):
        for k in range(5):
            t = 5 * a + k
            for m in range(9):
                c[t, 9 * a + m] = FIVE[k][m]
                c[AT_DD + t, IN_D + 9 * a + m] = FIVE[k][m]
            for i in range(H):
                for j in range(W):
                    ii, jj = i + a - 2, j + k - 2
                    if 0 <= ii < H and 0 <= jj < W:
                        c[AT_PLAIN + t, IN_CELLS + ii * W + jj] = 1.0
    for i in range(SQZ):
        c[AT_R + i, IN_R + i] = 1.0
    for i in range(IN_THIRD):
        c[AT_X + i, IN_X + i] = 1.0
    return c


def over_rows(x, weights, m, cols):
    w = [jnp.broadcast_to(weights[a * 9 + m : a * 9 + m + 1, cols], (8, LANE)) for a in range(5)]
    acc = [None] * H
    for i, ii, a in row_pairs():
        term = x[ii] * w[a]
        acc[i] = term if acc[i] is None else acc[i] + term
    return acc


def plus(a, b):
    return [u + v for u, v in zip(a, b)]


def convolve(column, weights, cols, kept, put):
    x13 = plus(column(1), column(3))
    x02 = plus(column(0), column(2))
    m1 = over_rows(x13, weights, 1, cols)
    m2 = over_rows(x02, weights, 2, cols)
    m0 = over_rows(plus(x02, x13), weights, 0, cols)
    for i, v in enumerate(plus(m0, m1) + plus(m0, m2)):
        kept[i] = v
    for first, left, right in ((3, 2, 0), (6, 0, 2)):
        both = over_rows(plus(column(left), column(left + 1)), weights, first, cols)
        for k, j in ((0, left + 1), (1, left)):
            own = over_rows(column(j), weights, first + 1 + k, cols)
            for i in range(H):
                put(i, right + k, kept[k * H + i] + (both[i] + own[i]))


def correlate(target, left, right):
    def add(m, y, x):
        acc = [None] * 5
        for i, ii, a in row_pairs():
            term = y[i] * x[ii]
            acc[a] = term if acc[a] is None else acc[a] + term
        for a in range(5):
            target[a * 9 + m] += fold(acc[a])

    y02, x13 = plus(left(0), left(2)), plus(right(1), right(3))
    add(1, y02, x13)
    y13, x02 = plus(left(1), left(3)), plus(right(0), right(2))
    add(2, y13, x02)
    add(0, plus(y02, y13), plus(x02, x13))
    for first, j, k in ((3, 0, 2), (6, 2, 0)):
        add(first, plus(left(j), left(j + 1)), plus(right(k), right(k + 1)))
        add(first + 1, left(j), right(k + 1))
        add(first + 2, left(j + 1), right(k))


def column_of(ref, base, cols):
    return lambda j: [ref[pl.ds(base + 2 * (i * W + j), 2), :, cols] for i in range(H)]


def row_sums(target, first, source, cols):
    for t in range(source.shape[0]):
        target[first + t : first + t + 1, cols] = row_sum(source[t])


def kernel(
    f_hbm, q_hbm, we_hbm, wp_hbm, wr_hbm, wx_hbm, wd_hbm, ga1_hbm, bi1_hbm, ga2_hbm, bi2_hbm, bx_hbm, br_hbm, ga3_hbm, bi3_hbm,
    combine_hbm, units,
    f_in, q_in, o_panel,
    we_in, wp_in, wr_in, wx_in, wd_in, ga1_in, bi1_in, ga2_in, bi2_in, bx_in, br_in, ga3_in, bi3_in,
    copy_sems, stage, wide_stage,
    f_rows, q_rows, p_rows, f3, ft, pg3, qpt, qa,
    e_ref, a1, dv, q2, act_hi, act_lo,
    gathered, we, wp, wr, wx, we_b, ws_b, wp_b, wd, wt, par, parts, combine, acc45, acc24, cov_we, kept,
    pool, gates, spread, vec, sums, gp_panel, misc, g_panel,
    near, far, near2, far2,
    g_first, g_second, g_third,
    p_first, p_parts, p_second, p_third,
    m_first, m_parts, m_second, m_third,
    e_first, e_parts, e_second, e_third,
    w_sems, v_sems, g_sems, s_sems,
):
    third = ROWS // 3
    fetch_f = []
    for i in range(3):
        at = pl.ds(i * third, third)
        fetch_f.append(pltpu.make_async_copy(f_hbm.at[:, at], f_in.at[:, at], copy_sems.at[16 + i]))
        fetch_f[i].start()
    small_copies = [
        pltpu.make_async_copy(source, target, copy_sems.at[2 + i])
        for i, (source, target) in enumerate((
            (we_hbm, we_in), (wp_hbm, wp_in), (wr_hbm, wr_in), (wx_hbm, wx_in), (wd_hbm, wd_in),
            (ga1_hbm, ga1_in), (bi1_hbm, bi1_in), (ga2_hbm, ga2_in), (bi2_hbm, bi2_in), (bx_hbm, bx_in),
            (br_hbm, br_in), (ga3_hbm, ga3_in), (bi3_hbm, bi3_in), (combine_hbm, combine),
        ))
    ]
    for copy in small_copies:
        copy.start()
    fetch_q = pltpu.make_async_copy(q_hbm, q_in, copy_sems.at[0])
    fetch_q.start()
    x, y, c, z = place()
    column, plane = column_peers(), plane_peers()
    barrier = pltpu.get_barrier_semaphore()
    for _, device in column[1] + plane[1]:
        pl.semaphore_signal(barrier, inc=1, device_id=device, device_id_type=MESH)

    sum2a = Vector(column, plane, near2.at[0], far2.at[0], v_sems.at[0])
    sum2b = Vector(column, plane, near2.at[1], far2.at[1], v_sems.at[1])
    sum3 = Vector(column, plane, near2.at[2], far2.at[2], v_sems.at[2])
    sum4 = Vector(column, plane, near.at[0], far.at[0], v_sems.at[3])
    sum5 = Vector(column, plane, near.at[1], far.at[1], v_sems.at[4])
    vectors = [sum2a, sum2b, sum3, sum4, sum5]
    reduce_g = Square(column, plane, g_panel, g_first, g_second, g_third, g_sems)
    whole = [(0, WIDE)]
    reduce_p = Panel(column, plane, whole, gp_panel, p_first, p_parts, p_second, p_third, s_sems.at[0])
    reduce_m = Panel(column, plane, whole, misc, m_first, m_parts, m_second, m_third, s_sems.at[1])
    early_late = [(0, 2 * GROUP), (2 * GROUP, WIDE)]
    reduce_e = Panel(column, plane, early_late, gp_panel, e_first, e_parts, e_second, e_third, s_sems.at[2])

    ones = jnp.where(lax.broadcasted_iota(jnp.int32, (16, third), 0) == 0, 1.0, 0.0)
    gram = None
    for i in range(3):
        fetch_f[i].wait()
        at = slice(i * third, (i + 1) * third)
        hi, lo = split(jnp.concatenate([f_in[:, at], ones], axis=0))
        both = jnp.concatenate([hi, lo], axis=0)
        part = mm_nt(both, both)
        gram = part if gram is None else gram + part
    gram = gram[0:128, 0:128] + (gram[0:128, 128:256] + gram[128:256, 0:128]) + gram[128:256, 128:256]
    g_panel[...] = gram.reshape(8, 16, LANE)
    pl.semaphore_wait(barrier, 22)
    reduce_g.start()

    sections = ((0, AT_DEPTH), (AT_DEPTH, AT_PROJECT), (AT_PROJECT, PANEL))
    odd = lax.rem(z, 2) == 1

    across = [(lax.rem(z + k, 4), {"chan": lax.rem(z + k, 4)}) for k in (2, 1, 3)]

    def halves(s):
        lo, hi = sections[s]
        size = (hi - lo) // 2
        return size, pl.ds(pl.multiple_of(lo + c * size, 8), size), pl.ds(lo, size)

    def send_section(s):
        lo, hi = sections[s]
        rest = gathered[z, lo:hi, LANE:GROUP]
        gathered[z, lo:hi, LANE:GROUP] = jnp.where(odd, pltpu.roll(rest, 64, 1), rest)
        size, rows, _ = halves(s)
        for _, device in across:
            pltpu.make_async_remote_copy(
                src_ref=gathered.at[z, rows],
                dst_ref=gathered.at[z, rows],
                send_sem=w_sems.at[0, s],
                recv_sem=w_sems.at[1, s],
                device_id=device,
                device_id_type=MESH,
            ).start()

    def forward_section(s):
        size, rows, some = halves(s)
        drain(gathered.at[pl.ds(0, 3), some], w_sems.at[1, s])
        for other, _ in across:
            pltpu.make_async_remote_copy(
                src_ref=gathered.at[other, rows],
                dst_ref=gathered.at[other, rows],
                send_sem=w_sems.at[0, s],
                recv_sem=w_sems.at[2, s],
                device_id=(x * 8 + y * 2 + 1 - c, z),
                device_id_type=MESH,
            ).start()

    def section(s):
        size, rows, some = halves(s)
        drain(gathered.at[pl.ds(0, 3), some], w_sems.at[2, s])

    def close_section(s):
        size, rows, some = halves(s)
        for _ in range(2):
            drain(gathered.at[pl.ds(0, 3), some], w_sems.at[0, s])

    def assembled(lo, rows):
        parts = [gathered[k, lo : lo + rows, 0:LANE] for k in range(4)]
        for k in (0, 2):
            parts.append(gathered[k, lo : lo + rows, LANE:GROUP] + gathered[k + 1, lo : lo + rows, LANE:GROUP])
        return jnp.concatenate(parts, axis=1)

    for copy in small_copies:
        copy.wait()
    gathered[z] = jnp.zeros((PANEL, GROUP), F32)
    wide_stage[...] = jnp.zeros_like(wide_stage)
    wide_stage[0:OWN, 0:D] = we_in[...]
    gathered[z, 0:D, :] = wide_stage[...].T[0:D]
    send_section(0)
    for a in range(5):
        gathered[z, AT_DEPTH + 5 * a : AT_DEPTH + 5 * a + 5, 0:OWN] = wd_in[a]
    for i, row in enumerate((ga1_in, bi1_in, ga2_in, bi2_in, bx_in)):
        gathered[z, AT_VECS + i : AT_VECS + i + 1, 0:OWN] = row[...]
    send_section(1)
    wide_stage[0:OWN, 0:D] = wp_in[...]
    gathered[z, AT_PROJECT : AT_PROJECT + D, :] = wide_stage[...].T[0:D]
    gathered[z, AT_REDUCE : AT_REDUCE + SQZ, 0:OWN] = wr_in[...]
    gathered[z, AT_EXCITE : AT_EXCITE + SQZ, 0:OWN] = wx_in[...]
    send_section(2)

    tail = jnp.where(lax.broadcasted_iota(jnp.int32, (16, LANE), 0) == 0, 1.0, 0.0)

    def rows_of(source, tail, target):
        @pl.loop(0, BLOCKS)
        def _(b):
            for i in range(3):
                v = source[:, pl.ds(pl.multiple_of(b * CHUNK + i * LANE, LANE), LANE)]
                stage[i * LANE : (i + 1) * LANE, :] = jnp.concatenate([v, tail], axis=0).T
            for cell in range(CELLS):
                v = stage[pl.ds(cell, BLOCK, stride=CELLS), :]
                target[pl.ds((b * CELLS + cell) * 2, 2)] = v.reshape(2, 8, LANE)

    rows_of(f_in, tail, f_rows)

    @rloop("ft", 18)
    def _(i):
        v = f_rows[pl.ds(i * 16, 16)].reshape(128, LANE)
        rows = pl.ds(pl.multiple_of(i * 128, 128), 128)
        hi, lo = split(v)
        f3[rows, 0:128] = hi
        f3[rows, 128:256] = hi
        f3[rows, 256:384] = lo
        hi, lo = split(v.T)
        ft[0:128, rows] = hi
        ft[128:256, rows] = lo

    def parts_of(source, row):
        @pl.loop(0, 18)
        def _(i):
            hi, lo = split(source[pl.ds(i * 16, 16)].reshape(128, LANE).T)
            rows = pl.ds(pl.multiple_of(i * 128, 128), 128)
            qpt[row : row + 128, rows] = hi
            qpt[256 + row : 384 + row, rows] = lo

    reduce_g.middle()
    fetch_q.wait()
    rows_of(q_in, jnp.zeros((16, LANE), F32), q_rows)
    parts_of(q_rows, 0)
    sums[...] = jnp.zeros_like(sums)
    parts[...] = jnp.zeros_like(parts)
    qa[...] = jnp.zeros_like(qa)

    forward_section(0)
    forward_section(1)
    reduce_g.last()
    section(0)
    we[0:D, :] = assembled(0, D)
    we[D:128, :] = jnp.zeros((128 - D, WIDE), F32)
    hi, lo = split(we[...])
    we_b[0:128, :] = hi
    we_b[128:256, :] = lo

    @rloop("E", BLOCKS)
    def _(b):
        @pl.when(b == 3)
        def _():
            forward_section(2)

        rows = pl.ds(pl.multiple_of(b * CHUNK, CHUNK), CHUNK)
        for n in range(3):
            cols = slice(n * GROUP, (n + 1) * GROUP)
            r = mm(f3[rows, 0:256], we_b[:, cols]) + mm(f3[rows, 256:384], we_b[0:128, cols])
            e_ref[pl.ds(b * 48, 48), :, cols] = r.reshape(48, 8, GROUP)

    section(1)
    taps = assembled(AT_DEPTH, 32)
    for a in range(5):
        row = [taps[5 * a + k : 5 * a + k + 1] for k in range(5)]
        for m, v in enumerate(nine_weights(row)):
            wd[a * 9 + m : a * 9 + m + 1, :] = v
        for m, v in enumerate(nine_weights(row[::-1])):
            wt[(4 - a) * 9 + m : (4 - a) * 9 + m + 1, :] = v
    gain1, bias1, gain2, bias2, bx = [taps[TAPS + i : TAPS + i + 1] for i in range(5)]

    section(2)
    wp[0:D, :] = assembled(AT_PROJECT, D)
    wp[D:128, :] = jnp.zeros((128 - D, WIDE), F32)
    hi, lo = split(assembled(AT_REDUCE, 32))
    wr[...] = jnp.concatenate([hi, lo, hi, lo], axis=0)
    hi, lo = split(assembled(AT_EXCITE, 32))
    wx[...] = jnp.concatenate([hi, lo, hi, lo], axis=0)
    gram = reduce_g.finish() * (1.0 / TOTAL)
    f_mean_row = gram[D : D + 1, :]
    f_mean = gram[:, D : D + 1]
    cov = gram - f_mean * f_mean_row
    hi, lo = split(cov)
    cov_we[...] = mm(jnp.concatenate([hi, hi], axis=1), we_b[...]) + mm(jnp.concatenate([lo, lo], axis=1), we_b[...])
    mean1 = row_sum(we[...] * f_mean)
    inv1 = lax.rsqrt(row_sum(we[...] * cov_we[...]) + EPSILON)
    s1 = gain1 * inv1
    t1 = bias1 - mean1 * s1

    def put(i, row, lo=0, hi=WIDE):
        par[i, :, lo:hi] = jnp.broadcast_to(row, (8, hi - lo))

    put(0, 0.5 * s1)
    put(1, 0.5 * t1)

    def put_sums(first, second, g, low, size):
        sums[pl.ds(g - low, 1), :] = row_sum(first)
        sums[pl.ds(g - low + size, 1), :] = row_sum(second)

    @rloop("conv1", GROUPS)
    def _(g):
        cols = lanes_of(g)

        def block(b, carry):
            total, square = carry
            base = b * 48
            scale, shift = par[0, :, cols], par[1, :, cols]
            for cell in range(CELLS):
                at = pl.ds(base + 2 * cell, 2)
                h, th = half_gate(e_ref[at, :, cols], scale, shift)
                a1[at, :, cols] = h + h * th
            tally = [total, square]

            def put(i, j, v):
                dv[pl.ds(base + 2 * (i * W + j), 2), :, cols] = v
                tally[0] = tally[0] + fold(v)
                tally[1] = tally[1] + fold(v * v)

            convolve(column_of(a1, base, cols), wd, cols, kept, put)
            total, square = tally
            return total, square

        zero = jnp.zeros((8, LANE), F32)
        total, square = lax.fori_loop(0, BLOCKS // 2, lambda i, v: block(2 * i + 1, block(2 * i, v)), (zero, zero))
        put_sums(total, square, g, jnp.where(g < 4, 0, 4), jnp.where(g < 4, 4, 2))

        @pl.when(g == 3)
        def _():
            sum2a.start(sums[0:8, :])

        @pl.when(g == 5)
        def _():
            sum2b.start(sums[0:8, :])

    def wide(rows, first, count):
        return jnp.concatenate([rows[first + g : first + g + 1, :] for g in range(count)], axis=1)

    mean2, inv2 = [None] * 2, [None] * 2

    def second_norm(got, lo, hi):
        count = (hi - lo) // LANE
        mean = wide(got, 0, count) * (1.0 / TOTAL)
        inv = lax.rsqrt(wide(got, count, count) * (1.0 / TOTAL) - mean * mean + EPSILON)
        scale = par[7, 0:1, lo:hi] * inv
        put(2, 0.5 * scale, lo, hi)
        put(3, 0.5 * (par[8, 0:1, lo:hi] - mean * scale), lo, hi)
        put(9, mean, lo, hi)
        put(10, inv, lo, hi)
        put(11, scale, lo, hi)

    put(7, gain2)
    put(8, bias2)

    def one_products(g):
        cols = lanes_of(g)
        acc45[...] = jnp.zeros_like(acc45)
        acc24[...] = jnp.zeros_like(acc24)

        @pl.loop(0, BLOCKS)
        def _(b):
            for cell in range(CELLS):
                acc24[cell] += fold(a1[pl.ds(b * 48 + 2 * cell, 2), :, cols])
            correlate(acc45, column_of(dv, b * 48, cols), column_of(a1, b * 48, cols))

        row_sums(parts, IN_D, acc45, cols)
        row_sums(parts, IN_CELLS, acc24, cols)

    def one_activation(g):
        cols = lanes_of(g)

        @pl.loop(0, BLOCKS)
        def _(b):
            scale, shift = par[2, :, cols], par[3, :, cols]
            pooled = jnp.zeros((8, LANE), F32)
            for cell in range(CELLS):
                at = pl.ds(b * 48 + 2 * cell, 2)
                h, th = half_gate(dv[at, :, cols], scale, shift)
                q2[at, :, cols] = th
                act = h + h * th
                pooled = pooled + fold(act)
                hi, lo = split(act.reshape(16, LANE))
                rows = pl.ds(b * CHUNK + 16 * cell, 16)
                act_hi[rows, cols] = hi
                act_lo[rows, cols] = lo
            pool[b, :, cols] = pooled

    @pl.loop(0, 11)
    def _(step):
        @pl.when(step == 1)
        def _():
            sum2a.middle()

        @pl.when(step == 3)
        def _():
            sum2b.middle()

        @pl.when(step == 5)
        def _():
            second_norm(sum2a.finish(), 0, 4 * LANE)

        @pl.when(step == 9)
        def _():
            second_norm(sum2b.finish(), 4 * LANE, WIDE)

        @pl.when(step < 5)
        def _():
            one_products(step)

        @pl.when(step >= 5)
        def _():
            one_activation(step - 5)

    seg = lax.broadcasted_iota(jnp.int32, (8, LANE), 0)
    blk = lax.broadcasted_iota(jnp.int32, (8, LANE), 1)
    u0, u1, u2 = units[z, 0], units[z, 1], units[z, 2]
    lower = jnp.where(seg == 0, 0, jnp.where(seg == 1, u0, u0 + u1))
    length = jnp.where(seg == 0, u0, jnp.where(seg == 1, u1, u2))
    member = jnp.where((seg < 3) & (blk >= lower) & (blk < lower + length), 1.0, 0.0)
    per_count = jnp.where(seg < 3, 1.0 / (length * (BLOCK * CELLS)).astype(F32), 0.0)[:, 0:1]
    live = jnp.where(seg < 3, 1.0, 0.0)[:, 0:1]

    vec[...] = jnp.zeros((8, LANE), F32)
    vec[0:1, 0:SQZ] = br_in[...]
    pooled = jnp.zeros((8, WIDE), F32)
    for b in range(BLOCKS):
        pooled = pooled + member[:, b : b + 1] * row_sum(pool[b])
    plain_sums = pooled
    pooled = pooled * per_count
    pooled_pair = pair(pooled)
    reduced = pair_nt(pooled_pair, wr[0:64, :], 8, 32) + vec[0:1, 0:32]
    sig_r = sigmoid(reduced)
    squeezed = reduced * sig_r * live

    def quad(values):
        hi, lo = split(values)
        return jnp.concatenate([hi, hi, lo, lo], axis=1)

    gate = sigmoid(mm(quad(squeezed), wx[...]) + bx)

    def of_blocks(rows, b):
        return row_sum(member[:, b : b + 1] * rows)

    for b in range(BLOCKS):
        gates[b : b + 1, :] = of_blocks(gate, b)

    def project(b, carry):
        rows = slice(b * CHUNK, (b + 1) * CHUNK)
        hi, lo = split(wp[...] * gates[b : b + 1, :])
        wp_b[b, 0:128, :] = hi
        wp_b[b, 128:256, :] = lo
        r = mm_nt(act_hi[rows, :], wp_b[b])
        r = r[:, 0:128] + r[:, 128:256] + mm_nt(act_lo[rows, :], wp_b[b, 0:128, :])
        r = r.reshape(48, 8, LANE)
        q = q_rows[pl.ds(b * 48, 48)]
        p_rows[pl.ds(b * 48, 48)] = r
        return tuple(old + jnp.sum(new, axis=0) for old, new in zip(carry, (r, r * r, q, q * r)))

    zero = jnp.zeros((8, LANE), F32)
    four = (zero,) * 4
    for b in range(BLOCKS):
        four = project(b, four)
    for i in range(4):
        vec[i : i + 1, :] = row_sum(four[i])
    sum3.start(vec[...])

    parts_of(p_rows, 128)

    for b in range(BLOCKS):
        rows = slice(b * CHUNK, (b + 1) * CHUNK)
        inside = [jnp.where((b >= low) & (b < high), 1.0, 0.0) for low, high in ((0, u0), (u0, u0 + u1), (u0 + u1, 6))]
        m = mm(qpt[:, rows], act_hi[rows, :])
        m = m[0:256] + m[256:512] + mm(qpt[0:256, rows], act_lo[rows, :])
        for k in range(3):
            qa[k] += m * inside[k]
        if b == 3:
            sum3.middle()

    @rloop("slope2", GROUPS)
    def _(g):
        cols = lanes_of(g)

        @pl.loop(0, BLOCKS)
        def _(b):
            scale, shift = par[2, :, cols], par[3, :, cols]
            for cell in range(CELLS):
                at = pl.ds(b * 48 + 2 * cell, 2)
                q2[at, :, cols] = twice_slope_of(dv[at, :, cols] * scale + shift, q2[at, :, cols])

    def one_slope(g):
        cols = lanes_of(g)

        @pl.loop(0, BLOCKS)
        def _(b):
            scale, shift = par[0, :, cols], par[1, :, cols]
            for cell in range(CELLS):
                at = pl.ds(b * 48 + 2 * cell, 2)
                e_ref[at, :, cols] = twice_slope_of(*half_gate(e_ref[at, :, cols], scale, shift))

    pl.loop(0, 3)(one_slope)
    got = sum3.finish() * (1.0 / TOTAL)
    vec[...] = jnp.zeros((8, LANE), F32)
    vec[0:1, 0:D] = ga3_in[...]
    vec[1:2, 0:D] = bi3_in[...]
    gain3, bias3 = vec[0:1, :], vec[1:2, :]
    mean3 = got[0:1]
    inv3 = lax.rsqrt(got[1:2] - mean3 * mean3 + EPSILON)
    b3 = got[2:3]
    g3 = (got[3:4] - mean3 * got[2:3]) * inv3
    o_panel[OUT_SMALL : OUT_SMALL + 1, 0:LANE] = g3 * TOTAL
    o_panel[OUT_SMALL + 1 : OUT_SMALL + 2, 0:LANE] = b3 * TOTAL
    s3 = gain3 * inv3
    t3 = bias3 - mean3 * s3
    pg_p = -s3 * inv3 * g3
    pg_0 = -s3 * b3 - pg_p * mean3

    columns = jnp.concatenate([s3, pg_p, pg_0, jnp.zeros((5, LANE), F32)], axis=0).T
    by_q, by_p, by_1 = columns[:, 0:1], columns[:, 1:2], columns[:, 2:3]
    base = row_sum(wp[...] * by_1)
    w_q, w_p = wp[...] * by_q, wp[...] * by_p
    gate_grad = jnp.concatenate(
        [row_sum(w_q * qa[k, 0:128] + w_p * qa[k, 128:256]) + base * plain_sums[k : k + 1] for k in range(3)]
        + [jnp.zeros((5, WIDE), F32)],
        axis=0,
    )
    excite_in = gate_grad * gate * (1.0 - gate)
    reduced_grad = pair_nt(pair(excite_in), wx[0:64, :], 8, 32) * (sig_r * (1.0 + reduced * (1.0 - sig_r))) * live
    pooled_grad = mm(quad(reduced_grad), wr[...]) * per_count
    for b in range(BLOCKS):
        spread[b : b + 1, :] = 0.5 * of_blocks(pooled_grad, b)

    for b in range(BLOCKS):
        at = pl.ds(b * 48, 48)
        hi, lo = split((q_rows[at] * (0.5 * s3) + (p_rows[at] * (0.5 * pg_p) + 0.5 * pg_0)).reshape(CHUNK, LANE))
        rows = pl.ds(b * CHUNK, CHUNK)
        pg3[rows, 0:128] = hi
        pg3[rows, 128:256] = hi
        pg3[rows, 256:384] = lo

    total = product = jnp.zeros((8, WIDE), F32)
    for b in range(BLOCKS):
        rows = slice(b * CHUNK, (b + 1) * CHUNK)
        at = slice(b * 48, (b + 1) * 48)
        r = mm(pg3[rows, 0:256], wp_b[b]) + mm(pg3[rows, 256:384], wp_b[b, 0:128, :])
        r = (r.reshape(48, 8, WIDE) + spread[b : b + 1, :]) * q2[at]
        q2[at] = r
        total, product = total + jnp.sum(r, axis=0), product + jnp.sum(r * dv[at], axis=0)
    total, product = row_sum(total), row_sum(product)
    for g in range(GROUPS):
        lanes = slice(g * LANE, (g + 1) * LANE)
        sums[g : g + 1, :] = total[:, lanes]
        sums[8 + g : 9 + g, :] = product[:, lanes]
    sum4.start(sums[...])

    gp = jnp.zeros((128, WIDE), F32)
    for k in range(3):
        gp = gp + gate[k : k + 1] * (by_q * qa[k, 0:128] + by_p * qa[k, 128:256] + by_1 * plain_sums[k : k + 1])
    gp_panel[...] = gp.reshape(16, 8, WIDE)
    g_excite = exact(squeezed, excite_in, (0, 0))
    gp_panel[14, 0:1, :] = row_sum(excite_in)
    gp_panel[15, 0:1, :] = jnp.zeros((1, WIDE), F32)
    for k in range(4):
        gp_panel[15, 0:1, k * LANE : k * LANE + 32] = row_sum(reduced_grad)
    for i in range(IN_THIRD, SQZ):
        gp_panel[14, 1 + i - IN_THIRD : 2 + i - IN_THIRD, :] = g_excite[i : i + 1]
    reduce_p.start(0)

    parts[IN_R : IN_R + 32, :] = exact(reduced_grad, pooled, (0, 0))
    parts[IN_X : IN_X + 32, :] = g_excite

    @rloop("tq", GROUPS)
    def _(g):
        cols = lanes_of(g)
        acc45[...] = jnp.zeros_like(acc45)

        @pl.loop(0, BLOCKS)
        def _(b):
            correlate(acc45, column_of(q2, b * 48, cols), column_of(a1, b * 48, cols))

        @pl.when(g >= 3)
        def _():
            one_slope(g)

        row_sums(parts, 0, acc45, cols)

        @pl.when(g == 2)
        def _():
            sum4.middle()

    def own_lanes(rows):
        first = rows[:, 0:LANE]
        rest = rows[:, LANE:GROUP]
        return first, jnp.where(odd, pltpu.roll(rest, 64, 1), rest)

    def own_wide(rows):
        first = jnp.zeros((rows.shape[0], LANE), F32)
        rest = jnp.zeros((rows.shape[0], LANE), F32)
        for k in range(4):
            first = jnp.where(z == k, rows[:, k * LANE : (k + 1) * LANE], first)
        for k in range(2):
            rest = jnp.where(z // 2 == k, rows[:, (4 + k) * LANE : (5 + k) * LANE], rest)
        return jnp.concatenate([first, rest], axis=1)

    def emit(row, values):
        first, rest = own_lanes(values)
        o_panel[row : row + values.shape[0], 0:LANE] = first
        o_panel[row : row + values.shape[0], LANE:GROUP] = rest

    def emit_vector(i, row):
        emit(OUT_VECS + i, own_wide(row))

    one_products(5)

    hi, lo = split(parts[...])
    picks = combine[...].astype(BF16)
    misc[...] = (mm(picks, hi) + mm(picks, lo)).reshape(16, 8, WIDE)
    reduce_m.start(0)

    got = sum4.finish()
    mean2, inv2, s2 = [par[i, 0:1, :] for i in (9, 10, 11)]
    b2 = wide(got, 0, GROUPS)
    g2 = (wide(got, 8, GROUPS) - mean2 * b2) * inv2
    c3 = -s2 * inv2 * g2 * (1.0 / TOTAL)
    c2 = -s2 * b2 * (1.0 / TOTAL) - c3 * mean2
    shift3 = -inv2 * g2 * (1.0 / TOTAL)
    put(4, -b2 * (1.0 / TOTAL) - shift3 * mean2)
    put(5, shift3)
    wt[...] = wt[...] * (0.5 * s2)
    emit_vector(2, g2)
    emit_vector(3, b2)

    @rloop("conv2", GROUPS)
    def _(g):
        @pl.when(g == 1)
        def _():
            reduce_p.sent()

        cols = lanes_of(g)

        def block(b):
            base = b * 48
            k2, k3 = par[4, :, cols], par[5, :, cols]

            for cell in range(CELLS):
                at = pl.ds(base + 2 * cell, 2)
                q2[at, :, cols] = q2[at, :, cols] + (dv[at, :, cols] * k3 + k2)

            def put(i, j, v):
                at = pl.ds(base + 2 * (i * W + j), 2)
                hi, lo = split((v * e_ref[at, :, cols]).reshape(16, LANE))
                rows = pl.ds(b * CHUNK + 16 * (i * W + j), 16)
                act_hi[rows, cols] = hi
                act_lo[rows, cols] = lo

            convolve(column_of(q2, base, cols), wt, cols, kept, put)

        @pl.loop(0, BLOCKS // 2)
        def _(i):
            block(2 * i)
            block(2 * i + 1)

        @pl.when(lax.rem(g, 2) == 1)
        def _():
            n = g // 2
            cols = pl.ds(pl.multiple_of(n * GROUP, GROUP), GROUP)
            m = mm(ft[...], act_hi[:, cols])
            m = m[0:128] + m[128:256] + mm(ft[0:128, :], act_lo[:, cols])
            gp_panel[:, :, cols] = m.reshape(16, 8, GROUP)

            @pl.when(g == 5)
            def _():
                reduce_e.start(1)

            product = row_sum(m * we[:, cols])
            for half in range(2):
                lanes = slice(half * LANE, (half + 1) * LANE)
                sums[pl.ds(g - 1 + half, 1), :] = m[D : D + 1, lanes]
                sums[pl.ds(g + 7 + half, 1), :] = product[:, lanes]

            @pl.when(g == 3)
            def _():
                reduce_e.start(0)

    sum5.start(sums[...])
    reduce_p.middle()
    reduce_m.middle()

    hi, lo = split(we[...] * s1)
    ws_b[0:128, :] = hi
    ws_b[128:256, :] = lo

    @rloop("ig", 3)
    def _(i):
        rows = pl.ds(pl.multiple_of(i * 2 * CHUNK, 2 * CHUNK), 2 * CHUNK)
        r = mm_nt(act_hi[rows, :], ws_b[...])
        r = r[:, 0:128] + r[:, 128:256] + mm_nt(act_lo[rows, :], ws_b[0:128, :])
        q_rows[pl.ds(i * 96, 96)] += r.reshape(96, 8, LANE)

    sum5.middle()

    def write(target, b, rows_of_cell):
        for cell in range(CELLS):
            stage[pl.ds(cell, BLOCK, stride=CELLS), :] = rows_of_cell(pl.ds(b * 48 + 2 * cell, 2)).reshape(16, LANE)
        for i in range(3):
            at = pl.ds(pl.multiple_of(b * CHUNK + i * LANE, LANE), LANE)
            target[:, at] = stage[i * LANE : (i + 1) * LANE, :].T[0:D]

    reduce_e.middle()
    reduce_p.last()
    reduce_m.last()

    @rloop("out", BLOCKS)
    def _(b):
        write(f_in, b, lambda at: f_rows[at] + (p_rows[at] * s3 + t3))

    reduce_e.last()
    got = sum5.finish()
    b1 = wide(got, 0, GROUPS)
    g1 = (wide(got, 8, GROUPS) - mean1 * b1) * inv1
    k3 = -s1 * inv1 * g1 * (1.0 / TOTAL)
    k2 = -s1 * b1 * (1.0 / TOTAL) - k3 * mean1
    left = jnp.where(lax.broadcasted_iota(jnp.int32, (128, WIDE), 0) == D, k2, we[...] * k3)
    mix = pair_nt(pair(left), we_b[...], 128, 128)
    mix_hi, mix_lo = split(mix)
    mix_all = jnp.concatenate([mix_hi, mix_lo], axis=0)

    @rloop("ig2", BLOCKS)
    def _(b):
        rows = pl.ds(pl.multiple_of(b * CHUNK, CHUNK), CHUNK)
        r = mm(f3[rows, 0:256], mix_all) + mm(f3[rows, 256:384], mix_hi)
        q_rows[pl.ds(b * 48, 48)] += r.reshape(48, 8, LANE)
        write(q_in, b, lambda at: q_rows[at])

    emit_vector(0, g1)
    emit_vector(1, b1)
    emit(OUT_PROJECT, reduce_p.finish())
    total_m = reduce_m.finish()
    emit(OUT_MISC, total_m)
    by = [own_wide(v) for v in (s2, c2, c3)]
    taps_grad = total_m[0:TAPS] * by[0] + total_m[AT_DD : AT_DD + TAPS] * by[2] + total_m[AT_PLAIN : AT_PLAIN + TAPS] * by[1]
    emit(OUT_MISC, taps_grad)
    scale_own = own_wide(s1)
    away = f_mean * own_wide(b1) + own_wide(cov_we[...]) * own_wide(inv1 * g1)
    for s in range(3):
        close_section(s)
    reduce_m.sent()
    reduce_e.sent()
    for item in vectors + [reduce_g, reduce_p, reduce_m, reduce_e]:
        item.close()
    emit(0, scale_own * (reduce_e.finish() - away))


def finish_kernel(
    out_in, igrad_in, panel,
    out, igrad, expand, gain1, bias1, depth, gain2, bias2, reduce, b_reduce, excite, b_excite, project, gain3, bias3,
    sems,
):
    large = [pltpu.make_async_copy(out_in, out, sems.at[0]), pltpu.make_async_copy(igrad_in, igrad, sems.at[1])]
    for copy in large:
        copy.start()
    expand[...] = panel[0:LANE, :].T[0:OWN, 0:D]
    project[...] = panel[OUT_PROJECT : OUT_PROJECT + LANE, :].T[0:OWN, 0:D]
    for a in range(5):
        depth[a] = panel[OUT_MISC + 5 * a : OUT_MISC + 5 * a + 5, 0:OWN]
    reduce[...] = panel[OUT_MISC + AT_R : OUT_MISC + AT_R + SQZ, 0:OWN]
    excite[0:IN_THIRD, :] = panel[OUT_MISC + AT_X : OUT_MISC + 128, 0:OWN]
    excite[IN_THIRD:SQZ, :] = panel[OUT_PROJECT + D + 1 : OUT_PROJECT + D + 1 + SQZ - IN_THIRD, 0:OWN]
    b_excite[...] = panel[OUT_PROJECT + D : OUT_PROJECT + D + 1, 0:OWN]
    b_reduce[...] = panel[OUT_PROJECT + D + 8 : OUT_PROJECT + D + 9, 0:SQZ]
    for i, ref in enumerate((gain1, bias1, gain2, bias2)):
        ref[...] = panel[OUT_VECS + i : OUT_VECS + i + 1, 0:OWN]
    gain3[...] = panel[OUT_SMALL : OUT_SMALL + 1, 0:D]
    bias3[...] = panel[OUT_SMALL + 1 : OUT_SMALL + 2, 0:D]
    for copy in large:
        copy.wait()


def body(
    features, seg_units, w_expand, gain_one, bias_one, w_depth, gain_two, bias_two,
    w_reduce, b_reduce, w_excite, b_excite, w_project, gain_three, bias_three, cotangent,
):
    vm = pl.BlockSpec(memory_space=pltpu.VMEM)
    anywhere = pl.BlockSpec(memory_space=pl.ANY)
    big = pltpu.VMEM((288, 8, WIDE), F32)
    rows128 = pltpu.VMEM((288, 8, LANE), F32)
    half = pltpu.VMEM((ROWS, WIDE), BF16)

    def f32(*shape):
        return pltpu.VMEM(shape, F32)

    def b16(*shape):
        return pltpu.VMEM(shape, BF16)

    def shape(*dims):
        return jax.ShapeDtypeStruct(dims, F32)

    def row(vector):
        return vector.reshape(1, vector.shape[0])

    dma = pltpu.SemaphoreType.DMA
    slots = [f32(16, 8, WIDE), f32(4, 8, GROUP), f32(8, 8, GROUP), f32(16, 8, GROUP)]
    out, igrad, panel = pl.pallas_call(
        kernel,
        out_shape=(f32(D, ROWS), f32(D, ROWS), f32(RESULTS, GROUP)),
        in_specs=[anywhere] * 16 + [pl.BlockSpec(memory_space=pltpu.SMEM)],
        out_specs=(vm,) * 3,
        scratch_shapes=[
            f32(OWN, D), f32(OWN, D), f32(SQZ, OWN), f32(SQZ, OWN), f32(5, 5, OWN),
            f32(1, OWN), f32(1, OWN), f32(1, OWN), f32(1, OWN), f32(1, OWN), f32(1, SQZ), f32(1, D), f32(1, D),
            dma((19,)), f32(CHUNK, LANE), f32(GROUP, LANE),
            rows128, rows128, rows128, b16(ROWS, 384), b16(256, ROWS), b16(ROWS, 384), b16(512, ROWS), f32(3, 256, WIDE),
            big, big, big, big, half, half,
            f32(4, PANEL, GROUP), f32(128, WIDE), f32(128, WIDE), b16(128, WIDE), b16(128, WIDE),
            b16(256, WIDE), b16(256, WIDE), b16(BLOCKS, 256, WIDE), f32(48, WIDE), f32(48, WIDE), f32(12, 8, WIDE),
            f32(SUMS, WIDE), f32(128, SUMS), f32(45, 8, LANE), f32(CELLS, 8, LANE), f32(128, WIDE), f32(2 * H, 2, 8, LANE),
            f32(BLOCKS, 8, WIDE), f32(8, WIDE), f32(8, WIDE), f32(8, LANE), f32(16, LANE),
            f32(16, 8, WIDE), f32(16, 8, WIDE), f32(8, 16, LANE),
            f32(2, 8, 16, LANE), f32(2, 16, 16, LANE), f32(3, 8, 8, LANE), f32(3, 16, 8, LANE),
            f32(8, 16, LANE), f32(16, 16, LANE), f32(8, 16, LANE),
        ]
        + slots * 3
        + [dma((3, 3)), dma((5, 4)), dma((6,)), dma((3, 8))],
        compiler_params=pltpu.CompilerParams(
            collective_id=0, has_side_effects=True, vmem_limit_bytes=61 * 1024 * 1024 + 256 * 1024
        ),
    )(
        features.T, cotangent.T, w_expand.T, w_project, w_reduce.T, w_excite, w_depth,
        row(gain_one), row(bias_one), row(gain_two), row(bias_two), row(b_excite), row(b_reduce), row(gain_three), row(bias_three),
        jnp.asarray(combination()), seg_units,
    )

    small = [
        (OWN, D), (1, OWN), (1, OWN), (5, 5, OWN), (1, OWN), (1, OWN),
        (SQZ, OWN), (1, SQZ), (SQZ, OWN), (1, OWN), (OWN, D), (1, D), (1, D),
    ]
    results = pl.pallas_call(
        finish_kernel,
        out_shape=(shape(D, ROWS), shape(D, ROWS)) + tuple(shape(*dims) for dims in small),
        in_specs=[vm] * 3,
        out_specs=(anywhere, anywhere) + (vm,) * 13,
        scratch_shapes=[dma((2,))],
        compiler_params=pltpu.CompilerParams(vmem_limit_bytes=8 * 1024 * 1024),
    )(*(pltpu.with_memory_space_constraint(v, pltpu.VMEM) for v in (out, igrad, panel)))
    (out, igrad, expand, gain1, bias1, depth, gain2, bias2, reduce, small_b, excite, b_x, project, gain3, bias3) = results
    return (
        out.T, igrad.T, expand.T, gain1[0], bias1[0], depth, gain2[0], bias2[0],
        reduce.T, small_b[0], excite, b_x[0], project, gain3[0], bias3[0],
    )


def solution(mesh):
    placed = (
        P(("dp", "chan"), None),
        P("dp", None),
        P(None, "chan"),
        P("chan"),
        P("chan"),
        P(None, None, "chan"),
        P("chan"),
        P("chan"),
        P("chan", None),
        P(),
        P(None, "chan"),
        P("chan"),
        P("chan", None),
        P(),
        P(),
        P(("dp", "chan"), None),
    )
    return jax.shard_map(
        body,
        mesh=mesh,
        in_specs=placed,
        out_specs=(
            P(("dp", "chan"), None),
            P(("dp", "chan"), None),
            P(None, "chan"),
            P("chan"),
            P("chan"),
            P(None, None, "chan"),
            P("chan"),
            P("chan"),
            P("chan", None),
            P(),
            P(None, "chan"),
            P("chan"),
            P("chan", None),
            P(),
            P(),
        ),
        check_vma=False,
    )
```

```python
import jax
import jax.numpy as jnp
import numpy as np
from jax import lax
from jax.experimental import pallas as pl
from jax.experimental.pallas import tpu as pltpu
from jax.sharding import PartitionSpec as P

MESH = pl.DeviceIdType.MESH
F32 = jnp.float32
BF16 = jnp.bfloat16
EPSILON = 0.001
PRECISE = lax.Precision.HIGHEST
D = 112
SQZ = 28
EXP = 672
H, W, CELLS = 6, 4, 24
TAPS = 25
BLOCK, BLOCKS = 16, 6
ROWS = 2304
CHUNK = BLOCK * CELLS
LANE = 128
WIDE = 768
GROUPS = WIDE // LANE
TOTAL = 294912.0
OWN = 168
REST = OWN - LANE

AT_EXPAND, AT_DEPTH, AT_VECS, AT_PROJECT, AT_REDUCE, AT_EXCITE, PANEL = 0, 112, 137, 144, 256, 288, 320
AT_DD, AT_PLAIN, AT_R, AT_X = TAPS, 2 * TAPS, 3 * TAPS, 3 * TAPS + SQZ
IN_THIRD = 128 - AT_X
OUT_PROJECT, OUT_MISC, OUT_VECS, OUT_SMALL, RESULTS = 128, 256, 384, 392, 400
GROUP = 2 * LANE


REPS = {}


def rep(name):
    count = REPS.get(name, 1)

    def run(fn):
        if count == 1:
            fn()
        else:
            lax.fori_loop(0, count, lambda i, carry: (fn(), carry)[1], 0)

    return run


def rloop(name, size):
    count = REPS.get(name, 1)

    def run(fn):
        if count == 1:
            pl.loop(0, size)(fn)
        else:
            pl.loop(0, size * count)(lambda i: fn(lax.rem(i, size)))

    return run


def split(values):
    high = values.astype(BF16)
    return high, (values - high.astype(F32)).astype(BF16)


def mm(a, b):
    return lax.dot_general(a, b, (((1,), (0,)), ((), ())), preferred_element_type=F32)


def mm_nt(a, b):
    return lax.dot_general(a, b, (((1,), (1,)), ((), ())), preferred_element_type=F32)


def exact(a, b, dims):
    return lax.dot_general(a, b, ((dims[:1], dims[1:]), ((), ())), precision=PRECISE, preferred_element_type=F32)


def pair(values):
    return jnp.concatenate(split(values), axis=0)


def pair_nt(a, b, rows, cols):
    r = mm_nt(a, b)
    return (r[0:rows, 0:cols] + r[rows:, cols:]) + (r[0:rows, cols:] + r[rows:, 0:cols])


def place():
    dp = lax.axis_index("dp")
    z = lax.axis_index("chan")
    return dp // 8, lax.rem(dp // 2, 4), lax.rem(dp, 2), z


def ring(step):
    return min(step, 4 - step)


def column_peers():
    x, y, c, z = place()
    moves = [(dz, dc) for dz in range(4) for dc in range(2) if dz or dc]
    moves.sort(key=lambda m: -10 * ring(m[0]) - m[1])
    base = x * 8 + y * 2
    zs = [lax.rem(z + dz, 4) for dz in range(4)]
    cs = [c, 1 - c]
    return z * 2 + c, [(zs[dz] * 2 + cs[dc], (base + cs[dc], zs[dz])) for dz, dc in moves]


def plane_peers():
    x, y, c, z = place()
    moves = [(dx, dy) for dx in range(4) for dy in range(4) if dx or dy]
    moves.sort(key=lambda m: -ring(m[0]) - ring(m[1]))
    xs = [lax.rem(x + dx, 4) for dx in range(4)]
    ys = [lax.rem(y + dy, 4) for dy in range(4)]
    peers = []
    for dx, dy in moves:
        rank = xs[dx] * 4 + ys[dy]
        peers.append((rank, (rank * 2 + c, z)))
    return x * 4 + y, peers


def push(sources, slots, mine, peers, send, recv):
    for rank, device in peers:
        pltpu.make_async_remote_copy(
            src_ref=sources(rank),
            dst_ref=slots.at[mine],
            send_sem=send,
            recv_sem=recv,
            device_id=device,
            device_id_type=MESH,
        ).start()


def drain(view, sem):
    pltpu.make_async_copy(view, view, sem).wait()


def add_slots(slots, count):
    total = slots[0]
    for k in range(1, count):
        total = total + slots[k]
    return total


class Vector:
    def __init__(self, column, plane, near, far, sems):
        self.column, self.plane, self.near, self.far, self.sems = column, plane, near, far, sems

    def start(self, value):
        mine, peers = self.column
        self.near[mine] = value
        push(lambda rank: self.near.at[mine], self.near, mine, peers, self.sems.at[0], self.sems.at[1])

    def middle(self):
        drain(self.near.at[pl.ds(0, 7)], self.sems.at[1])
        mine, peers = self.plane
        self.far[mine] = add_slots(self.near, 8)
        push(lambda rank: self.far.at[mine], self.far, mine, peers, self.sems.at[2], self.sems.at[3])

    def finish(self):
        drain(self.far.at[pl.ds(0, 15)], self.sems.at[3])
        return add_slots(self.far, 16)

    def close(self):
        drain(self.near.at[pl.ds(0, 7)], self.sems.at[0])
        drain(self.far.at[pl.ds(0, 15)], self.sems.at[2])


class Square:
    def __init__(self, column, plane, source, first, second, third, sems):
        self.column, self.plane = column, plane
        self.source, self.first, self.second, self.third, self.sems = source, first, second, third, sems

    def start(self):
        mine, peers = self.column
        self.first[mine] = self.source[mine]
        push(lambda rank: self.source.at[rank], self.first, mine, peers, self.sems.at[0], self.sems.at[1])

    def middle(self):
        drain(self.first.at[pl.ds(0, 7)], self.sems.at[1])
        mine, peers = self.plane
        self.second[mine] = add_slots(self.first, 8)
        push(lambda rank: self.second.at[mine], self.second, mine, peers, self.sems.at[2], self.sems.at[3])

    def last(self):
        drain(self.second.at[pl.ds(0, 15)], self.sems.at[3])
        mine, peers = self.column
        self.third[mine] = add_slots(self.second, 16)
        push(lambda rank: self.third.at[mine], self.third, mine, peers, self.sems.at[4], self.sems.at[5])

    def finish(self):
        drain(self.third.at[pl.ds(0, 7)], self.sems.at[5])
        return self.third[...].reshape(128, LANE)

    def close(self):
        drain(self.first.at[pl.ds(0, 7)], self.sems.at[0])
        drain(self.second.at[pl.ds(0, 15)], self.sems.at[2])
        drain(self.third.at[pl.ds(0, 7)], self.sems.at[4])


class Panel:
    def __init__(self, column, plane, ranges, source, first, parts, second, third, sems):
        self.column, self.plane, self.ranges = column, plane, ranges
        self.source, self.first, self.parts, self.second, self.third, self.sems = source, first, parts, second, third, sems

    def start(self, index):
        mine, peers = self.plane
        lo, hi = self.ranges[index]
        lanes = pl.ds(lo, hi - lo)
        self.first[mine, :, lo:hi] = self.source[mine, :, lo:hi]
        for rank, device in peers:
            pltpu.make_async_remote_copy(
                src_ref=self.source.at[rank, :, lanes],
                dst_ref=self.first.at[mine, :, lanes],
                send_sem=self.sems.at[0],
                recv_sem=self.sems.at[1 + index],
                device_id=device,
                device_id_type=MESH,
            ).start()

    def scattered(self, index, sem):
        lo, hi = self.ranges[index]
        drain(self.first.at[pl.ds(0, 15), :, pl.ds(lo, hi - lo)], self.sems.at[sem])

    def middle(self):
        for index in range(len(self.ranges)):
            self.scattered(index, 1 + index)
        total = add_slots(self.first, 16)
        mine, peers = self.column
        for z in range(4):
            self.parts[z, :, 0:LANE] = total[:, z * LANE : (z + 1) * LANE]
            rest = 4 + z // 2
            self.parts[z, :, LANE:GROUP] = total[:, rest * LANE : (rest + 1) * LANE]
        self.second[mine] = self.parts[mine // 2]
        push(lambda rank: self.parts.at[rank // 2], self.second, mine, peers, self.sems.at[4], self.sems.at[5])

    def last(self):
        drain(self.second.at[pl.ds(0, 7)], self.sems.at[5])
        mine, peers = self.plane
        self.third[mine] = add_slots(self.second, 8)
        push(lambda rank: self.third.at[mine], self.third, mine, peers, self.sems.at[6], self.sems.at[7])

    def finish(self):
        drain(self.third.at[pl.ds(0, 15)], self.sems.at[7])
        return self.third[...].reshape(128, GROUP)

    def sent(self):
        for index in range(len(self.ranges)):
            self.scattered(index, 0)

    def close(self):
        drain(self.second.at[pl.ds(0, 7)], self.sems.at[4])
        drain(self.third.at[pl.ds(0, 15)], self.sems.at[6])


def half_gate(values, scale, shift):
    h = values * scale + shift
    return h, jnp.tanh(h)


def twice_slope_of(h, th):
    return (1.0 + th) * (1.0 + (h - h * th))


def sigmoid(v):
    return 1.0 / (1.0 + jnp.exp(-v))


def lanes_of(g):
    return pl.ds(pl.multiple_of(g * LANE, LANE), LANE)


def fold(v):
    return v[0] + v[1]


def row_sum(v):
    return jnp.sum(v, axis=0, keepdims=True)


def row_pairs():
    return [(i, i + a - 2, a) for a in range(5) for i in range(H) if 0 <= i + a - 2 < H]


def nine_weights(w):
    m2, m1, w0, p1, p2 = w
    return [
        w0, p1 - w0, m1 - w0,
        p2 - w0, w0 - p1 - p2, (p1 - m1) + (w0 - p2),
        m2 - w0, (m1 - p1) + (w0 - m2), w0 - m1 - m2,
    ]


FIVE = (
    (0, 0, 0, 0, 0, 0, 1, -1, -1),
    (0, 0, 1, 0, 0, -1, 0, 1, -1),
    (1, -1, -1, -1, 1, 1, -1, 1, 1),
    (0, 1, 0, 0, -1, 1, 0, -1, 0),
    (0, 0, 0, 1, -1, -1, 0, 0, 0),
)
IN_D, IN_CELLS, IN_R, IN_X, SUMS = 48, 96, 120, 152, 192


def combination():
    c = np.zeros((128, SUMS), np.float32)
    for a in range(5):
        for k in range(5):
            t = 5 * a + k
            for m in range(9):
                c[t, 9 * a + m] = FIVE[k][m]
                c[AT_DD + t, IN_D + 9 * a + m] = FIVE[k][m]
            for i in range(H):
                for j in range(W):
                    ii, jj = i + a - 2, j + k - 2
                    if 0 <= ii < H and 0 <= jj < W:
                        c[AT_PLAIN + t, IN_CELLS + ii * W + jj] = 1.0
    for i in range(SQZ):
        c[AT_R + i, IN_R + i] = 1.0
    for i in range(IN_THIRD):
        c[AT_X + i, IN_X + i] = 1.0
    return c


def over_rows(x, weights, m, cols):
    w = [jnp.broadcast_to(weights[a * 9 + m : a * 9 + m + 1, cols], (8, LANE)) for a in range(5)]
    acc = [None] * H
    for i, ii, a in row_pairs():
        term = x[ii] * w[a]
        acc[i] = term if acc[i] is None else acc[i] + term
    return acc


def plus(a, b):
    return [u + v for u, v in zip(a, b)]


def convolve(column, weights, cols, kept, put):
    x13 = plus(column(1), column(3))
    x02 = plus(column(0), column(2))
    m1 = over_rows(x13, weights, 1, cols)
    m2 = over_rows(x02, weights, 2, cols)
    m0 = over_rows(plus(x02, x13), weights, 0, cols)
    for i, v in enumerate(plus(m0, m1) + plus(m0, m2)):
        kept[i] = v
    for first, left, right in ((3, 2, 0), (6, 0, 2)):
        both = over_rows(plus(column(left), column(left + 1)), weights, first, cols)
        for k, j in ((0, left + 1), (1, left)):
            own = over_rows(column(j), weights, first + 1 + k, cols)
            for i in range(H):
                put(i, right + k, kept[k * H + i] + (both[i] + own[i]))


def correlate(target, left, right):
    def add(m, y, x):
        acc = [None] * 5
        for i, ii, a in row_pairs():
            term = y[i] * x[ii]
            acc[a] = term if acc[a] is None else acc[a] + term
        for a in range(5):
            target[a * 9 + m] += fold(acc[a])

    y02, x13 = plus(left(0), left(2)), plus(right(1), right(3))
    add(1, y02, x13)
    y13, x02 = plus(left(1), left(3)), plus(right(0), right(2))
    add(2, y13, x02)
    add(0, plus(y02, y13), plus(x02, x13))
    for first, j, k in ((3, 0, 2), (6, 2, 0)):
        add(first, plus(left(j), left(j + 1)), plus(right(k), right(k + 1)))
        add(first + 1, left(j), right(k + 1))
        add(first + 2, left(j + 1), right(k))


def column_of(ref, base, cols):
    return lambda j: [ref[pl.ds(base + 2 * (i * W + j), 2), :, cols] for i in range(H)]


def row_sums(target, first, source, cols):
    for t in range(source.shape[0]):
        target[first + t : first + t + 1, cols] = row_sum(source[t])


def kernel(
    f_hbm, q_hbm, we_hbm, wp_hbm, wr_hbm, wx_hbm, wd_hbm, ga1_hbm, bi1_hbm, ga2_hbm, bi2_hbm, bx_hbm, br_hbm, ga3_hbm, bi3_hbm,
    combine_hbm, units,
    f_in, q_in, o_panel,
    we_in, wp_in, wr_in, wx_in, wd_in, ga1_in, bi1_in, ga2_in, bi2_in, bx_in, br_in, ga3_in, bi3_in,
    copy_sems, stage, wide_stage,
    f_rows, q_rows, p_rows, f3, ft, pg3, qpt, qa,
    e_ref, a1, dv, q2, act_hi, act_lo,
    gathered, we, wp, wr, wx, we_b, ws_b, wp_b, wd, wt, par, parts, combine, acc45, acc24, cov_we, kept,
    pool, gates, spread, vec, sums, gp_panel, misc, g_panel,
    near, far, near2, far2,
    g_first, g_second, g_third,
    p_first, p_parts, p_second, p_third,
    m_first, m_parts, m_second, m_third,
    e_first, e_parts, e_second, e_third,
    w_sems, v_sems, g_sems, s_sems,
):
    third = ROWS // 3
    fetch_f = []
    for i in range(3):
        at = pl.ds(i * third, third)
        fetch_f.append(pltpu.make_async_copy(f_hbm.at[:, at], f_in.at[:, at], copy_sems.at[16 + i]))
        fetch_f[i].start()
    small_copies = [
        pltpu.make_async_copy(source, target, copy_sems.at[2 + i])
        for i, (source, target) in enumerate((
            (we_hbm, we_in), (wp_hbm, wp_in), (wr_hbm, wr_in), (wx_hbm, wx_in), (wd_hbm, wd_in),
            (ga1_hbm, ga1_in), (bi1_hbm, bi1_in), (ga2_hbm, ga2_in), (bi2_hbm, bi2_in), (bx_hbm, bx_in),
            (br_hbm, br_in), (ga3_hbm, ga3_in), (bi3_hbm, bi3_in), (combine_hbm, combine),
        ))
    ]
    for copy in small_copies:
        copy.start()
    fetch_q = pltpu.make_async_copy(q_hbm, q_in, copy_sems.at[0])
    fetch_q.start()
    x, y, c, z = place()
    column, plane = column_peers(), plane_peers()
    barrier = pltpu.get_barrier_semaphore()
    for _, device in column[1] + plane[1]:
        pl.semaphore_signal(barrier, inc=1, device_id=device, device_id_type=MESH)

    sum2a = Vector(column, plane, near2.at[0], far2.at[0], v_sems.at[0])
    sum2b = Vector(column, plane, near2.at[1], far2.at[1], v_sems.at[1])
    sum3 = Vector(column, plane, near2.at[2], far2.at[2], v_sems.at[2])
    sum4 = Vector(column, plane, near.at[0], far.at[0], v_sems.at[3])
    sum5 = Vector(column, plane, near.at[1], far.at[1], v_sems.at[4])
    vectors = [sum2a, sum2b, sum3, sum4, sum5]
    reduce_g = Square(column, plane, g_panel, g_first, g_second, g_third, g_sems)
    whole = [(0, WIDE)]
    reduce_p = Panel(column, plane, whole, gp_panel, p_first, p_parts, p_second, p_third, s_sems.at[0])
    reduce_m = Panel(column, plane, whole, misc, m_first, m_parts, m_second, m_third, s_sems.at[1])
    early_late = [(0, 2 * GROUP), (2 * GROUP, WIDE)]
    reduce_e = Panel(column, plane, early_late, gp_panel, e_first, e_parts, e_second, e_third, s_sems.at[2])

    ones = jnp.where(lax.broadcasted_iota(jnp.int32, (16, third), 0) == 0, 1.0, 0.0)
    gram = None
    for i in range(3):
        fetch_f[i].wait()
        at = slice(i * third, (i + 1) * third)
        hi, lo = split(jnp.concatenate([f_in[:, at], ones], axis=0))
        both = jnp.concatenate([hi, lo], axis=0)
        part = mm_nt(both, both)
        gram = part if gram is None else gram + part
    gram = gram[0:128, 0:128] + (gram[0:128, 128:256] + gram[128:256, 0:128]) + gram[128:256, 128:256]
    g_panel[...] = gram.reshape(8, 16, LANE)
    pl.semaphore_wait(barrier, 22)
    reduce_g.start()

    sections = ((0, AT_DEPTH), (AT_DEPTH, AT_PROJECT), (AT_PROJECT, PANEL))
    odd = lax.rem(z, 2) == 1

    across = [(lax.rem(z + k, 4), {"chan": lax.rem(z + k, 4)}) for k in (2, 1, 3)]

    def halves(s):
        lo, hi = sections[s]
        size = (hi - lo) // 2
        return size, pl.ds(pl.multiple_of(lo + c * size, 8), size), pl.ds(lo, size)

    def send_section(s):
        lo, hi = sections[s]
        rest = gathered[z, lo:hi, LANE:GROUP]
        gathered[z, lo:hi, LANE:GROUP] = jnp.where(odd, pltpu.roll(rest, 64, 1), rest)
        size, rows, _ = halves(s)
        for _, device in across:
            pltpu.make_async_remote_copy(
                src_ref=gathered.at[z, rows],
                dst_ref=gathered.at[z, rows],
                send_sem=w_sems.at[0, s],
                recv_sem=w_sems.at[1, s],
                device_id=device,
                device_id_type=MESH,
            ).start()

    def forward_section(s):
        size, rows, some = halves(s)
        drain(gathered.at[pl.ds(0, 3), some], w_sems.at[1, s])
        for other, _ in across:
            pltpu.make_async_remote_copy(
                src_ref=gathered.at[other, rows],
                dst_ref=gathered.at[other, rows],
                send_sem=w_sems.at[0, s],
                recv_sem=w_sems.at[2, s],
                device_id=(x * 8 + y * 2 + 1 - c, z),
                device_id_type=MESH,
            ).start()

    def section(s):
        size, rows, some = halves(s)
        drain(gathered.at[pl.ds(0, 3), some], w_sems.at[2, s])

    def close_section(s):
        size, rows, some = halves(s)
        for _ in range(2):
            drain(gathered.at[pl.ds(0, 3), some], w_sems.at[0, s])

    def assembled(lo, rows):
        parts = [gathered[k, lo : lo + rows, 0:LANE] for k in range(4)]
        for k in (0, 2):
            parts.append(gathered[k, lo : lo + rows, LANE:GROUP] + gathered[k + 1, lo : lo + rows, LANE:GROUP])
        return jnp.concatenate(parts, axis=1)

    for copy in small_copies:
        copy.wait()
    gathered[z] = jnp.zeros((PANEL, GROUP), F32)
    wide_stage[...] = jnp.zeros_like(wide_stage)
    wide_stage[0:OWN, 0:D] = we_in[...]
    gathered[z, 0:D, :] = wide_stage[...].T[0:D]
    send_section(0)
    for a in range(5):
        gathered[z, AT_DEPTH + 5 * a : AT_DEPTH + 5 * a + 5, 0:OWN] = wd_in[a]
    for i, row in enumerate((ga1_in, bi1_in, ga2_in, bi2_in, bx_in)):
        gathered[z, AT_VECS + i : AT_VECS + i + 1, 0:OWN] = row[...]
    send_section(1)
    wide_stage[0:OWN, 0:D] = wp_in[...]
    gathered[z, AT_PROJECT : AT_PROJECT + D, :] = wide_stage[...].T[0:D]
    gathered[z, AT_REDUCE : AT_REDUCE + SQZ, 0:OWN] = wr_in[...]
    gathered[z, AT_EXCITE : AT_EXCITE + SQZ, 0:OWN] = wx_in[...]
    send_section(2)

    tail = jnp.where(lax.broadcasted_iota(jnp.int32, (16, LANE), 0) == 0, 1.0, 0.0)

    def rows_of(source, tail, target):
        @pl.loop(0, BLOCKS)
        def _(b):
            for i in range(3):
                v = source[:, pl.ds(pl.multiple_of(b * CHUNK + i * LANE, LANE), LANE)]
                stage[i * LANE : (i + 1) * LANE, :] = jnp.concatenate([v, tail], axis=0).T
            for cell in range(CELLS):
                v = stage[pl.ds(cell, BLOCK, stride=CELLS), :]
                target[pl.ds((b * CELLS + cell) * 2, 2)] = v.reshape(2, 8, LANE)

    rows_of(f_in, tail, f_rows)

    @rloop("ft", 18)
    def _(i):
        v = f_rows[pl.ds(i * 16, 16)].reshape(128, LANE)
        rows = pl.ds(pl.multiple_of(i * 128, 128), 128)
        hi, lo = split(v)
        f3[rows, 0:128] = hi
        f3[rows, 128:256] = hi
        f3[rows, 256:384] = lo
        hi, lo = split(v.T)
        ft[0:128, rows] = hi
        ft[128:256, rows] = lo

    def parts_of(source, row):
        @pl.loop(0, 18)
        def _(i):
            hi, lo = split(source[pl.ds(i * 16, 16)].reshape(128, LANE).T)
            rows = pl.ds(pl.multiple_of(i * 128, 128), 128)
            qpt[row : row + 128, rows] = hi
            qpt[256 + row : 384 + row, rows] = lo

    reduce_g.middle()
    fetch_q.wait()
    rows_of(q_in, jnp.zeros((16, LANE), F32), q_rows)
    parts_of(q_rows, 0)
    sums[...] = jnp.zeros_like(sums)
    parts[...] = jnp.zeros_like(parts)
    qa[...] = jnp.zeros_like(qa)

    forward_section(0)
    forward_section(1)
    reduce_g.last()
    section(0)
    we[0:D, :] = assembled(0, D)
    we[D:128, :] = jnp.zeros((128 - D, WIDE), F32)
    hi, lo = split(we[...])
    we_b[0:128, :] = hi
    we_b[128:256, :] = lo

    @rloop("E", BLOCKS)
    def _(b):
        @pl.when(b == 3)
        def _():
            forward_section(2)

        rows = pl.ds(pl.multiple_of(b * CHUNK, CHUNK), CHUNK)
        for n in range(3):
            cols = slice(n * GROUP, (n + 1) * GROUP)
            r = mm(f3[rows, 0:256], we_b[:, cols]) + mm(f3[rows, 256:384], we_b[0:128, cols])
            e_ref[pl.ds(b * 48, 48), :, cols] = r.reshape(48, 8, GROUP)

    section(1)
    taps = assembled(AT_DEPTH, 32)
    for a in range(5):
        row = [taps[5 * a + k : 5 * a + k + 1] for k in range(5)]
        for m, v in enumerate(nine_weights(row)):
            wd[a * 9 + m : a * 9 + m + 1, :] = v
        for m, v in enumerate(nine_weights(row[::-1])):
            wt[(4 - a) * 9 + m : (4 - a) * 9 + m + 1, :] = v
    gain1, bias1, gain2, bias2, bx = [taps[TAPS + i : TAPS + i + 1] for i in range(5)]

    section(2)
    wp[0:D, :] = assembled(AT_PROJECT, D)
    wp[D:128, :] = jnp.zeros((128 - D, WIDE), F32)
    hi, lo = split(assembled(AT_REDUCE, 32))
    wr[...] = jnp.concatenate([hi, lo, hi, lo], axis=0)
    hi, lo = split(assembled(AT_EXCITE, 32))
    wx[...] = jnp.concatenate([hi, lo, hi, lo], axis=0)
    gram = reduce_g.finish() * (1.0 / TOTAL)
    f_mean_row = gram[D : D + 1, :]
    f_mean = gram[:, D : D + 1]
    cov = gram - f_mean * f_mean_row
    hi, lo = split(cov)
    cov_we[...] = mm(jnp.concatenate([hi, hi], axis=1), we_b[...]) + mm(jnp.concatenate([lo, lo], axis=1), we_b[...])
    mean1 = row_sum(we[...] * f_mean)
    inv1 = lax.rsqrt(row_sum(we[...] * cov_we[...]) + EPSILON)
    s1 = gain1 * inv1
    t1 = bias1 - mean1 * s1

    def put(i, row, lo=0, hi=WIDE):
        par[i, :, lo:hi] = jnp.broadcast_to(row, (8, hi - lo))

    put(0, 0.5 * s1)
    put(1, 0.5 * t1)

    def put_sums(first, second, g, low, size):
        sums[pl.ds(g - low, 1), :] = row_sum(first)
        sums[pl.ds(g - low + size, 1), :] = row_sum(second)

    @rloop("conv1", GROUPS)
    def _(g):
        cols = lanes_of(g)

        def block(b, carry):
            total, square = carry
            base = b * 48
            scale, shift = par[0, :, cols], par[1, :, cols]
            for cell in range(CELLS):
                at = pl.ds(base + 2 * cell, 2)
                h, th = half_gate(e_ref[at, :, cols], scale, shift)
                a1[at, :, cols] = h + h * th
            tally = [total, square]

            def put(i, j, v):
                dv[pl.ds(base + 2 * (i * W + j), 2), :, cols] = v
                tally[0] = tally[0] + fold(v)
                tally[1] = tally[1] + fold(v * v)

            convolve(column_of(a1, base, cols), wd, cols, kept, put)
            total, square = tally
            return total, square

        zero = jnp.zeros((8, LANE), F32)
        total, square = lax.fori_loop(0, BLOCKS // 2, lambda i, v: block(2 * i + 1, block(2 * i, v)), (zero, zero))
        put_sums(total, square, g, jnp.where(g < 4, 0, 4), jnp.where(g < 4, 4, 2))

        @pl.when(g == 3)
        def _():
            sum2a.start(sums[0:8, :])

        @pl.when(g == 5)
        def _():
            sum2b.start(sums[0:8, :])

    def wide(rows, first, count):
        return jnp.concatenate([rows[first + g : first + g + 1, :] for g in range(count)], axis=1)

    mean2, inv2 = [None] * 2, [None] * 2

    def second_norm(got, lo, hi):
        count = (hi - lo) // LANE
        mean = wide(got, 0, count) * (1.0 / TOTAL)
        inv = lax.rsqrt(wide(got, count, count) * (1.0 / TOTAL) - mean * mean + EPSILON)
        scale = par[7, 0:1, lo:hi] * inv
        put(2, 0.5 * scale, lo, hi)
        put(3, 0.5 * (par[8, 0:1, lo:hi] - mean * scale), lo, hi)
        put(9, mean, lo, hi)
        put(10, inv, lo, hi)
        put(11, scale, lo, hi)

    put(7, gain2)
    put(8, bias2)

    def one_products(g):
        cols = lanes_of(g)
        acc45[...] = jnp.zeros_like(acc45)
        acc24[...] = jnp.zeros_like(acc24)

        @pl.loop(0, BLOCKS)
        def _(b):
            for cell in range(CELLS):
                acc24[cell] += fold(a1[pl.ds(b * 48 + 2 * cell, 2), :, cols])
            correlate(acc45, column_of(dv, b * 48, cols), column_of(a1, b * 48, cols))

        row_sums(parts, IN_D, acc45, cols)
        row_sums(parts, IN_CELLS, acc24, cols)

    def one_activation(g):
        cols = lanes_of(g)

        def block(b):
            scale, shift = par[2, :, cols], par[3, :, cols]
            pooled = jnp.zeros((8, LANE), F32)
            for cell in range(CELLS):
                at = pl.ds(b * 48 + 2 * cell, 2)
                h, th = half_gate(dv[at, :, cols], scale, shift)
                q2[at, :, cols] = th
                act = h + h * th
                pooled = pooled + fold(act)
                hi, lo = split(act.reshape(16, LANE))
                rows = pl.ds(b * CHUNK + 16 * cell, 16)
                act_hi[rows, cols] = hi
                act_lo[rows, cols] = lo
            pool[b, :, cols] = pooled

        @pl.loop(0, BLOCKS // 2)
        def _(i):
            block(2 * i)
            block(2 * i + 1)

    @pl.loop(0, 11)
    def _(step):
        @pl.when(step == 1)
        def _():
            sum2a.middle()

        @pl.when(step == 3)
        def _():
            sum2b.middle()

        @pl.when(step == 5)
        def _():
            second_norm(sum2a.finish(), 0, 4 * LANE)

        @pl.when(step == 9)
        def _():
            second_norm(sum2b.finish(), 4 * LANE, WIDE)

        @pl.when(step < 5)
        def _():
            one_products(step)

        @pl.when(step >= 5)
        def _():
            one_activation(step - 5)

    seg = lax.broadcasted_iota(jnp.int32, (8, LANE), 0)
    blk = lax.broadcasted_iota(jnp.int32, (8, LANE), 1)
    u0, u1, u2 = units[z, 0], units[z, 1], units[z, 2]
    lower = jnp.where(seg == 0, 0, jnp.where(seg == 1, u0, u0 + u1))
    length = jnp.where(seg == 0, u0, jnp.where(seg == 1, u1, u2))
    member = jnp.where((seg < 3) & (blk >= lower) & (blk < lower + length), 1.0, 0.0)
    per_count = jnp.where(seg < 3, 1.0 / (length * (BLOCK * CELLS)).astype(F32), 0.0)[:, 0:1]
    live = jnp.where(seg < 3, 1.0, 0.0)[:, 0:1]

    vec[...] = jnp.zeros((8, LANE), F32)
    vec[0:1, 0:SQZ] = br_in[...]
    pooled = jnp.zeros((8, WIDE), F32)
    for b in range(BLOCKS):
        pooled = pooled + member[:, b : b + 1] * row_sum(pool[b])
    plain_sums = pooled
    pooled = pooled * per_count
    pooled_pair = pair(pooled)
    reduced = pair_nt(pooled_pair, wr[0:64, :], 8, 32) + vec[0:1, 0:32]
    sig_r = sigmoid(reduced)
    squeezed = reduced * sig_r * live

    def quad(values):
        hi, lo = split(values)
        return jnp.concatenate([hi, hi, lo, lo], axis=1)

    gate = sigmoid(mm(quad(squeezed), wx[...]) + bx)

    def of_blocks(rows, b):
        return row_sum(member[:, b : b + 1] * rows)

    for b in range(BLOCKS):
        gates[b : b + 1, :] = of_blocks(gate, b)

    def project(b, carry):
        rows = slice(b * CHUNK, (b + 1) * CHUNK)
        hi, lo = split(wp[...] * gates[b : b + 1, :])
        wp_b[b, 0:128, :] = hi
        wp_b[b, 128:256, :] = lo
        r = mm_nt(act_hi[rows, :], wp_b[b])
        r = r[:, 0:128] + r[:, 128:256] + mm_nt(act_lo[rows, :], wp_b[b, 0:128, :])
        r = r.reshape(48, 8, LANE)
        q = q_rows[pl.ds(b * 48, 48)]
        p_rows[pl.ds(b * 48, 48)] = r
        return tuple(old + jnp.sum(new, axis=0) for old, new in zip(carry, (r, r * r, q, q * r)))

    zero = jnp.zeros((8, LANE), F32)
    four = (zero,) * 4
    for b in range(BLOCKS):
        four = project(b, four)
    for i in range(4):
        vec[i : i + 1, :] = row_sum(four[i])
    sum3.start(vec[...])

    parts_of(p_rows, 128)

    for b in range(BLOCKS):
        rows = slice(b * CHUNK, (b + 1) * CHUNK)
        inside = [jnp.where((b >= low) & (b < high), 1.0, 0.0) for low, high in ((0, u0), (u0, u0 + u1), (u0 + u1, 6))]
        m = mm(qpt[:, rows], act_hi[rows, :])
        m = m[0:256] + m[256:512] + mm(qpt[0:256, rows], act_lo[rows, :])
        for k in range(3):
            qa[k] += m * inside[k]
        if b == 3:
            sum3.middle()

    @rloop("slope2", GROUPS)
    def _(g):
        cols = lanes_of(g)

        @pl.loop(0, BLOCKS)
        def _(b):
            scale, shift = par[2, :, cols], par[3, :, cols]
            for cell in range(CELLS):
                at = pl.ds(b * 48 + 2 * cell, 2)
                q2[at, :, cols] = twice_slope_of(dv[at, :, cols] * scale + shift, q2[at, :, cols])

    def one_slope(g):
        cols = lanes_of(g)

        @pl.loop(0, BLOCKS)
        def _(b):
            scale, shift = par[0, :, cols], par[1, :, cols]
            for cell in range(CELLS):
                at = pl.ds(b * 48 + 2 * cell, 2)
                e_ref[at, :, cols] = twice_slope_of(*half_gate(e_ref[at, :, cols], scale, shift))

    pl.loop(0, 3)(one_slope)
    got = sum3.finish() * (1.0 / TOTAL)
    vec[...] = jnp.zeros((8, LANE), F32)
    vec[0:1, 0:D] = ga3_in[...]
    vec[1:2, 0:D] = bi3_in[...]
    gain3, bias3 = vec[0:1, :], vec[1:2, :]
    mean3 = got[0:1]
    inv3 = lax.rsqrt(got[1:2] - mean3 * mean3 + EPSILON)
    b3 = got[2:3]
    g3 = (got[3:4] - mean3 * got[2:3]) * inv3
    o_panel[OUT_SMALL : OUT_SMALL + 1, 0:LANE] = g3 * TOTAL
    o_panel[OUT_SMALL + 1 : OUT_SMALL + 2, 0:LANE] = b3 * TOTAL
    s3 = gain3 * inv3
    t3 = bias3 - mean3 * s3
    pg_p = -s3 * inv3 * g3
    pg_0 = -s3 * b3 - pg_p * mean3

    columns = jnp.concatenate([s3, pg_p, pg_0, jnp.zeros((5, LANE), F32)], axis=0).T
    by_q, by_p, by_1 = columns[:, 0:1], columns[:, 1:2], columns[:, 2:3]
    base = row_sum(wp[...] * by_1)
    w_q, w_p = wp[...] * by_q, wp[...] * by_p
    gate_grad = jnp.concatenate(
        [row_sum(w_q * qa[k, 0:128] + w_p * qa[k, 128:256]) + base * plain_sums[k : k + 1] for k in range(3)]
        + [jnp.zeros((5, WIDE), F32)],
        axis=0,
    )
    excite_in = gate_grad * gate * (1.0 - gate)
    reduced_grad = pair_nt(pair(excite_in), wx[0:64, :], 8, 32) * (sig_r * (1.0 + reduced * (1.0 - sig_r))) * live
    pooled_grad = mm(quad(reduced_grad), wr[...]) * per_count
    for b in range(BLOCKS):
        spread[b : b + 1, :] = 0.5 * of_blocks(pooled_grad, b)

    for b in range(BLOCKS):
        at = pl.ds(b * 48, 48)
        hi, lo = split((q_rows[at] * (0.5 * s3) + (p_rows[at] * (0.5 * pg_p) + 0.5 * pg_0)).reshape(CHUNK, LANE))
        rows = pl.ds(b * CHUNK, CHUNK)
        pg3[rows, 0:128] = hi
        pg3[rows, 128:256] = hi
        pg3[rows, 256:384] = lo

    total = product = jnp.zeros((8, WIDE), F32)
    for b in range(BLOCKS):
        rows = slice(b * CHUNK, (b + 1) * CHUNK)
        at = slice(b * 48, (b + 1) * 48)
        r = mm(pg3[rows, 0:256], wp_b[b]) + mm(pg3[rows, 256:384], wp_b[b, 0:128, :])
        r = (r.reshape(48, 8, WIDE) + spread[b : b + 1, :]) * q2[at]
        q2[at] = r
        total, product = total + jnp.sum(r, axis=0), product + jnp.sum(r * dv[at], axis=0)
    total, product = row_sum(total), row_sum(product)
    for g in range(GROUPS):
        lanes = slice(g * LANE, (g + 1) * LANE)
        sums[g : g + 1, :] = total[:, lanes]
        sums[8 + g : 9 + g, :] = product[:, lanes]
    sum4.start(sums[...])

    gp = jnp.zeros((128, WIDE), F32)
    for k in range(3):
        gp = gp + gate[k : k + 1] * (by_q * qa[k, 0:128] + by_p * qa[k, 128:256] + by_1 * plain_sums[k : k + 1])
    gp_panel[...] = gp.reshape(16, 8, WIDE)
    g_excite = exact(squeezed, excite_in, (0, 0))
    gp_panel[14, 0:1, :] = row_sum(excite_in)
    gp_panel[15, 0:1, :] = jnp.zeros((1, WIDE), F32)
    for k in range(4):
        gp_panel[15, 0:1, k * LANE : k * LANE + 32] = row_sum(reduced_grad)
    for i in range(IN_THIRD, SQZ):
        gp_panel[14, 1 + i - IN_THIRD : 2 + i - IN_THIRD, :] = g_excite[i : i + 1]
    reduce_p.start(0)

    parts[IN_R : IN_R + 32, :] = exact(reduced_grad, pooled, (0, 0))
    parts[IN_X : IN_X + 32, :] = g_excite

    @rloop("tq", GROUPS)
    def _(g):
        cols = lanes_of(g)
        acc45[...] = jnp.zeros_like(acc45)

        @pl.loop(0, BLOCKS)
        def _(b):
            correlate(acc45, column_of(q2, b * 48, cols), column_of(a1, b * 48, cols))

        @pl.when(g >= 3)
        def _():
            one_slope(g)

        row_sums(parts, 0, acc45, cols)

        @pl.when(g == 2)
        def _():
            sum4.middle()

    def own_lanes(rows):
        first = rows[:, 0:LANE]
        rest = rows[:, LANE:GROUP]
        return first, jnp.where(odd, pltpu.roll(rest, 64, 1), rest)

    def own_wide(rows):
        first = jnp.zeros((rows.shape[0], LANE), F32)
        rest = jnp.zeros((rows.shape[0], LANE), F32)
        for k in range(4):
            first = jnp.where(z == k, rows[:, k * LANE : (k + 1) * LANE], first)
        for k in range(2):
            rest = jnp.where(z // 2 == k, rows[:, (4 + k) * LANE : (5 + k) * LANE], rest)
        return jnp.concatenate([first, rest], axis=1)

    def emit(row, values):
        first, rest = own_lanes(values)
        o_panel[row : row + values.shape[0], 0:LANE] = first
        o_panel[row : row + values.shape[0], LANE:GROUP] = rest

    def emit_vector(i, row):
        emit(OUT_VECS + i, own_wide(row))

    one_products(5)

    hi, lo = split(parts[...])
    picks = combine[...].astype(BF16)
    misc[...] = (mm(picks, hi) + mm(picks, lo)).reshape(16, 8, WIDE)
    reduce_m.start(0)

    got = sum4.finish()
    mean2, inv2, s2 = [par[i, 0:1, :] for i in (9, 10, 11)]
    b2 = wide(got, 0, GROUPS)
    g2 = (wide(got, 8, GROUPS) - mean2 * b2) * inv2
    c3 = -s2 * inv2 * g2 * (1.0 / TOTAL)
    c2 = -s2 * b2 * (1.0 / TOTAL) - c3 * mean2
    shift3 = -inv2 * g2 * (1.0 / TOTAL)
    put(4, -b2 * (1.0 / TOTAL) - shift3 * mean2)
    put(5, shift3)
    wt[...] = wt[...] * (0.5 * s2)
    emit_vector(2, g2)
    emit_vector(3, b2)

    @rloop("conv2", GROUPS)
    def _(g):
        @pl.when(g == 1)
        def _():
            reduce_p.sent()

        cols = lanes_of(g)

        def block(b):
            base = b * 48
            k2, k3 = par[4, :, cols], par[5, :, cols]

            for cell in range(CELLS):
                at = pl.ds(base + 2 * cell, 2)
                q2[at, :, cols] = q2[at, :, cols] + (dv[at, :, cols] * k3 + k2)

            def put(i, j, v):
                at = pl.ds(base + 2 * (i * W + j), 2)
                hi, lo = split((v * e_ref[at, :, cols]).reshape(16, LANE))
                rows = pl.ds(b * CHUNK + 16 * (i * W + j), 16)
                act_hi[rows, cols] = hi
                act_lo[rows, cols] = lo

            convolve(column_of(q2, base, cols), wt, cols, kept, put)

        @pl.loop(0, BLOCKS // 2)
        def _(i):
            block(2 * i)
            block(2 * i + 1)

        @pl.when(lax.rem(g, 2) == 1)
        def _():
            n = g // 2
            cols = pl.ds(pl.multiple_of(n * GROUP, GROUP), GROUP)
            m = mm(ft[...], act_hi[:, cols])
            m = m[0:128] + m[128:256] + mm(ft[0:128, :], act_lo[:, cols])
            gp_panel[:, :, cols] = m.reshape(16, 8, GROUP)

            @pl.when(g == 5)
            def _():
                reduce_e.start(1)

            product = row_sum(m * we[:, cols])
            for half in range(2):
                lanes = slice(half * LANE, (half + 1) * LANE)
                sums[pl.ds(g - 1 + half, 1), :] = m[D : D + 1, lanes]
                sums[pl.ds(g + 7 + half, 1), :] = product[:, lanes]

            @pl.when(g == 3)
            def _():
                reduce_e.start(0)

    sum5.start(sums[...])
    reduce_p.middle()
    reduce_m.middle()

    hi, lo = split(we[...] * s1)
    ws_b[0:128, :] = hi
    ws_b[128:256, :] = lo

    @rloop("ig", 3)
    def _(i):
        rows = pl.ds(pl.multiple_of(i * 2 * CHUNK, 2 * CHUNK), 2 * CHUNK)
        r = mm_nt(act_hi[rows, :], ws_b[...])
        r = r[:, 0:128] + r[:, 128:256] + mm_nt(act_lo[rows, :], ws_b[0:128, :])
        q_rows[pl.ds(i * 96, 96)] += r.reshape(96, 8, LANE)

    def write(target, b, rows_of_cell):
        for cell in range(CELLS):
            stage[pl.ds(cell, BLOCK, stride=CELLS), :] = rows_of_cell(pl.ds(b * 48 + 2 * cell, 2)).reshape(16, LANE)
        for i in range(3):
            at = pl.ds(pl.multiple_of(b * CHUNK + i * LANE, LANE), LANE)
            target[:, at] = stage[i * LANE : (i + 1) * LANE, :].T[0:D]

    reduce_e.middle()
    sum5.middle()
    reduce_p.last()
    reduce_m.last()

    @rloop("out", BLOCKS)
    def _(b):
        write(f_in, b, lambda at: f_rows[at] + (p_rows[at] * s3 + t3))

    reduce_e.last()
    got = sum5.finish()
    b1 = wide(got, 0, GROUPS)
    g1 = (wide(got, 8, GROUPS) - mean1 * b1) * inv1
    k3 = -s1 * inv1 * g1 * (1.0 / TOTAL)
    k2 = -s1 * b1 * (1.0 / TOTAL) - k3 * mean1
    left = jnp.where(lax.broadcasted_iota(jnp.int32, (128, WIDE), 0) == D, k2, we[...] * k3)
    mix = pair_nt(pair(left), we_b[...], 128, 128)
    mix_hi, mix_lo = split(mix)
    mix_all = jnp.concatenate([mix_hi, mix_lo], axis=0)

    @rloop("ig2", BLOCKS)
    def _(b):
        rows = pl.ds(pl.multiple_of(b * CHUNK, CHUNK), CHUNK)
        r = mm(f3[rows, 0:256], mix_all) + mm(f3[rows, 256:384], mix_hi)
        q_rows[pl.ds(b * 48, 48)] += r.reshape(48, 8, LANE)
        write(q_in, b, lambda at: q_rows[at])

    emit_vector(0, g1)
    emit_vector(1, b1)
    emit(OUT_PROJECT, reduce_p.finish())
    total_m = reduce_m.finish()
    emit(OUT_MISC, total_m)
    by = [own_wide(v) for v in (s2, c2, c3)]
    taps_grad = total_m[0:TAPS] * by[0] + total_m[AT_DD : AT_DD + TAPS] * by[2] + total_m[AT_PLAIN : AT_PLAIN + TAPS] * by[1]
    emit(OUT_MISC, taps_grad)
    scale_own = own_wide(s1)
    away = f_mean * own_wide(b1) + own_wide(cov_we[...]) * own_wide(inv1 * g1)
    for s in range(3):
        close_section(s)
    reduce_m.sent()
    reduce_e.sent()
    for item in vectors + [reduce_g, reduce_p, reduce_m, reduce_e]:
        item.close()
    emit(0, scale_own * (reduce_e.finish() - away))


def finish_kernel(
    out_in, igrad_in, panel,
    out, igrad, expand, gain1, bias1, depth, gain2, bias2, reduce, b_reduce, excite, b_excite, project, gain3, bias3,
    sems,
):
    large = [pltpu.make_async_copy(out_in, out, sems.at[0]), pltpu.make_async_copy(igrad_in, igrad, sems.at[1])]
    for copy in large:
        copy.start()
    expand[...] = panel[0:LANE, :].T[0:OWN, 0:D]
    project[...] = panel[OUT_PROJECT : OUT_PROJECT + LANE, :].T[0:OWN, 0:D]
    for a in range(5):
        depth[a] = panel[OUT_MISC + 5 * a : OUT_MISC + 5 * a + 5, 0:OWN]
    reduce[...] = panel[OUT_MISC + AT_R : OUT_MISC + AT_R + SQZ, 0:OWN]
    excite[0:IN_THIRD, :] = panel[OUT_MISC + AT_X : OUT_MISC + 128, 0:OWN]
    excite[IN_THIRD:SQZ, :] = panel[OUT_PROJECT + D + 1 : OUT_PROJECT + D + 1 + SQZ - IN_THIRD, 0:OWN]
    b_excite[...] = panel[OUT_PROJECT + D : OUT_PROJECT + D + 1, 0:OWN]
    b_reduce[...] = panel[OUT_PROJECT + D + 8 : OUT_PROJECT + D + 9, 0:SQZ]
    for i, ref in enumerate((gain1, bias1, gain2, bias2)):
        ref[...] = panel[OUT_VECS + i : OUT_VECS + i + 1, 0:OWN]
    gain3[...] = panel[OUT_SMALL : OUT_SMALL + 1, 0:D]
    bias3[...] = panel[OUT_SMALL + 1 : OUT_SMALL + 2, 0:D]
    for copy in large:
        copy.wait()


def body(
    features, seg_units, w_expand, gain_one, bias_one, w_depth, gain_two, bias_two,
    w_reduce, b_reduce, w_excite, b_excite, w_project, gain_three, bias_three, cotangent,
):
    vm = pl.BlockSpec(memory_space=pltpu.VMEM)
    anywhere = pl.BlockSpec(memory_space=pl.ANY)
    big = pltpu.VMEM((288, 8, WIDE), F32)
    rows128 = pltpu.VMEM((288, 8, LANE), F32)
    half = pltpu.VMEM((ROWS, WIDE), BF16)

    def f32(*shape):
        return pltpu.VMEM(shape, F32)

    def b16(*shape):
        return pltpu.VMEM(shape, BF16)

    def shape(*dims):
        return jax.ShapeDtypeStruct(dims, F32)

    def row(vector):
        return vector.reshape(1, vector.shape[0])

    dma = pltpu.SemaphoreType.DMA
    slots = [f32(16, 8, WIDE), f32(4, 8, GROUP), f32(8, 8, GROUP), f32(16, 8, GROUP)]
    out, igrad, panel = pl.pallas_call(
        kernel,
        out_shape=(f32(D, ROWS), f32(D, ROWS), f32(RESULTS, GROUP)),
        in_specs=[anywhere] * 16 + [pl.BlockSpec(memory_space=pltpu.SMEM)],
        out_specs=(vm,) * 3,
        scratch_shapes=[
            f32(OWN, D), f32(OWN, D), f32(SQZ, OWN), f32(SQZ, OWN), f32(5, 5, OWN),
            f32(1, OWN), f32(1, OWN), f32(1, OWN), f32(1, OWN), f32(1, OWN), f32(1, SQZ), f32(1, D), f32(1, D),
            dma((19,)), f32(CHUNK, LANE), f32(GROUP, LANE),
            rows128, rows128, rows128, b16(ROWS, 384), b16(256, ROWS), b16(ROWS, 384), b16(512, ROWS), f32(3, 256, WIDE),
            big, big, big, big, half, half,
            f32(4, PANEL, GROUP), f32(128, WIDE), f32(128, WIDE), b16(128, WIDE), b16(128, WIDE),
            b16(256, WIDE), b16(256, WIDE), b16(BLOCKS, 256, WIDE), f32(48, WIDE), f32(48, WIDE), f32(12, 8, WIDE),
            f32(SUMS, WIDE), f32(128, SUMS), f32(45, 8, LANE), f32(CELLS, 8, LANE), f32(128, WIDE), f32(2 * H, 2, 8, LANE),
            f32(BLOCKS, 8, WIDE), f32(8, WIDE), f32(8, WIDE), f32(8, LANE), f32(16, LANE),
            f32(16, 8, WIDE), f32(16, 8, WIDE), f32(8, 16, LANE),
            f32(2, 8, 16, LANE), f32(2, 16, 16, LANE), f32(3, 8, 8, LANE), f32(3, 16, 8, LANE),
            f32(8, 16, LANE), f32(16, 16, LANE), f32(8, 16, LANE),
        ]
        + slots * 3
        + [dma((3, 3)), dma((5, 4)), dma((6,)), dma((3, 8))],
        compiler_params=pltpu.CompilerParams(
            collective_id=0, has_side_effects=True, vmem_limit_bytes=61 * 1024 * 1024 + 256 * 1024
        ),
    )(
        features.T, cotangent.T, w_expand.T, w_project, w_reduce.T, w_excite, w_depth,
        row(gain_one), row(bias_one), row(gain_two), row(bias_two), row(b_excite), row(b_reduce), row(gain_three), row(bias_three),
        jnp.asarray(combination()), seg_units,
    )

    small = [
        (OWN, D), (1, OWN), (1, OWN), (5, 5, OWN), (1, OWN), (1, OWN),
        (SQZ, OWN), (1, SQZ), (SQZ, OWN), (1, OWN), (OWN, D), (1, D), (1, D),
    ]
    results = pl.pallas_call(
        finish_kernel,
        out_shape=(shape(D, ROWS), shape(D, ROWS)) + tuple(shape(*dims) for dims in small),
        in_specs=[vm] * 3,
        out_specs=(anywhere, anywhere) + (vm,) * 13,
        scratch_shapes=[dma((2,))],
        compiler_params=pltpu.CompilerParams(vmem_limit_bytes=8 * 1024 * 1024),
    )(*(pltpu.with_memory_space_constraint(v, pltpu.VMEM) for v in (out, igrad, panel)))
    (out, igrad, expand, gain1, bias1, depth, gain2, bias2, reduce, small_b, excite, b_x, project, gain3, bias3) = results
    return (
        out.T, igrad.T, expand.T, gain1[0], bias1[0], depth, gain2[0], bias2[0],
        reduce.T, small_b[0], excite, b_x[0], project, gain3[0], bias3[0],
    )


def solution(mesh):
    placed = (
        P(("dp", "chan"), None),
        P("dp", None),
        P(None, "chan"),
        P("chan"),
        P("chan"),
        P(None, None, "chan"),
        P("chan"),
        P("chan"),
        P("chan", None),
        P(),
        P(None, "chan"),
        P("chan"),
        P("chan", None),
        P(),
        P(),
        P(("dp", "chan"), None),
    )
    return jax.shard_map(
        body,
        mesh=mesh,
        in_specs=placed,
        out_specs=(
            P(("dp", "chan"), None),
            P(("dp", "chan"), None),
            P(None, "chan"),
            P("chan"),
            P("chan"),
            P(None, None, "chan"),
            P("chan"),
            P("chan"),
            P("chan", None),
            P(),
            P(None, "chan"),
            P("chan"),
            P("chan", None),
            P(),
            P(),
        ),
        check_vma=False,
    )
```
